128 devices in a mesh: rep: 4 (over x_lo, core), fsdp: 32 (over z, x_hi, y).
Axes of the slice: x: 4 (x_hi: 2, x_lo: 2; x = x_hi * 2 + x_lo), y: 4, z: 4, core: 2. Of those that a mesh axis runs over, the one named last changes fastest.
Arguments:
- inputs: bfloat16 [4, 4096, 1792], P('rep', 'fsdp'), may hold values from -6 to 6
- cotangent: bfloat16 [4, 4096, 1792], P('rep', 'fsdp'), may hold values from -18 to 18
- up_weight: bfloat16 [4, 14336, 1792], P('rep', 'fsdp'), may hold values from -6 to 6
- down_weight: bfloat16 [4, 14336, 1792], P('rep', 'fsdp'), may hold values from -6 to 6
- momentum_up: bfloat16 [4, 14336, 1792], P('rep', 'fsdp'), may hold values from -4.1875 to 4.1875
- momentum_down: bfloat16 [4, 14336, 1792], P('rep', 'fsdp'), may hold values from -4.1875 to 4.1875
- variance_up: bfloat16 [4, 14336, 1792], P('rep', 'fsdp'), may hold values from 0.25 to 4
- variance_down: bfloat16 [4, 14336, 1792], P('rep', 'fsdp'), may hold values from 0.25 to 4
- step_index: int32 [1], replicated, may hold values from 1 to 16
Outputs:
- mixed_up: bfloat16 [4, 14336, 1792], P('rep', 'fsdp')
- mixed_down: bfloat16 [4, 14336, 1792], P('rep', 'fsdp')
- moment_up: bfloat16 [4, 14336, 1792], P('rep', 'fsdp')
- moment_down: bfloat16 [4, 14336, 1792], P('rep', 'fsdp')
- squares_up: bfloat16 [4, 14336, 1792], P('rep', 'fsdp')
- squares_down: bfloat16 [4, 14336, 1792], P('rep', 'fsdp')
The draws below stay inside these ranges and needn't reach their ends.
All inputs are finite; a program needn't handle non-finite values.
Results may differ from the reference program's by a relative error of at most 0.0052.
Values may be sent and summed in bfloat16 or wider, within the bound.
No kernel may reach another device: no remote copies, remote signals or barrier semaphores. Data moves between devices by JAX's collectives and lax.ppermute only.
A program may use at most 128 MiB of HBM per device.

```python
import math
import jax
import jax.numpy as jnp
from jax import lax

D = 1792
FF = 14336
TOKENS = 4096
REPS = 4


def block_scale(key, dims, cuts, least, top_value):
    loudness, own = 1.0, jax.random.fold_in(key, 6)
    for position, shards_of in cuts:
        steps = jnp.exp(jax.random.uniform(jax.random.fold_in(own, position), (shards_of,), jnp.float32, least / len(cuts), top_value / len(cuts)))
        loudness = loudness * jnp.repeat(steps, dims[position] // shards_of).reshape([-1 if axis == position else 1 for axis in range(len(dims))])
    return loudness


def gaussian(key, dims, deviation, bound, pieces=(), held_as=jnp.bfloat16):
    loudness = block_scale(key, dims, pieces, -0.22, 0.18) if pieces else 1.0
    entries = jax.random.normal(key, dims, jnp.float32) * deviation * loudness
    return jnp.minimum(jnp.maximum(entries, -bound), bound).astype(held_as)


def setup_inputs(seed: int = 0) -> dict:
    splits = jax.random.split(jax.random.key(seed), 10)
    return {
        "inputs": gaussian(splits[0], (REPS, TOKENS, D), 1.0, 6.0, ((0, 4), (1, 32))),
        "cotangent": gaussian(splits[1], (REPS, TOKENS, D), 3.0, 18.0, ((0, 4), (1, 32))),
        "up_weight": gaussian(splits[2], (REPS, FF, D), 1.0, 6.0, ((0, 4), (1, 32))),
        "down_weight": gaussian(splits[3], (REPS, FF, D), 1.0, 6.0, ((0, 4), (1, 32))),
        "momentum_up": gaussian(splits[4], (REPS, FF, D), 0.7, 4.1875, ((0, 4), (1, 32))),
        "momentum_down": gaussian(splits[5], (REPS, FF, D), 0.7, 4.1875, ((0, 4), (1, 32))),
        "variance_up": jnp.clip(jnp.exp(math.log(4.0) - 2.7725887 * jax.random.uniform(splits[6], (REPS, FF, D), jnp.float32) ** block_scale(splits[6], (REPS, FF, D), ((0, 4), (1, 32)), -0.2, 0.2)), 0.25, 4.0).astype(jnp.bfloat16),
        "variance_down": jnp.clip(jnp.exp(math.log(4.0) - 2.7725887 * jax.random.uniform(splits[7], (REPS, FF, D), jnp.float32) ** block_scale(splits[7], (REPS, FF, D), ((0, 4), (1, 32)), -0.2, 0.2)), 0.25, 4.0).astype(jnp.bfloat16),
        "step_index": jax.random.randint(splits[8], (1,), 1, 17).astype(jnp.int32),
    }


beta_one = 0.9
beta_two = 0.95
learn_rate = 0.05
adam_eps = 1e-08
norm_eps = 1e-06
root_coef = math.sqrt(2.0 / math.pi)

def gelu_pair(pre):
    inner = root_coef * (pre + 0.044715 * pre * pre * pre)
    tangent = jnp.tanh(inner)
    value = 0.5 * pre * (1.0 + tangent)
    slope = 0.5 * (1.0 + tangent) + 0.5 * pre * (1.0 - tangent * tangent) * root_coef * (1.0 + 3.0 * 0.044715 * pre * pre)
    return (value, slope)

def normalize(rows):
    wide = rows.astype(jnp.float32)
    factor = lax.rsqrt(lax.optimization_barrier(jnp.mean(wide * wide, axis=-1, keepdims=True)) + norm_eps)
    return (wide * factor).astype(jnp.bfloat16)

def adam_step(weight, first, second, grad, bias_one, bias_two):
    first_new = beta_one * first.astype(jnp.float32) + (1.0 - beta_one) * grad
    second_new = beta_two * second.astype(jnp.float32) + (1.0 - beta_two) * grad * grad
    update = learn_rate * (first_new / bias_one) / (jnp.sqrt(second_new / bias_two) + adam_eps)
    moved = (weight.astype(jnp.float32) - update).astype(jnp.bfloat16)
    return (moved, first_new.astype(jnp.bfloat16), second_new.astype(jnp.bfloat16))

def group_grads(rows_in, tangent, up_rows, down_rows):
    up_scale = 1.0 / math.sqrt(D)
    down_scale = 1.0 / math.sqrt(FF)
    normed = normalize(rows_in)
    pre = up_scale * jnp.dot(normed, up_rows.T, preferred_element_type=jnp.float32)
    value, slope = gelu_pair(pre)
    hidden = value.astype(jnp.bfloat16)
    grad_down = down_scale * jnp.dot(hidden.T, tangent, preferred_element_type=jnp.float32)
    back = down_scale * jnp.dot(tangent, down_rows.T, preferred_element_type=jnp.float32)
    delta = (back * slope).astype(jnp.bfloat16)
    grad_up = up_scale * jnp.dot(delta.T, normed, preferred_element_type=jnp.float32)
    return (grad_up, grad_down)

def reference(inputs, cotangent, up_weight, down_weight, momentum_up, momentum_down, variance_up, variance_down, step_index):
    count = step_index[0].astype(jnp.float32)
    bias_one = 1.0 - jnp.exp(count * math.log(beta_one))
    bias_two = 1.0 - jnp.exp(count * math.log(beta_two))
    results = []
    for group in range(REPS):
        grad_up, grad_down = group_grads(inputs[group], cotangent[group], up_weight[group], down_weight[group])
        upper = adam_step(up_weight[group], momentum_up[group], variance_up[group], grad_up, bias_one, bias_two)
        lower = adam_step(down_weight[group], momentum_down[group], variance_down[group], grad_down, bias_one, bias_two)
        results.append(upper + lower)
    stacked = [jnp.stack([item[k] for item in results]) for k in range(6)]
    levels = max(REPS.bit_length() - 1, 1)
    hop = jnp.left_shift(jnp.int32(1), (step_index[0] % levels).astype(jnp.int32))
    peer_up = jnp.roll(stacked[0], hop, axis=0)
    peer_down = jnp.roll(stacked[3], hop, axis=0)
    mixed_up = ((stacked[0].astype(jnp.float32) + peer_up.astype(jnp.float32)) * 0.5).astype(jnp.bfloat16)
    mixed_down = ((stacked[3].astype(jnp.float32) + peer_down.astype(jnp.float32)) * 0.5).astype(jnp.bfloat16)
    return (mixed_up, mixed_down, stacked[1], stacked[4], stacked[2], stacked[5])
```

```python
import functools
import math

import jax
import jax.numpy as jnp
from jax import lax
from jax.experimental import pallas as pl
from jax.experimental.pallas import tpu as pltpu
from jax.sharding import PartitionSpec as P

D = 1792
FF = 14336

beta_one = 0.9
beta_two = 0.95
learn_rate = 0.05
adam_eps = 1e-08
norm_eps = 1e-06
root_coef = math.sqrt(2.0 / math.pi)
up_scale = 1.0 / math.sqrt(D)
down_scale = 1.0 / math.sqrt(FF)

ROWS = 128
HELD = 448
PARTS = 4
WEIGHT_PARTS = 2
NZ, NX, NY = 4, 2, 4


def moved(block, place):
    route = []
    for z in range(NZ):
        for x in range(NX):
            for y in range(NY):
                a, b, c = place(z, x, y)
                route.append(((z * NX + x) * NY + y, (a % NZ * NX + b) * NY + c))
    return lax.ppermute(block, "fsdp", route)


def z_up(z, x, y):
    return z + 1, x, y


def z_down(z, x, y):
    return z - 1, x, y


def z_over(z, x, y):
    return z + 2, x, y


def x_other(z, x, y):
    return z, 1 - x, y


def y_same_half(z, x, y):
    return z, x, 3 - y


def diagonal(z, x, y):
    return z, 1 - x, 3 - y


def y_sharing(z, x, y):
    return z, x, y ^ 1


def gelu_pair(pre):
    inner = root_coef * (pre + 0.044715 * pre * pre * pre)
    tangent = jnp.tanh(inner)
    value = 0.5 * pre * (1.0 + tangent)
    slope = 0.5 * (1.0 + tangent) + 0.5 * pre * (1.0 - tangent * tangent) * root_coef * (
        1.0 + 3.0 * 0.044715 * pre * pre
    )
    return (value, slope)


def normalize(rows):
    wide = rows.astype(jnp.float32)
    factor = lax.rsqrt(jnp.mean(wide * wide, axis=-1, keepdims=True) + norm_eps)
    return (wide * factor).astype(jnp.bfloat16)


def adam_step(weight, first, second, grad, bias_one, bias_two):
    first_new = beta_one * first.astype(jnp.float32) + (1.0 - beta_one) * grad
    second_new = beta_two * second.astype(jnp.float32) + (1.0 - beta_two) * grad * grad
    update = learn_rate * (first_new / bias_one) / (jnp.sqrt(second_new / bias_two) + adam_eps)
    moved = (weight.astype(jnp.float32) - update).astype(jnp.bfloat16)
    return (moved, first_new.astype(jnp.bfloat16), second_new.astype(jnp.bfloat16))


contract_last = (((1,), (1,)), ((), ()))
VMEM_LIMIT = 56 * 1024 * 1024


def hidden_kernel(tile, widths, *refs):
    count = len(widths)
    up_ref, down_ref = refs[0], refs[1]
    blocks = refs[2 : 2 + count]
    hidden_ref, delta_ref = refs[2 + count :]
    start = 0
    for block, width in zip(blocks, widths):

        def step(i, carry, block=block, start=start):
            rows = pl.ds(pl.multiple_of(i * tile, tile), tile)
            cols = pl.ds(pl.multiple_of(start + i * tile, tile), tile)
            pre = up_scale * lax.dot_general(
                up_ref[...], block[0, rows], contract_last, preferred_element_type=jnp.float32
            )
            back = down_scale * lax.dot_general(
                down_ref[...], block[1, rows], contract_last, preferred_element_type=jnp.float32
            )
            value, slope = gelu_pair(pre)
            hidden_ref[:, cols] = value.astype(jnp.bfloat16)
            delta_ref[:, cols] = (back * slope).astype(jnp.bfloat16)
            return carry

        lax.fori_loop(0, width // tile, step, 0)
        start += width


def hidden_and_delta(up, down, blocks):
    tile = 128
    widths = tuple(b.shape[1] for b in blocks)
    total = sum(widths)
    rows = up.shape[0]
    out = jax.ShapeDtypeStruct((rows, total), jnp.bfloat16)
    whole = pl.BlockSpec(memory_space=pltpu.VMEM)
    return pl.pallas_call(
        functools.partial(hidden_kernel, tile, widths),
        out_shape=(out, out),
        in_specs=[whole] * (2 + len(blocks)),
        out_specs=(whole, whole),
        compiler_params=pltpu.CompilerParams(vmem_limit_bytes=VMEM_LIMIT),
        cost_estimate=pl.CostEstimate(
            flops=4 * rows * total * D,
            bytes_accessed=4 * total * D + 4 * rows * D + 4 * rows * total,
            transcendentals=rows * total,
        ),
    )(up, down, *blocks)


def grads_kernel(groups, *refs):
    count = len(groups)
    hidden = refs[:count]
    delta = refs[count : 2 * count]
    blocks = refs[2 * count : -1]
    out_ref = refs[-1]
    for which, parts in ((0, delta), (1, hidden)):
        total = None
        position = 0
        for part, widths in zip(parts, groups):
            start = 0
            for width in widths:
                term = jnp.dot(
                    part[:, start : start + width],
                    blocks[position][which],
                    preferred_element_type=jnp.float32,
                )
                total = term if total is None else total + term
                start += width
                position += 1
        scale = up_scale if which == 0 else down_scale
        out_ref[which] = (scale * total).astype(out_ref.dtype)


def partial_grads(hidden, delta, token_groups, first_row, rows, dtype):
    groups = tuple(tuple(b.shape[1] for b in g) for g in token_groups)
    blocks = [b for g in token_groups for b in g]
    tile = 256
    at = first_row // rows
    in_specs = [
        pl.BlockSpec((rows, h.shape[1]), lambda j, at=at: (at, 0)) for h in hidden + delta
    ] + [pl.BlockSpec((2, b.shape[1], tile), lambda j: (0, 0, j)) for b in blocks]
    total = sum(sum(g) for g in groups)
    return pl.pallas_call(
        functools.partial(grads_kernel, groups),
        out_shape=jax.ShapeDtypeStruct((2, rows, D), dtype),
        grid=(D // tile,),
        in_specs=in_specs,
        out_specs=pl.BlockSpec((2, rows, tile), lambda j: (0, 0, j)),
        compiler_params=pltpu.CompilerParams(vmem_limit_bytes=VMEM_LIMIT),
        cost_estimate=pl.CostEstimate(
            flops=4 * rows * total * D,
            bytes_accessed=4 * total * D + 4 * rows * D + 4 * rows * total,
            transcendentals=0,
        ),
    )(*hidden, *delta, *blocks)


def on_device(
    inputs,
    cotangent,
    up_weight,
    down_weight,
    momentum_up,
    momentum_down,
    variance_up,
    variance_down,
    step_index,
):
    up, down = up_weight[0], down_weight[0]
    own = jnp.stack([normalize(inputs[0]), cotangent[0]])
    half = ROWS // 2

    a, b = own[:, :half], own[:, half:]
    a_all = jnp.concatenate([a, moved(a, x_other), moved(a, y_same_half), moved(a, diagonal)], 1)
    b_all = jnp.concatenate([b, moved(b, z_up), moved(b, z_down), moved(b, z_over)], 1)

    part = HELD // WEIGHT_PARTS
    shared = []
    for i in range(WEIGHT_PARTS):
        rows = slice(i * part, (i + 1) * part)
        shared.append((moved(up[rows], y_sharing), moved(down[rows], y_sharing)))

    mid = 2 * half
    a_up, a_down = moved(a_all, z_up), moved(a_all, z_down)
    b_x, b_y = moved(b_all, x_other), moved(b_all, y_same_half)
    a_over = [moved(a_up[:, :mid], z_up), moved(a_down[:, mid:], z_down)]
    b_over = [moved(b_x[:, :mid], y_same_half), moved(b_y[:, mid:], x_other)]
    groups = [[a_all, b_all], [a_up, a_down, b_x, b_y], a_over + b_over]

    own_pairs = [hidden_and_delta(up, down, g) for g in groups]
    shared_pairs = [[hidden_and_delta(u, d, g) for g in groups] for u, d in shared]

    count = step_index[0].astype(jnp.float32)
    bias_one = 1.0 - jnp.exp(count * math.log(beta_one))
    bias_two = 1.0 - jnp.exp(count * math.log(beta_two))

    def finish(hop):
        rows = HELD // PARTS
        results = []
        sizes = 4
        route = [(g, (g + hop) % sizes) for g in range(sizes)]
        for i in range(PARTS):
            first = i * rows
            pairs = shared_pairs[first // part]
            theirs = partial_grads(
                [p[0] for p in pairs], [p[1] for p in pairs], groups, first % part, rows, jnp.bfloat16
            )
            arrived = moved(theirs, y_sharing)
            mine = partial_grads(
                [p[0] for p in own_pairs], [p[1] for p in own_pairs], groups, first, rows, jnp.float32
            )
            grad = mine + arrived.astype(jnp.float32)
            at = slice(first, first + rows)
            up_new = adam_step(
                up[at], momentum_up[0, at], variance_up[0, at], grad[0], bias_one, bias_two
            )
            down_new = adam_step(
                down[at], momentum_down[0, at], variance_down[0, at], grad[1], bias_one, bias_two
            )
            stacked = jnp.stack([up_new[0], down_new[0]])
            other = lax.ppermute(stacked, "rep", route)
            mixed = (
                (stacked.astype(jnp.float32) + other.astype(jnp.float32)) * 0.5
            ).astype(jnp.bfloat16)
            results.append((mixed[0], mixed[1], up_new[1], down_new[1], up_new[2], down_new[2]))
        return tuple(jnp.concatenate(parts, 0) for parts in zip(*results))

    outs = lax.cond(step_index[0] % 2 == 0, lambda: finish(1), lambda: finish(2))
    return tuple(o[None] for o in outs)


def solution(mesh):
    shard = P("rep", "fsdp", None)
    return jax.shard_map(
        on_device,
        mesh=mesh,
        in_specs=(shard,) * 8 + (P(),),
        out_specs=(shard,) * 6,
        check_vma=False,
    )
```

```python
import functools
import math

import jax
import jax.numpy as jnp
from jax import lax
from jax.experimental import pallas as pl
from jax.experimental.pallas import tpu as pltpu
from jax.sharding import PartitionSpec as P

D = 1792
FF = 14336

beta_one = 0.9
beta_two = 0.95
learn_rate = 0.05
adam_eps = 1e-08
norm_eps = 1e-06
root_coef = math.sqrt(2.0 / math.pi)
up_scale = 1.0 / math.sqrt(D)
down_scale = 1.0 / math.sqrt(FF)

ROWS = 128
HELD = 448
SHARED = 2 * HELD
FIRST_ROWS = 160
TOKENS = 2048
COLUMNS = 256
NZ, NX, NY = 4, 2, 4


def moved(block, place):
    route = []
    for z in range(NZ):
        for x in range(NX):
            for y in range(NY):
                a, b, c = place(z, x, y)
                route.append(((z * NX + x) * NY + y, (a % NZ * NX + b) * NY + c))
    return lax.ppermute(block, "fsdp", route)


def z_up(z, x, y):
    return z + 1, x, y


def z_down(z, x, y):
    return z - 1, x, y


def z_over(z, x, y):
    return z + 2, x, y


def x_other(z, x, y):
    return z, 1 - x, y


def y_same_half(z, x, y):
    return z, x, 3 - y


def diagonal(z, x, y):
    return z, 1 - x, 3 - y


def y_sharing(z, x, y):
    return z, x, y ^ 1


def gelu_pair(pre):
    square = pre * pre
    tangent = jnp.tanh(pre * (root_coef + (root_coef * 0.044715) * square))
    half = 0.5 * tangent + 0.5
    value = pre * half
    slope = half + pre * (0.5 - 0.5 * tangent * tangent) * (
        root_coef + (3.0 * 0.044715 * root_coef) * square
    )
    return (value, slope)


def normalize(rows):
    wide = rows.astype(jnp.float32)
    factor = lax.rsqrt(jnp.mean(wide * wide, axis=-1, keepdims=True) + norm_eps)
    return (wide * factor).astype(jnp.bfloat16)


contract_last = (((1,), (1,)), ((), ()))
ANY = pl.BlockSpec(memory_space=pl.ANY)
PARAMS = pltpu.CompilerParams(vmem_limit_bytes=56 * 1024 * 1024)


def cost(flops, moved_bytes):
    return pl.CostEstimate(flops=2 * flops, bytes_accessed=moved_bytes, transcendentals=0)


def size(x):
    return math.prod(x.shape) * x.dtype.itemsize


def copies_kernel(plan, count_in, count_out, *refs):
    ins, outs, sems = refs[:count_in], refs[count_in : count_in + count_out], refs[-1]
    going = []
    for k, (i, source, o, target) in enumerate(plan):
        going.append(pltpu.make_async_copy(ins[i].at[source], outs[o].at[target], sems.at[k]))
        going[-1].start()
    for copy in going:
        copy.wait()


def copies(plan, arrays, shapes, after=()):
    out = [jax.ShapeDtypeStruct(s, jnp.bfloat16) for s in shapes]
    arrays = list(arrays) + list(after)
    return pl.pallas_call(
        functools.partial(copies_kernel, plan, len(arrays), len(out)),
        out_shape=out,
        in_specs=[ANY] * len(arrays),
        out_specs=[ANY] * len(out),
        scratch_shapes=[pltpu.SemaphoreType.DMA((len(plan),))],
        compiler_params=PARAMS,
        cost_estimate=cost(0, 2 * sum(size(o) for o in out)),
    )(*arrays)


def hidden_kernel(jobs, sizes, pieces, count_extra, tile, *refs):
    up_ref, down_ref = refs[0], refs[1]
    shared = refs[2 : 2 + len(pieces)]
    blocks = refs[2 + len(pieces) : 2 + len(pieces) + len(sizes)]
    at = 2 + len(pieces) + len(sizes) + count_extra
    hidden_out, delta_out, weights, tokens, hidden, delta, weight_sem, token_sem, out_sem = refs[at:]
    loads = [
        pltpu.make_async_copy(up_ref, weights.at[0, pl.ds(0, HELD)], weight_sem.at[0]),
        pltpu.make_async_copy(down_ref, weights.at[1, pl.ds(0, HELD)], weight_sem.at[1]),
    ]
    for k, (ref, (first, rows)) in enumerate(zip(shared, pieces)):
        loads.append(pltpu.make_async_copy(ref, weights.at[:, pl.ds(first, rows)], weight_sem.at[2 + k]))
    first = 0
    for k, (ref, count) in enumerate(zip(blocks, sizes)):
        loads.append(pltpu.make_async_copy(ref, tokens.at[:, pl.ds(first, count)], token_sem.at[k]))
        first += count
    for load in loads:
        load.start()
    for load in loads:
        load.wait()
    stores = []
    for k, (row, end, token, count, column) in enumerate(jobs):

        def step(i, carry, row=row, end=end, token=token):
            at = pl.ds(pl.multiple_of(token + i * tile, tile), tile)
            pre = up_scale * lax.dot_general(
                weights[0, row:end], tokens[0, at], contract_last, preferred_element_type=jnp.float32
            )
            back = down_scale * lax.dot_general(
                weights[1, row:end], tokens[1, at], contract_last, preferred_element_type=jnp.float32
            )
            value, slope = gelu_pair(pre)
            hidden[row:end, at] = value.astype(jnp.bfloat16)
            delta[row:end, at] = (back * slope).astype(jnp.bfloat16)
            return carry

        lax.fori_loop(0, count // tile, step, 0)
        for j, (source, target) in enumerate(((hidden, hidden_out), (delta, delta_out))):
            store = pltpu.make_async_copy(
                source.at[pl.ds(row, end - row), pl.ds(token, count)],
                target.at[pl.ds(row, end - row), pl.ds(column, count)],
                out_sem.at[2 * k + j],
            )
            store.start()
            stores.append(store)
    for store in stores:
        store.wait()


def hidden_step(jobs, up, down, shared, blocks, results=(), after=()):
    sizes = tuple(b.shape[1] for b in blocks)
    pieces, first = [], HELD
    for w in shared:
        pieces.append((first, w.shape[1]))
        first += w.shape[1]
    total = sum(sizes)
    out = jax.ShapeDtypeStruct((SHARED, TOKENS), jnp.bfloat16)
    operands = [up, down, *shared, *blocks]
    aliases = {len(operands) + k: k for k in range(len(results))}
    operands += [*results, *after]
    flops = sum(4 * (end - row) * count * D for row, end, _, count, _ in jobs)
    return pl.pallas_call(
        functools.partial(hidden_kernel, jobs, sizes, tuple(pieces), len(results) + len(after), 256),
        out_shape=(out, out),
        in_specs=[ANY] * len(operands),
        out_specs=(ANY, ANY),
        input_output_aliases=aliases,
        scratch_shapes=[
            pltpu.VMEM((2, first, D), jnp.bfloat16),
            pltpu.VMEM((2, total, D), jnp.bfloat16),
            pltpu.VMEM((SHARED, total), jnp.bfloat16),
            pltpu.VMEM((SHARED, total), jnp.bfloat16),
            pltpu.SemaphoreType.DMA((2 + len(shared),)),
            pltpu.SemaphoreType.DMA((len(blocks),)),
            pltpu.SemaphoreType.DMA((2 * len(jobs),)),
        ],
        compiler_params=PARAMS,
        cost_estimate=cost(flops, 4 * (total + first) * D + 4 * first * total),
    )(*operands)


def chunk_grads(hidden, delta, blocks, which):
    side, scale = ((delta, up_scale), (hidden, down_scale))[which]
    total, first = None, 0
    for block in blocks:
        count = block.shape[1]
        term = jnp.dot(
            side[:, first : first + count], block[which], preferred_element_type=jnp.float32
        )
        total = term if total is None else total + term
        first += count
    return scale * total


def theirs_kernel(count, hidden, delta, *refs):
    out_ref = refs[-1]
    for which in (0, 1):
        out_ref[which] = chunk_grads(hidden, delta, refs[:count], which).astype(jnp.bfloat16)


def token_specs(blocks, c):
    return [pl.BlockSpec((2, b.shape[1], COLUMNS), lambda j, c=c: (0, 0, c)) for b in blocks]


def theirs_chunk(c, hidden, delta, blocks, after):
    rows = pl.BlockSpec((HELD, TOKENS), lambda j: (1, 0))
    return pl.pallas_call(
        functools.partial(theirs_kernel, len(blocks)),
        out_shape=jax.ShapeDtypeStruct((2, HELD, COLUMNS), jnp.bfloat16),
        grid=(1,),
        in_specs=[rows, rows] + token_specs(blocks, c) + [ANY] * len(after),
        out_specs=pl.BlockSpec((2, HELD, COLUMNS), lambda j: (0, 0, 0)),
        compiler_params=PARAMS,
        cost_estimate=cost(4 * HELD * TOKENS * COLUMNS, 4 * TOKENS * (HELD + COLUMNS)),
    )(hidden, delta, *blocks, *after)


def adam_kernel(count, *refs):
    hidden, delta = refs[:2]
    blocks = refs[2 : 2 + count]
    bias, arrived = refs[2 + count], refs[3 + count]
    state = refs[4 + count : 10 + count]
    moved_ref = refs[-5]
    outs = refs[-4:]
    for which in (0, 1):
        weight, first, second = state[3 * which : 3 * which + 3]
        grad = chunk_grads(hidden, delta, blocks, which) + arrived[which].astype(jnp.float32)
        first_new = beta_one * first[...].astype(jnp.float32) + (1.0 - beta_one) * grad
        second_new = beta_two * second[...].astype(jnp.float32) + (1.0 - beta_two) * grad * grad
        update = (learn_rate * bias[0]) * first_new / (jnp.sqrt(second_new * bias[1]) + adam_eps)
        moved_ref[which] = (weight[...].astype(jnp.float32) - update).astype(jnp.bfloat16)
        outs[2 * which][...] = first_new.astype(jnp.bfloat16)
        outs[2 * which + 1][...] = second_new.astype(jnp.bfloat16)


def adam_chunk(c, hidden, delta, blocks, bias, arrived, state, results):
    rows = pl.BlockSpec((HELD, TOKENS), lambda j: (0, 0))
    column = pl.BlockSpec((HELD, COLUMNS), lambda j, c=c: (0, c))
    pair = pl.BlockSpec((2, HELD, COLUMNS), lambda j: (0, 0, 0))
    whole = jax.ShapeDtypeStruct((HELD, D), jnp.bfloat16)
    operands = [hidden, delta, *blocks, bias, arrived, *state]
    aliases = {len(operands) + k: 1 + k for k in range(len(results))}
    return pl.pallas_call(
        functools.partial(adam_kernel, len(blocks)),
        out_shape=[jax.ShapeDtypeStruct((2, HELD, COLUMNS), jnp.bfloat16)] + [whole] * 4,
        grid=(1,),
        in_specs=[rows, rows]
        + token_specs(blocks, c)
        + [pl.BlockSpec(memory_space=pltpu.SMEM), pair]
        + [column] * 6
        + [ANY] * len(results),
        out_specs=[pair] + [column] * 4,
        input_output_aliases=aliases,
        compiler_params=PARAMS,
        cost_estimate=cost(
            4 * HELD * TOKENS * COLUMNS, 4 * TOKENS * (HELD + COLUMNS) + 24 * HELD * COLUMNS
        ),
    )(*operands, *results)


def mix_kernel(own, other, *refs):
    for which in (0, 1):
        both = own[which].astype(jnp.float32) + other[which].astype(jnp.float32)
        refs[which - 2][...] = (both * 0.5).astype(jnp.bfloat16)


def mix_chunk(c, own, other, results):
    pair = pl.BlockSpec((2, HELD, COLUMNS), lambda j: (0, 0, 0))
    column = pl.BlockSpec((HELD, COLUMNS), lambda j, c=c: (0, c))
    whole = jax.ShapeDtypeStruct((HELD, D), jnp.bfloat16)
    return pl.pallas_call(
        mix_kernel,
        out_shape=[whole] * 2,
        grid=(1,),
        in_specs=[pair, pair] + [ANY] * len(results),
        out_specs=[column] * 2,
        input_output_aliases={2 + k: k for k in range(len(results))},
        compiler_params=PARAMS,
        cost_estimate=cost(0, 12 * HELD * COLUMNS),
    )(own, other, *results)


def on_device(
    inputs,
    cotangent,
    up_weight,
    down_weight,
    momentum_up,
    momentum_down,
    variance_up,
    variance_down,
    step_index,
):
    up, down = up_weight[0], down_weight[0]
    half = ROWS // 2
    whole = slice(None)

    own = jnp.stack([normalize(inputs[0]), cotangent[0]])
    a, b = own[:, :half], own[:, half:]
    first_weights = moved(jnp.stack([up[:FIRST_ROWS], down[:FIRST_ROWS]]), y_sharing)
    pieces = [a, moved(a, x_other), moved(a, y_same_half), moved(a, diagonal)]
    pieces += [b, moved(b, z_up), moved(b, z_down), moved(b, z_over)]
    plan = [
        (k, whole, k // 4, (whole, pl.ds(k % 4 * half, half))) for k in range(8)
    ]
    rest = HELD - FIRST_ROWS
    plan += [(8 + k, pl.ds(FIRST_ROWS, rest), 2, k) for k in range(2)]
    a_all, b_all, second_weights = copies(
        tuple(plan),
        pieces + [up, down],
        [(2, 4 * half, D), (2, 4 * half, D), (2, rest, D)],
        [first_weights],
    )

    second_sent = moved(second_weights, y_sharing)
    a_up, a_down = moved(a_all, z_up), moved(a_all, z_down)
    b_x, b_y = moved(b_all, x_other), moved(b_all, y_same_half)
    middle = HELD + FIRST_ROWS
    job = (0, middle, 0, 512, 0)
    hidden, delta = hidden_step((job,), up, down, [first_weights], [a_all, b_all])

    mid = 2 * half
    near, far = (whole, pl.ds(0, mid)), (whole, pl.ds(mid, mid))
    plan = ((0, near, 0, whole), (1, far, 1, whole), (2, near, 2, whole), (3, far, 3, whole))
    cut = copies(plan, [a_up, a_down, b_x, b_y], [(2, mid, D)] * 4, [second_sent, hidden])
    last = [
        moved(cut[0], z_up),
        moved(cut[1], z_down),
        moved(cut[2], y_same_half),
        moved(cut[3], x_other),
    ]
    shared = [first_weights, second_sent]
    jobs = ((0, SHARED, 0, 1024, 512), (middle, SHARED, 1024, 512, 0))
    hidden, delta = hidden_step(
        jobs, up, down, shared, [a_up, a_down, b_x, b_y, a_all, b_all], (hidden, delta), cut[:1]
    )
    jobs = ((0, SHARED, 0, 512, 1536),)
    hidden, delta = hidden_step(jobs, up, down, shared, last, (hidden, delta))
    blocks = [a_all, b_all, a_up, a_down, b_x, b_y, *last]

    count = step_index[0].astype(jnp.float32)
    bias_one = 1.0 - jnp.exp(count * math.log(beta_one))
    bias_two = 1.0 - jnp.exp(count * math.log(beta_two))
    bias = jnp.stack([1.0 / bias_one, 1.0 / bias_two])
    state = [up, momentum_up[0], variance_up[0], down, momentum_down[0], variance_down[0]]

    def finish(hop):
        route = [(g, (g + hop) % 4) for g in range(4)]
        news, mixed, updated = [], [], []
        for c in range(D // COLUMNS):
            after = updated[c - 2 : c - 1] if c >= 2 else []
            theirs = theirs_chunk(c, hidden, delta, blocks, after)
            arrived = moved(theirs, y_sharing)
            out = adam_chunk(c, hidden, delta, blocks, bias, arrived, state, news)
            updated.append(out[0])
            news = out[1:]
            other = lax.ppermute(out[0], "rep", route)
            mixed = mix_chunk(c, out[0], other, mixed)
        return mixed[0], mixed[1], news[0], news[2], news[1], news[3]

    outs = lax.cond(step_index[0] % 2 == 0, lambda: finish(1), lambda: finish(2))
    return tuple(o[None] for o in outs)


def solution(mesh):
    shard = P("rep", "fsdp", None)
    return jax.shard_map(
        on_device,
        mesh=mesh,
        in_specs=(shard,) * 8 + (P(),),
        out_specs=(shard,) * 6,
        check_vma=False,
    )
```

```python
import functools
import math

import jax
import jax.numpy as jnp
from jax import lax
from jax.experimental import pallas as pl
from jax.experimental.pallas import tpu as pltpu
from jax.sharding import PartitionSpec as P

D = 1792
FF = 14336

beta_one = 0.9
beta_two = 0.95
learn_rate = 0.05
adam_eps = 1e-08
norm_eps = 1e-06
root_coef = math.sqrt(2.0 / math.pi)
up_scale = 1.0 / math.sqrt(D)
down_scale = 1.0 / math.sqrt(FF)

ROWS = 128
HELD = 448
SHARED = 2 * HELD
FIRST_ROWS = 192
TOKENS = 2048
CHUNKS = ((0, 128),) + tuple((256 * k, 256) for k in range(1, 7)) + ((128, 128),)
NZ, NX, NY = 4, 2, 4


def moved(block, place):
    route = []
    for z in range(NZ):
        for x in range(NX):
            for y in range(NY):
                a, b, c = place(z, x, y)
                route.append(((z * NX + x) * NY + y, (a % NZ * NX + b) * NY + c))
    return lax.ppermute(block, "fsdp", route)


def z_up(z, x, y):
    return z + 1, x, y


def z_down(z, x, y):
    return z - 1, x, y


def z_over(z, x, y):
    return z + 2, x, y


def x_other(z, x, y):
    return z, 1 - x, y


def y_same_half(z, x, y):
    return z, x, 3 - y


def diagonal(z, x, y):
    return z, 1 - x, 3 - y


def y_sharing(z, x, y):
    return z, x, y ^ 1


def gelu_pair(pre):
    square = pre * pre
    tangent = jnp.tanh(pre * (root_coef + (root_coef * 0.044715) * square))
    half = 0.5 * tangent + 0.5
    value = pre * half
    slope = half + pre * (0.5 - 0.5 * tangent * tangent) * (
        root_coef + (3.0 * 0.044715 * root_coef) * square
    )
    return (value, slope)


def normalize(rows):
    wide = rows.astype(jnp.float32)
    factor = lax.rsqrt(jnp.mean(wide * wide, axis=-1, keepdims=True) + norm_eps)
    return (wide * factor).astype(jnp.bfloat16)


contract_last = (((1,), (1,)), ((), ()))
ANY = pl.BlockSpec(memory_space=pl.ANY)


def vmem(mebibytes):
    return pltpu.CompilerParams(vmem_limit_bytes=mebibytes * 1024 * 1024)


def cost(flops, moved_bytes):
    return pl.CostEstimate(flops=2 * flops, bytes_accessed=moved_bytes, transcendentals=0)


def copies_kernel(plan, count_in, count_out, *refs):
    ins, outs = refs[:count_in], refs[count_in : count_in + count_out]
    held = refs[count_in + count_out : -2]
    load_sem, store_sem = refs[-2:]
    loads, stores = [], []
    for k, (i, source, o, target) in enumerate(plan):
        loads.append(pltpu.make_async_copy(ins[i].at[source], held[k], load_sem.at[k]))
        stores.append(pltpu.make_async_copy(held[k], outs[o].at[target], store_sem.at[k]))
    for load in loads:
        load.start()
    for load, store in zip(loads, stores):
        load.wait()
        store.start()
    for store in stores:
        store.wait()


def copies(plan, parts, arrays, shapes, after=()):
    out = [jax.ShapeDtypeStruct(s, jnp.bfloat16) for s in shapes]
    arrays = list(arrays) + list(after)
    return pl.pallas_call(
        functools.partial(copies_kernel, plan, len(arrays), len(out)),
        out_shape=out,
        in_specs=[ANY] * len(arrays),
        out_specs=[ANY] * len(out),
        scratch_shapes=[pltpu.VMEM(shape, jnp.bfloat16) for shape in parts]
        + [pltpu.SemaphoreType.DMA((len(plan),))] * 2,
        compiler_params=vmem(16),
        cost_estimate=cost(0, 2 * sum(2 * math.prod(s) for s in shapes)),
    )(*arrays)


def hidden_kernel(jobs, sizes, pieces, skipped, kept, tile, *refs):
    arrays = refs[: len(pieces)]
    blocks = refs[len(pieces) : len(pieces) + len(sizes)]
    refs = refs[len(pieces) + len(sizes) + skipped :]
    weights, tokens, hidden, delta, weight_sem, token_sem, out_sem, keep_sem = refs[-8:]
    loads = []
    for k, (ref, (which, first, rows)) in enumerate(zip(arrays, pieces)):
        target = weights.at[:, pl.ds(first, rows)]
        if which is not None:
            target = weights.at[which, pl.ds(first, rows)]
        loads.append(pltpu.make_async_copy(ref, target, weight_sem.at[k]))
    first = 0
    for k, (ref, count) in enumerate(zip(blocks, sizes)):
        loads.append(pltpu.make_async_copy(ref, tokens.at[:, pl.ds(first, count)], token_sem.at[k]))
        first += count
    for load in loads:
        load.start()
    for load in loads:
        load.wait()
    stores = []
    if kept is not None:
        source = tokens.at[:, pl.ds(0, kept[1])]
        target = refs[4].at[:, pl.ds(kept[0], kept[1])]
        stores.append(pltpu.make_async_copy(source, target, keep_sem.at[0]))
        stores[-1].start()
    for k, (shared, row, end, token, count, place) in enumerate(jobs):

        def step(i, carry, row=row, end=end, token=token):
            at = pl.ds(pl.multiple_of(token + i * tile, tile), tile)
            pre = up_scale * lax.dot_general(
                weights[0, row:end], tokens[0, at], contract_last, preferred_element_type=jnp.float32
            )
            back = down_scale * lax.dot_general(
                weights[1, row:end], tokens[1, at], contract_last, preferred_element_type=jnp.float32
            )
            value, slope = gelu_pair(pre)
            hidden[row:end, at] = value.astype(jnp.bfloat16)
            delta[row:end, at] = (back * slope).astype(jnp.bfloat16)
            return carry

        lax.fori_loop(0, count // tile, step, 0)
        base = HELD if shared else 0
        for j, source in enumerate((hidden, delta)):
            store = pltpu.make_async_copy(
                source.at[pl.ds(row, end - row), pl.ds(token, count)],
                refs[2 * shared + j].at[pl.ds(row - base, end - row), pl.ds(place, count)],
                out_sem.at[2 * k + j],
            )
            store.start()
            stores.append(store)
    for store in stores:
        store.wait()


def hidden_step(jobs, pieces, arrays, blocks, results, kept=None, after=()):
    sizes = tuple(b.shape[1] for b in blocks)
    total = sum(sizes)
    top = max(first + rows for _, first, rows in pieces)
    half = jax.ShapeDtypeStruct((HELD, TOKENS), jnp.bfloat16)
    out = [half] * 4 + [jax.ShapeDtypeStruct((2, TOKENS, D), jnp.bfloat16)]
    operands = [*arrays, *blocks]
    aliases = {len(operands) + k: k for k in range(len(results))}
    operands += [*results, *after]
    flops = sum(4 * (end - row) * count * D for _, row, end, _, count, _ in jobs)
    skipped = len(results) + len(after)
    return pl.pallas_call(
        functools.partial(hidden_kernel, jobs, sizes, pieces, skipped, kept, 256),
        out_shape=out,
        in_specs=[ANY] * len(operands),
        out_specs=[ANY] * 5,
        input_output_aliases=aliases,
        scratch_shapes=[
            pltpu.VMEM((2, top, D), jnp.bfloat16),
            pltpu.VMEM((2, total, D), jnp.bfloat16),
            pltpu.VMEM((top, total), jnp.bfloat16),
            pltpu.VMEM((top, total), jnp.bfloat16),
            pltpu.SemaphoreType.DMA((len(pieces),)),
            pltpu.SemaphoreType.DMA((len(blocks),)),
            pltpu.SemaphoreType.DMA((2 * len(jobs),)),
            pltpu.SemaphoreType.DMA((1,)),
        ],
        compiler_params=vmem(40),
        cost_estimate=cost(flops, 4 * (total + top) * D + 4 * top * total),
    )(*operands)


def column_spec(c):
    first, width = CHUNKS[c]
    return pl.BlockSpec((HELD, width), lambda j: (0, first // width))


def token_spec(c):
    first, width = CHUNKS[c]
    return pl.BlockSpec((2, TOKENS, width), lambda j: (0, 0, first // width))


def pair_spec(c):
    return pl.BlockSpec((2, HELD, CHUNKS[c][1]), lambda j: (0, 0, 0))


all_rows = pl.BlockSpec((HELD, TOKENS), lambda j: (0, 0))


def theirs_kernel(hidden, delta, tokens, *refs):
    up_grad = jnp.dot(delta[...], tokens[0], preferred_element_type=jnp.float32)
    down_grad = jnp.dot(hidden[...], tokens[1], preferred_element_type=jnp.float32)
    refs[-1][0] = (up_scale * up_grad).astype(jnp.bfloat16)
    refs[-1][1] = (down_scale * down_grad).astype(jnp.bfloat16)


def theirs_chunk(c, hidden, delta, tokens, after):
    width = CHUNKS[c][1]
    return pl.pallas_call(
        theirs_kernel,
        out_shape=jax.ShapeDtypeStruct((2, HELD, width), jnp.bfloat16),
        grid=(1,),
        in_specs=[all_rows, all_rows, token_spec(c)] + [ANY] * len(after),
        out_specs=pair_spec(c),
        compiler_params=vmem(28),
        cost_estimate=cost(4 * HELD * TOKENS * width, 4 * TOKENS * (HELD + width)),
    )(hidden, delta, tokens, *after)


def adam_kernel(mixing, *refs):
    hidden, delta, tokens, bias, arrived = refs[:5]
    state = refs[5:11]
    outs = refs[-7:]
    for which, side, scale in ((0, delta, up_scale), (1, hidden, down_scale)):
        weight, first, second = state[3 * which : 3 * which + 3]
        grad = scale * jnp.dot(side[...], tokens[which], preferred_element_type=jnp.float32)
        grad = grad + arrived[which].astype(jnp.float32)
        first_new = beta_one * first[...].astype(jnp.float32) + (1.0 - beta_one) * grad
        second_new = beta_two * second[...].astype(jnp.float32) + (1.0 - beta_two) * grad * grad
        update = (learn_rate * bias[0]) * first_new / (jnp.sqrt(second_new * bias[1]) + adam_eps)
        outs[0][which] = (weight[...].astype(jnp.float32) - update).astype(jnp.bfloat16)
        outs[1 + 2 * which][...] = first_new.astype(jnp.bfloat16)
        outs[2 + 2 * which][...] = second_new.astype(jnp.bfloat16)
    if mixing:
        mix_kernel(refs[11], refs[12], *outs[-2:])


def mix_kernel(own, other, *refs):
    for which in (0, 1):
        both = own[which].astype(jnp.float32) + other[which].astype(jnp.float32)
        refs[which - 2][...] = (both * 0.5).astype(jnp.bfloat16)


whole = jax.ShapeDtypeStruct((HELD, D), jnp.bfloat16)


def adam_chunk(c, hidden, delta, tokens, bias, arrived, state, mixed, results):
    width = CHUNKS[c][1]
    operands = [hidden, delta, tokens, bias, arrived, *state, *mixed]
    aliases = {len(operands) + k: 1 + k for k in range(len(results))}
    before = max(c - 2, 0)
    return pl.pallas_call(
        functools.partial(adam_kernel, bool(mixed)),
        out_shape=[jax.ShapeDtypeStruct((2, HELD, width), jnp.bfloat16)] + [whole] * 6,
        grid=(1,),
        in_specs=[all_rows, all_rows, token_spec(c), pl.BlockSpec(memory_space=pltpu.SMEM), pair_spec(c)]
        + [column_spec(c)] * 6
        + [pair_spec(before)] * len(mixed)
        + [ANY] * len(results),
        out_specs=[pair_spec(c)] + [column_spec(c)] * 4 + [column_spec(before)] * 2,
        input_output_aliases=aliases,
        compiler_params=vmem(28),
        cost_estimate=cost(4 * HELD * TOKENS * width, 4 * TOKENS * (HELD + width) + 36 * HELD * width),
    )(*operands, *results)


def mix_chunk(c, own, other, results):
    return pl.pallas_call(
        mix_kernel,
        out_shape=[whole] * 2,
        grid=(1,),
        in_specs=[pair_spec(c)] * 2 + [ANY] * 2,
        out_specs=[column_spec(c)] * 2,
        input_output_aliases={2: 0, 3: 1},
        compiler_params=vmem(28),
        cost_estimate=cost(0, 12 * HELD * CHUNKS[c][1]),
    )(own, other, *results)


def on_device(
    inputs,
    cotangent,
    up_weight,
    down_weight,
    momentum_up,
    momentum_down,
    variance_up,
    variance_down,
    step_index,
):
    up, down = up_weight[0], down_weight[0]
    half, quarter = ROWS // 2, ROWS // 4
    every = slice(None)

    own = jnp.stack([normalize(inputs[0]), cotangent[0]])
    a, b = own[:, :half], own[:, half:]
    first_weights = moved(jnp.stack([up[:FIRST_ROWS], down[:FIRST_ROWS]]), y_sharing)
    a_x, a_y = moved(a, x_other), moved(a, y_same_half)
    b_up, b_down = moved(b, z_up), moved(b, z_down)
    a_far = [moved(a_x[:, :quarter], y_same_half), moved(a_y[:, quarter:], x_other)]
    b_far = [moved(b_up[:, :quarter], z_up), moved(b_down[:, quarter:], z_down)]
    a_all = jnp.concatenate([a, a_x, a_y, *a_far], 1)
    b_all = jnp.concatenate([b, b_up, b_down, *b_far], 1)
    rest = HELD - FIRST_ROWS
    plan = tuple((k, pl.ds(FIRST_ROWS, rest), 0, k) for k in (0, 1))
    (second_weights,) = copies(plan, [(rest, D)] * 2, [up, down], [(2, rest, D)], [first_weights])

    second_sent = moved(second_weights, y_sharing)
    a_up, a_down = moved(a_all, z_up), moved(a_all, z_down)
    b_x, b_y = moved(b_all, x_other), moved(b_all, y_same_half)
    middle = HELD + FIRST_ROWS
    held = ((0, 0, HELD), (1, 0, HELD))
    shared = ((None, HELD, FIRST_ROWS), (None, middle, rest))
    arrays = [up, down, first_weights, second_sent]
    results = hidden_step(
        ((0, 0, HELD, 0, 512, 0), (1, HELD, middle, 0, 512, 0)),
        held + shared[:1],
        arrays[:3],
        [a_all, b_all],
        (),
        (0, 512),
    )

    mid = 2 * half
    near, far = (every, pl.ds(0, mid)), (every, pl.ds(mid, mid))
    plan = ((0, near, 0, ()), (1, far, 1, ()), (2, near, 2, ()), (3, far, 3, ()))
    part = (2, mid, D)
    cut = copies(plan, [part] * 4, [a_up, a_down, b_x, b_y], [part] * 4, [second_sent, results[0]])
    last = [
        moved(cut[0], z_up),
        moved(cut[1], z_down),
        moved(cut[2], y_same_half),
        moved(cut[3], x_other),
    ]
    results = hidden_step(
        ((0, 0, HELD, 0, 1024, 512), (1, HELD, SHARED, 0, 1024, 512), (1, middle, SHARED, 1024, 512, 0)),
        held + shared,
        arrays,
        [a_up, a_down, b_x, b_y, a_all, b_all],
        results,
        (512, 1024),
        cut[:1],
    )
    results = hidden_step(
        ((1, HELD, SHARED, 0, 512, 1536), (0, 0, HELD, 0, 512, 1536)),
        held + shared,
        arrays,
        last,
        results,
        (1536, 512),
    )
    hidden, delta, hidden_shared, delta_shared, tokens = results

    count = step_index[0].astype(jnp.float32)
    bias_one = 1.0 - jnp.exp(count * math.log(beta_one))
    bias_two = 1.0 - jnp.exp(count * math.log(beta_two))
    bias = jnp.stack([1.0 / bias_one, 1.0 / bias_two])
    state = [up, momentum_up[0], variance_up[0], down, momentum_down[0], variance_down[0]]

    def finish(hop):
        route = [(g, (g + hop) % 4) for g in range(4)]
        news, updated, others = (), [], []
        for c in range(len(CHUNKS)):
            after = updated[c - 2 : c - 1] if c >= 2 else []
            theirs = theirs_chunk(c, hidden_shared, delta_shared, tokens, after)
            arrived = moved(theirs, y_sharing)
            mixed = [updated[c - 2], others[c - 2]] if c >= 2 else []
            out = adam_chunk(c, hidden, delta, tokens, bias, arrived, state, mixed, news)
            updated.append(out[0])
            news = out[1:]
            others.append(lax.ppermute(out[0], "rep", route))
        mixed = news[4:]
        for c in range(len(CHUNKS) - 2, len(CHUNKS)):
            mixed = mix_chunk(c, updated[c], others[c], mixed)
        return mixed[0], mixed[1], news[0], news[2], news[1], news[3]

    outs = lax.cond(step_index[0] % 2 == 0, lambda: finish(1), lambda: finish(2))
    return tuple(o[None] for o in outs)


def solution(mesh):
    shard = P("rep", "fsdp", None)
    return jax.shard_map(
        on_device,
        mesh=mesh,
        in_specs=(shard,) * 8 + (P(),),
        out_specs=(shard,) * 6,
        check_vma=False,
    )
```

```python
import functools
import math

import jax
import jax.numpy as jnp
from jax import lax
from jax.experimental import pallas as pl
from jax.experimental.pallas import tpu as pltpu
from jax.sharding import PartitionSpec as P

D = 1792
FF = 14336

beta_one = 0.9
beta_two = 0.95
learn_rate = 0.05
adam_eps = 1e-08
norm_eps = 1e-06
root_coef = math.sqrt(2.0 / math.pi)
up_scale = 1.0 / math.sqrt(D)
down_scale = 1.0 / math.sqrt(FF)

ROWS = 128
HELD = 448
SHARED = 2 * HELD
FIRST_ROWS = 160
TOKENS = 2048
CHUNKS = ((0, 128),) + tuple((256 * k, 256) for k in range(1, 6))
CHUNKS += ((1536, 128), (1664, 128), (128, 128))
MIXING = 7
EARLY = 1536
NZ, NX, NY = 4, 2, 4


def moved(block, place):
    route = []
    for z in range(NZ):
        for x in range(NX):
            for y in range(NY):
                a, b, c = place(z, x, y)
                route.append(((z * NX + x) * NY + y, (a % NZ * NX + b) * NY + c))
    return lax.ppermute(block, "fsdp", route)


def z_up(z, x, y):
    return z + 1, x, y


def z_down(z, x, y):
    return z - 1, x, y


def z_over(z, x, y):
    return z + 2, x, y


def x_other(z, x, y):
    return z, 1 - x, y


def y_same_half(z, x, y):
    return z, x, 3 - y


def diagonal(z, x, y):
    return z, 1 - x, 3 - y


def y_sharing(z, x, y):
    return z, x, y ^ 1


def gelu_pair(pre):
    square = pre * pre
    tangent = jnp.tanh(pre * (root_coef + (root_coef * 0.044715) * square))
    half = 0.5 * tangent + 0.5
    value = pre * half
    slope = half + pre * (0.5 - 0.5 * tangent * tangent) * (
        root_coef + (3.0 * 0.044715 * root_coef) * square
    )
    return (value, slope)


def normalize(rows):
    wide = rows.astype(jnp.float32)
    factor = lax.rsqrt(jnp.mean(wide * wide, axis=-1, keepdims=True) + norm_eps)
    return (wide * factor).astype(jnp.bfloat16)


def prepare_kernel(inputs, cotangent, up, down, a_ref, b_ref, weights, sem):
    half = ROWS // 2
    loads = [
        pltpu.make_async_copy(ref.at[pl.ds(0, FIRST_ROWS)], weights.at[k], sem.at[k])
        for k, ref in enumerate((up, down))
    ]
    for load in loads:
        load.start()
    for k, ref in enumerate((a_ref, b_ref)):
        rows = slice(k * half, (k + 1) * half)
        ref[0] = normalize(inputs[rows])
        ref[1] = cotangent[rows]
    for load in loads:
        load.wait()


def prepare(inputs, cotangent, up, down):
    inside = pl.BlockSpec(memory_space=pltpu.VMEM)
    half = jax.ShapeDtypeStruct((2, ROWS // 2, D), jnp.bfloat16)
    return pl.pallas_call(
        prepare_kernel,
        out_shape=[half, half, jax.ShapeDtypeStruct((2, FIRST_ROWS, D), jnp.bfloat16)],
        in_specs=[inside, inside, ANY, ANY],
        out_specs=[inside] * 3,
        scratch_shapes=[pltpu.SemaphoreType.DMA((2,))],
        compiler_params=vmem(16),
        cost_estimate=cost(0, 8 * (ROWS + FIRST_ROWS) * D),
    )(inputs, cotangent, up, down)


contract_last = (((1,), (1,)), ((), ()))
ANY = pl.BlockSpec(memory_space=pl.ANY)


def vmem(mebibytes):
    return pltpu.CompilerParams(vmem_limit_bytes=mebibytes * 1024 * 1024)


def cost(flops, moved_bytes):
    return pl.CostEstimate(flops=2 * flops, bytes_accessed=moved_bytes, transcendentals=0)


def copies_kernel(plan, count_in, count_out, *refs):
    ins, outs = refs[:count_in], refs[count_in : count_in + count_out]
    held = refs[count_in + count_out : -2]
    load_sem, store_sem = refs[-2:]
    loads, stores = [], []
    for k, (i, source, o, target) in enumerate(plan):
        loads.append(pltpu.make_async_copy(ins[i].at[source], held[k], load_sem.at[k]))
        stores.append(pltpu.make_async_copy(held[k], outs[o].at[target], store_sem.at[k]))
    for load in loads:
        load.start()
    for load, store in zip(loads, stores):
        load.wait()
        store.start()
    for store in stores:
        store.wait()


def copies(plan, parts, arrays, shapes, after=()):
    out = [jax.ShapeDtypeStruct(s, jnp.bfloat16) for s in shapes]
    arrays = list(arrays) + list(after)
    return pl.pallas_call(
        functools.partial(copies_kernel, plan, len(arrays), len(out)),
        out_shape=out,
        in_specs=[ANY] * len(arrays),
        out_specs=[ANY] * len(out),
        scratch_shapes=[pltpu.VMEM(shape, jnp.bfloat16) for shape in parts]
        + [pltpu.SemaphoreType.DMA((len(plan),))] * 2,
        compiler_params=vmem(16),
        cost_estimate=cost(0, 2 * sum(2 * math.prod(s) for s in shapes)),
    )(*arrays)


def hidden_kernel(jobs, sizes, pieces, skipped, kept, tile, *refs):
    arrays = refs[: len(pieces)]
    blocks = refs[len(pieces) : len(pieces) + len(sizes)]
    refs = refs[len(pieces) + len(sizes) + skipped :]
    weights, tokens, hidden, delta, weight_sem, token_sem, out_sem, keep_sem = refs[-8:]
    loads = []
    for k, (ref, (which, first, rows)) in enumerate(zip(arrays, pieces)):
        target = weights.at[:, pl.ds(first, rows)]
        if which is not None:
            target = weights.at[which, pl.ds(first, rows)]
        loads.append(pltpu.make_async_copy(ref, target, weight_sem.at[k]))
    first = 0
    for k, (ref, count) in enumerate(zip(blocks, sizes)):
        loads.append(pltpu.make_async_copy(ref, tokens.at[:, pl.ds(first, count)], token_sem.at[k]))
        first += count
    for load in loads:
        load.start()
    for load in loads:
        load.wait()
    stores = []
    if kept is not None:
        source = tokens.at[:, pl.ds(0, kept[1])]
        target = refs[4].at[:, pl.ds(kept[0], kept[1])]
        stores.append(pltpu.make_async_copy(source, target, keep_sem.at[0]))
        stores[-1].start()
    for k, (shared, row, end, token, count, place) in enumerate(jobs):

        def step(i, carry, row=row, end=end, token=token):
            at = pl.ds(pl.multiple_of(token + i * tile, tile), tile)
            pre = up_scale * lax.dot_general(
                weights[0, row:end], tokens[0, at], contract_last, preferred_element_type=jnp.float32
            )
            back = down_scale * lax.dot_general(
                weights[1, row:end], tokens[1, at], contract_last, preferred_element_type=jnp.float32
            )
            value, slope = gelu_pair(pre)
            hidden[row:end, at] = value.astype(jnp.bfloat16)
            delta[row:end, at] = (back * slope).astype(jnp.bfloat16)
            return carry

        lax.fori_loop(0, count // tile, step, 0)
        base = HELD if shared and end > HELD else 0
        for j, source in enumerate((hidden, delta)):
            store = pltpu.make_async_copy(
                source.at[pl.ds(row, end - row), pl.ds(token, count)],
                refs[2 * shared + j].at[pl.ds(row - base, end - row), pl.ds(place, count)],
                out_sem.at[2 * k + j],
            )
            store.start()
            stores.append(store)
    for store in stores:
        store.wait()


def hidden_step(jobs, pieces, arrays, blocks, results, kept=None, after=()):
    sizes = tuple(b.shape[1] for b in blocks)
    total = sum(sizes)
    top = max(first + rows for _, first, rows in pieces)
    early = jax.ShapeDtypeStruct((HELD, EARLY), jnp.bfloat16)
    half = jax.ShapeDtypeStruct((HELD, TOKENS), jnp.bfloat16)
    out = [early] * 2 + [half] * 2 + [jax.ShapeDtypeStruct((2, TOKENS, D), jnp.bfloat16)]
    operands = [*arrays, *blocks]
    aliases = {len(operands) + k: k for k in range(len(results))}
    operands += [*results, *after]
    flops = sum(4 * (end - row) * count * D for _, row, end, _, count, _ in jobs)
    skipped = len(results) + len(after)
    return pl.pallas_call(
        functools.partial(hidden_kernel, jobs, sizes, pieces, skipped, kept, 256),
        out_shape=out,
        in_specs=[ANY] * len(operands),
        out_specs=[ANY] * 5,
        input_output_aliases=aliases,
        scratch_shapes=[
            pltpu.VMEM((2, top, D), jnp.bfloat16),
            pltpu.VMEM((2, total, D), jnp.bfloat16),
            pltpu.VMEM((top, total), jnp.bfloat16),
            pltpu.VMEM((top, total), jnp.bfloat16),
            pltpu.SemaphoreType.DMA((len(pieces),)),
            pltpu.SemaphoreType.DMA((len(blocks),)),
            pltpu.SemaphoreType.DMA((2 * len(jobs),)),
            pltpu.SemaphoreType.DMA((1,)),
        ],
        compiler_params=vmem(40),
        cost_estimate=cost(flops, 4 * (total + top) * D + 4 * top * total),
    )(*operands)


def last_own_kernel(up, down, *refs):
    blocks, (hidden, delta) = refs[:4], refs[-2:]
    first = 0
    for block in blocks:
        at = pl.ds(first, block.shape[1])
        pre = up_scale * lax.dot_general(
            up[...], block[0], contract_last, preferred_element_type=jnp.float32
        )
        back = down_scale * lax.dot_general(
            down[...], block[1], contract_last, preferred_element_type=jnp.float32
        )
        value, slope = gelu_pair(pre)
        hidden[:, at] = value.astype(jnp.bfloat16)
        delta[:, at] = (back * slope).astype(jnp.bfloat16)
        first += block.shape[1]


def last_own(up, down, blocks, after):
    inside = pl.BlockSpec(memory_space=pltpu.VMEM)
    out = jax.ShapeDtypeStruct((HELD, TOKENS - EARLY), jnp.bfloat16)
    return pl.pallas_call(
        last_own_kernel,
        out_shape=[out, out],
        in_specs=[inside] * 6 + [ANY] * len(after),
        out_specs=[inside] * 2,
        compiler_params=vmem(28),
        cost_estimate=cost(4 * HELD * (TOKENS - EARLY) * D, 4 * (HELD + TOKENS - EARLY) * D),
    )(up, down, *blocks, *after)


def column_spec(c):
    first, width = CHUNKS[c]
    return pl.BlockSpec((HELD, width), lambda j: (0, first // width))


def token_spec(c):
    first, width = CHUNKS[c]
    return pl.BlockSpec((2, TOKENS, width), lambda j: (0, 0, first // width))


def pair_spec(c):
    return pl.BlockSpec((2, HELD, CHUNKS[c][1]), lambda j: (0, 0, 0))


all_rows = pl.BlockSpec((HELD, TOKENS), lambda j: (0, 0))


def theirs_kernel(hidden, delta, tokens, *refs):
    up_grad = jnp.dot(delta[...], tokens[0], preferred_element_type=jnp.float32)
    down_grad = jnp.dot(hidden[...], tokens[1], preferred_element_type=jnp.float32)
    refs[-1][0] = (up_scale * up_grad).astype(jnp.bfloat16)
    refs[-1][1] = (down_scale * down_grad).astype(jnp.bfloat16)


def theirs_chunk(c, hidden, delta, tokens, after):
    width = CHUNKS[c][1]
    return pl.pallas_call(
        theirs_kernel,
        out_shape=jax.ShapeDtypeStruct((2, HELD, width), jnp.bfloat16),
        grid=(1,),
        in_specs=[all_rows, all_rows, token_spec(c)] + [ANY] * len(after),
        out_specs=pair_spec(c),
        compiler_params=vmem(28),
        cost_estimate=cost(4 * HELD * TOKENS * width, 4 * TOKENS * (HELD + width)),
    )(hidden, delta, tokens, *after)


def adam_kernel(mixing, *refs):
    hidden, delta, hidden_last, delta_last, tokens, bias, arrived = refs[:7]
    state = refs[7:13]
    outs = refs[-7:]
    sides = ((delta, delta_last, up_scale), (hidden, hidden_last, down_scale))
    for which, (side, last, scale) in enumerate(sides):
        weight, first, second = state[3 * which : 3 * which + 3]
        early = jnp.dot(side[...], tokens[which, :EARLY], preferred_element_type=jnp.float32)
        late = jnp.dot(last[...], tokens[which, EARLY:], preferred_element_type=jnp.float32)
        grad = scale * (early + late) + arrived[which].astype(jnp.float32)
        first_new = beta_one * first[...].astype(jnp.float32) + (1.0 - beta_one) * grad
        second_new = beta_two * second[...].astype(jnp.float32) + (1.0 - beta_two) * grad * grad
        update = (learn_rate * bias[0]) * first_new / (jnp.sqrt(second_new * bias[1]) + adam_eps)
        outs[0][which] = (weight[...].astype(jnp.float32) - update).astype(jnp.bfloat16)
        outs[1 + 2 * which][...] = first_new.astype(jnp.bfloat16)
        outs[2 + 2 * which][...] = second_new.astype(jnp.bfloat16)
    if mixing:
        mix_kernel(refs[13], refs[14], *outs[-2:])


def mix_kernel(own, other, *refs):
    for which in (0, 1):
        both = own[which].astype(jnp.float32) + other[which].astype(jnp.float32)
        refs[which - 2][...] = (both * 0.5).astype(jnp.bfloat16)


whole = jax.ShapeDtypeStruct((HELD, D), jnp.bfloat16)


def adam_chunk(c, sides, tokens, bias, arrived, state, mixed, results):
    width = CHUNKS[c][1]
    operands = [*sides, tokens, bias, arrived, *state, *mixed]
    aliases = {len(operands) + k: 1 + k for k in range(len(results))}
    before = max(c - 2, 0)
    mixing = [column_spec(before)] * 2 if mixed or not results else []
    early = pl.BlockSpec((HELD, EARLY), lambda j: (0, 0))
    last = pl.BlockSpec((HELD, TOKENS - EARLY), lambda j: (0, 0))
    smem = pl.BlockSpec(memory_space=pltpu.SMEM)
    return pl.pallas_call(
        functools.partial(adam_kernel, bool(mixed)),
        out_shape=[jax.ShapeDtypeStruct((2, HELD, width), jnp.bfloat16)] + [whole] * 6,
        grid=(1,),
        in_specs=[early, early, last, last, token_spec(c), smem, pair_spec(c)]
        + [column_spec(c)] * 6
        + [pair_spec(before)] * len(mixed)
        + [ANY] * len(results),
        out_specs=[pair_spec(c)] + [column_spec(c)] * 4 + (mixing or [ANY] * 2),
        input_output_aliases=aliases,
        compiler_params=vmem(28),
        cost_estimate=cost(4 * HELD * TOKENS * width, 4 * TOKENS * (HELD + width) + 36 * HELD * width),
    )(*operands, *results)


def mix_chunk(c, own, other, results):
    return pl.pallas_call(
        mix_kernel,
        out_shape=[whole] * 2,
        grid=(1,),
        in_specs=[pair_spec(c)] * 2 + [ANY] * 2,
        out_specs=[column_spec(c)] * 2,
        input_output_aliases={2: 0, 3: 1},
        compiler_params=vmem(28),
        cost_estimate=cost(0, 12 * HELD * CHUNKS[c][1]),
    )(own, other, *results)


def on_device(
    inputs,
    cotangent,
    up_weight,
    down_weight,
    momentum_up,
    momentum_down,
    variance_up,
    variance_down,
    step_index,
):
    up, down = up_weight[0], down_weight[0]
    half = ROWS // 2
    every = slice(None)

    a, b, weights = prepare(inputs[0], cotangent[0], up, down)
    first_weights = moved(weights, y_sharing)
    a_x, a_y = moved(a, x_other), moved(a, y_same_half)
    b_up, b_down = moved(b, z_up), moved(b, z_down)
    pieces = [a, a_x, a_y, moved(a_x, y_same_half), b, b_up, b_down, moved(b_up, z_up)]
    rest = HELD - FIRST_ROWS
    plan = tuple((k, every, k // 4, (every, pl.ds(k % 4 * half, half))) for k in range(8))
    plan += tuple((8 + k, pl.ds(FIRST_ROWS, rest), 2, k) for k in (0, 1))
    a_all, b_all, second_weights = copies(
        plan,
        [(2, half, D)] * 8 + [(rest, D)] * 2,
        pieces + [up, down],
        [(2, 4 * half, D)] * 2 + [(2, rest, D)],
        [first_weights],
    )

    second_sent = moved(second_weights, y_sharing)
    a_up, a_down = moved(a_all, z_up), moved(a_all, z_down)
    b_x, b_y = moved(b_all, x_other), moved(b_all, y_same_half)
    middle = HELD + FIRST_ROWS
    held = ((0, 0, HELD), (1, 0, HELD))
    shared = ((None, HELD, FIRST_ROWS), (None, middle, rest))
    arrays = [up, down, first_weights, second_sent]
    results = hidden_step(
        ((0, 0, HELD, 0, 512, 0), (1, HELD, middle, 0, 512, 0)),
        held + shared[:1],
        arrays[:3],
        [a_all, b_all],
        (),
        (0, 512),
    )

    mid = 2 * half
    near, far = (every, pl.ds(0, mid)), (every, pl.ds(mid, mid))
    plan = ((0, near, 0, ()), (1, far, 1, ()), (2, near, 2, ()), (3, far, 3, ()))
    part = (2, mid, D)
    cut = copies(plan, [part] * 4, [a_up, a_down, b_x, b_y], [part] * 4, [second_sent, results[0]])
    last = [
        moved(cut[0], z_up),
        moved(cut[1], z_down),
        moved(cut[2], y_same_half),
        moved(cut[3], x_other),
    ]
    results = hidden_step(
        ((0, 0, HELD, 0, 1024, 512), (1, HELD, SHARED, 0, 1024, 512), (1, middle, SHARED, 1024, 512, 0)),
        held + shared,
        arrays,
        [a_up, a_down, b_x, b_y, a_all, b_all],
        results,
        (512, 1024),
        cut[:1],
    )
    shared = ((None, 0, FIRST_ROWS), (None, FIRST_ROWS, rest))
    job = (1, 0, HELD, 0, 512, EARLY)
    results = hidden_step((job,), shared, arrays[2:], last, results, (EARLY, 512))
    hidden, delta, hidden_shared, delta_shared, tokens = results

    count = step_index[0].astype(jnp.float32)
    bias_one = 1.0 - jnp.exp(count * math.log(beta_one))
    bias_two = 1.0 - jnp.exp(count * math.log(beta_two))
    bias = jnp.stack([1.0 / bias_one, 1.0 / bias_two])
    state = [up, momentum_up[0], variance_up[0], down, momentum_down[0], variance_down[0]]

    def finish(hop):
        route = [(g, (g + hop) % 4) for g in range(4)]
        news, updated, others, sent = (), [], [], []
        for c in range(2):
            theirs = theirs_chunk(c, hidden_shared, delta_shared, tokens, [])
            sent.append(moved(theirs, y_sharing))
        sides = [hidden, delta, *last_own(up, down, last, [theirs])]
        for c in range(len(CHUNKS)):
            mixed = [updated[c - 2], others[c - 2]] if 2 <= c < MIXING else []
            out = adam_chunk(c, sides, tokens, bias, sent[c], state, mixed, news)
            updated.append(out[0])
            news = out[1:]
            others.append(lax.ppermute(out[0], "rep", route))
            if c + 2 < len(CHUNKS):
                theirs = theirs_chunk(c + 2, hidden_shared, delta_shared, tokens, [out[0]])
                sent.append(moved(theirs, y_sharing))
        mixed = news[4:]
        for c in range(MIXING - 2, len(CHUNKS)):
            mixed = mix_chunk(c, updated[c], others[c], mixed)
        return mixed[0], mixed[1], news[0], news[2], news[1], news[3]

    outs = lax.cond(step_index[0] % 2 == 0, lambda: finish(1), lambda: finish(2))
    return tuple(o[None] for o in outs)


def solution(mesh):
    shard = P("rep", "fsdp", None)
    return jax.shard_map(
        on_device,
        mesh=mesh,
        in_specs=(shard,) * 8 + (P(),),
        out_specs=(shard,) * 6,
        check_vma=False,
    )
```

```python
import functools
import math

import jax
import jax.numpy as jnp
from jax import lax
from jax.experimental import pallas as pl
from jax.experimental.pallas import tpu as pltpu
from jax.sharding import PartitionSpec as P

D = 1792
FF = 14336

beta_one = 0.9
beta_two = 0.95
learn_rate = 0.05
adam_eps = 1e-08
norm_eps = 1e-06
root_coef = math.sqrt(2.0 / math.pi)
up_scale = 1.0 / math.sqrt(D)
down_scale = 1.0 / math.sqrt(FF)

ROWS = 128
HELD = 448
SHARED = 2 * HELD
TOKENS = 2048
CHUNKS = ((0, 128),) + tuple((256 * k, 256) for k in range(1, 7)) + ((128, 128),)
MIXING = 7
EARLY = 1536
NZ, NX, NY = 4, 2, 4


def moved(block, place):
    route = []
    for z in range(NZ):
        for x in range(NX):
            for y in range(NY):
                a, b, c = place(z, x, y)
                route.append(((z * NX + x) * NY + y, (a % NZ * NX + b) * NY + c))
    return lax.ppermute(block, "fsdp", route)


def z_up(z, x, y):
    return z + 1, x, y


def z_down(z, x, y):
    return z - 1, x, y


def z_over(z, x, y):
    return z + 2, x, y


def x_other(z, x, y):
    return z, 1 - x, y


def y_same_half(z, x, y):
    return z, x, 3 - y


def diagonal(z, x, y):
    return z, 1 - x, 3 - y


def y_sharing(z, x, y):
    return z, x, y ^ 1


def gelu_pair(pre):
    square = pre * pre
    tangent = jnp.tanh(pre * (root_coef + (root_coef * 0.044715) * square))
    half = 0.5 * tangent + 0.5
    value = pre * half
    slope = half + pre * (0.5 - 0.5 * tangent * tangent) * (
        root_coef + (3.0 * 0.044715 * root_coef) * square
    )
    return (value, slope)


def normalize(rows):
    wide = rows.astype(jnp.float32)
    factor = lax.rsqrt(jnp.mean(wide * wide, axis=-1, keepdims=True) + norm_eps)
    return (wide * factor).astype(jnp.bfloat16)


contract_last = (((1,), (1,)), ((), ()))
ANY = pl.BlockSpec(memory_space=pl.ANY)
INSIDE = pl.BlockSpec(memory_space=pltpu.VMEM)


def vmem(mebibytes):
    return pltpu.CompilerParams(vmem_limit_bytes=mebibytes * 1024 * 1024)


def cost(flops, moved_bytes):
    return pl.CostEstimate(flops=2 * flops, bytes_accessed=moved_bytes, transcendentals=0)


def prepare_kernel(inputs, cotangent, a_ref, b_ref, held, sem):
    half = ROWS // 2
    loads = [
        pltpu.make_async_copy(inputs, held, sem.at[0]),
        pltpu.make_async_copy(cotangent.at[pl.ds(0, half)], a_ref.at[1], sem.at[1]),
        pltpu.make_async_copy(cotangent.at[pl.ds(half, half)], b_ref.at[1], sem.at[2]),
    ]
    for load in loads:
        load.start()
    loads[0].wait()
    a_ref[0] = normalize(held[:half])
    b_ref[0] = normalize(held[half:])
    for load in loads[1:]:
        load.wait()


def prepare(inputs, cotangent):
    half = jax.ShapeDtypeStruct((2, ROWS // 2, D), jnp.bfloat16)
    return pl.pallas_call(
        prepare_kernel,
        out_shape=[half, half],
        in_specs=[ANY] * 2,
        out_specs=[INSIDE] * 2,
        scratch_shapes=[pltpu.VMEM((ROWS, D), jnp.bfloat16), pltpu.SemaphoreType.DMA((3,))],
        compiler_params=vmem(16),
        cost_estimate=cost(0, 8 * ROWS * D),
    )(inputs, cotangent)


def stack_kernel(up, down, out, held, load_sem, store_sem):
    parts = 2
    rows = HELD // parts
    loads, stores = [], []
    for which, ref in enumerate((up, down)):
        for part in range(parts):
            k, at = which * parts + part, pl.ds(part * rows, rows)
            place = held.at[which, at]
            loads.append(pltpu.make_async_copy(ref.at[at], place, load_sem.at[k]))
            stores.append(pltpu.make_async_copy(place, out.at[which, at], store_sem.at[k]))
    for load in loads:
        load.start()
    for load, store in zip(loads, stores):
        load.wait()
        store.start()
    for store in stores:
        store.wait()


def stack_weights(up, down):
    shape = (2, HELD, D)
    return pl.pallas_call(
        stack_kernel,
        out_shape=jax.ShapeDtypeStruct(shape, jnp.bfloat16),
        in_specs=[ANY] * 2,
        out_specs=ANY,
        scratch_shapes=[pltpu.VMEM(shape, jnp.bfloat16)] + [pltpu.SemaphoreType.DMA((4,))] * 2,
        compiler_params=vmem(16),
        cost_estimate=cost(0, 8 * HELD * D),
    )(up, down)


def join_kernel(count, *refs):
    first = 0
    for ref in refs[:count]:
        rows = ref.shape[1]
        refs[-1][:, first : first + rows] = ref[...]
        first += rows


def join(pieces, after):
    rows = sum(p.shape[1] for p in pieces)
    return pl.pallas_call(
        functools.partial(join_kernel, len(pieces)),
        out_shape=jax.ShapeDtypeStruct((2, rows, D), jnp.bfloat16),
        in_specs=[INSIDE] * len(pieces) + [ANY] * len(after),
        out_specs=INSIDE,
        compiler_params=vmem(16),
        cost_estimate=cost(0, 8 * rows * D),
    )(*pieces, *after)


def cut_kernel(firsts, count_in, *refs):
    sem = refs[-1]
    loads = []
    for k, first in enumerate(firsts):
        out = refs[count_in + k]
        source = refs[k].at[:, pl.ds(first, out.shape[1])]
        loads.append(pltpu.make_async_copy(source, out, sem.at[k]))
        loads[-1].start()
    for load in loads:
        load.wait()


def cut(blocks, firsts, rows, after):
    out = jax.ShapeDtypeStruct((2, rows, D), jnp.bfloat16)
    operands = list(blocks) + list(after)
    return pl.pallas_call(
        functools.partial(cut_kernel, firsts, len(operands)),
        out_shape=[out] * len(blocks),
        in_specs=[ANY] * len(operands),
        out_specs=[INSIDE] * len(blocks),
        scratch_shapes=[pltpu.SemaphoreType.DMA((len(blocks),))],
        compiler_params=vmem(16),
        cost_estimate=cost(0, 8 * rows * D * len(blocks)),
    )(*operands)


def hidden_kernel(jobs, sizes, pieces, skipped, kept, tile, both, *refs):
    arrays = refs[: len(pieces)]
    blocks = refs[len(pieces) : len(pieces) + len(sizes)]
    refs = refs[len(pieces) + len(sizes) + skipped :]
    weights, tokens, pair, weight_sem, token_sem, out_sem, keep_sem = refs[-7:]
    top, total = weights.shape[1], tokens.shape[1]
    loads = []
    for k, (ref, (which, first, rows)) in enumerate(zip(arrays, pieces)):
        target = weights.at[:, pl.ds(first, rows)]
        if which is not None:
            target = weights.at[which, pl.ds(first, rows)]
        loads.append(pltpu.make_async_copy(ref, target, weight_sem.at[k]))
    first = 0
    for k, (ref, count) in enumerate(zip(blocks, sizes)):
        loads.append(pltpu.make_async_copy(ref, tokens.at[:, pl.ds(first, count)], token_sem.at[k]))
        first += count
    for load in loads:
        load.start()
    for load in loads:
        load.wait()
    stores = []
    if kept is not None:
        source = tokens.at[:, pl.ds(0, kept[1])]
        target = refs[2].at[:, pl.ds(kept[0], kept[1])]
        stores.append(pltpu.make_async_copy(source, target, keep_sem.at[0]))
        stores[-1].start()

    def step(i, carry):
        blocks = top // HELD
        here = i < blocks * both
        row = jnp.where(here, i % blocks, blocks - 1) * HELD
        token = jnp.where(here, i // blocks, i - (blocks - 1) * both) * tile
        rows = pl.ds(pl.multiple_of(row, HELD), HELD)
        at = pl.ds(pl.multiple_of(token, tile), tile)
        pre = up_scale * lax.dot_general(
            weights[0, rows], tokens[0, at], contract_last, preferred_element_type=jnp.float32
        )
        back = down_scale * lax.dot_general(
            weights[1, rows], tokens[1, at], contract_last, preferred_element_type=jnp.float32
        )
        value, slope = gelu_pair(pre)
        pair[0, rows, at] = (back * slope).astype(jnp.bfloat16)
        pair[1, rows, at] = value.astype(jnp.bfloat16)
        return carry

    lax.fori_loop(0, top // HELD * both + (total // tile - both), step, 0)
    for k, (shared, token, count, place) in enumerate(jobs):
        stores.append(
            pltpu.make_async_copy(
                pair.at[:, pl.ds(shared * HELD, HELD), pl.ds(token, count)],
                refs[shared].at[:, :, pl.ds(place, count)],
                out_sem.at[k],
            )
        )
        stores[-1].start()
    for store in stores:
        store.wait()


def hidden_step(jobs, pieces, arrays, blocks, results, kept, both, after=()):
    sizes = tuple(b.shape[1] for b in blocks)
    total = sum(sizes)
    top = max(first + rows for _, first, rows in pieces)
    shapes = ((2, HELD, EARLY), (2, HELD, TOKENS), (2, TOKENS, D))
    out = [jax.ShapeDtypeStruct(shape, jnp.bfloat16) for shape in shapes]
    operands = [*arrays, *blocks]
    aliases = {len(operands) + k: k for k in range(len(results))}
    operands += [*results, *after]
    flops = sum(4 * HELD * count * D for _, _, count, _ in jobs)
    skipped = len(results) + len(after)
    return pl.pallas_call(
        functools.partial(hidden_kernel, jobs, sizes, pieces, skipped, kept, 512, both),
        out_shape=out,
        in_specs=[ANY] * len(operands),
        out_specs=[ANY] * 3,
        input_output_aliases=aliases,
        scratch_shapes=[
            pltpu.VMEM((2, top, D), jnp.bfloat16),
            pltpu.VMEM((2, total, D), jnp.bfloat16),
            pltpu.VMEM((2, top, total), jnp.bfloat16),
            pltpu.SemaphoreType.DMA((len(pieces),)),
            pltpu.SemaphoreType.DMA((len(blocks),)),
            pltpu.SemaphoreType.DMA((len(jobs),)),
            pltpu.SemaphoreType.DMA((1,)),
        ],
        compiler_params=vmem(36 if len(jobs) > 1 else 24),
        cost_estimate=cost(flops, 4 * (total + top) * D + 4 * top * total),
    )(*operands)


def last_own_kernel(up, down, tokens_in, *refs):
    pair, weights, tokens, sem = refs[-4:]
    loads = [
        pltpu.make_async_copy(up, weights.at[0], sem.at[0]),
        pltpu.make_async_copy(down, weights.at[1], sem.at[1]),
        pltpu.make_async_copy(tokens_in.at[:, pl.ds(EARLY, TOKENS - EARLY)], tokens, sem.at[2]),
    ]
    for load in loads:
        load.start()
    for load in loads:
        load.wait()
    tile = 256

    def step(i, carry):
        at = pl.ds(pl.multiple_of(i * tile, tile), tile)
        pre = up_scale * lax.dot_general(
            weights[0], tokens[0, at], contract_last, preferred_element_type=jnp.float32
        )
        back = down_scale * lax.dot_general(
            weights[1], tokens[1, at], contract_last, preferred_element_type=jnp.float32
        )
        value, slope = gelu_pair(pre)
        pair[0, :, at] = (back * slope).astype(jnp.bfloat16)
        pair[1, :, at] = value.astype(jnp.bfloat16)
        return carry

    lax.fori_loop(0, (TOKENS - EARLY) // tile, step, 0)


def last_own(up, down, tokens, after):
    out = jax.ShapeDtypeStruct((2, HELD, TOKENS - EARLY), jnp.bfloat16)
    return pl.pallas_call(
        last_own_kernel,
        out_shape=out,
        in_specs=[ANY] * (3 + len(after)),
        out_specs=INSIDE,
        scratch_shapes=[
            pltpu.VMEM((2, HELD, D), jnp.bfloat16),
            pltpu.VMEM((2, TOKENS - EARLY, D), jnp.bfloat16),
            pltpu.SemaphoreType.DMA((3,)),
        ],
        compiler_params=vmem(22),
        cost_estimate=cost(4 * HELD * (TOKENS - EARLY) * D, 4 * (HELD + TOKENS - EARLY) * D),
    )(up, down, tokens, *after)


def last_shared_kernel(*refs):
    weights_in, blocks = refs[0], refs[1:5]
    pair_in, tokens_in, pair_out, tokens_out, chunk = refs[5:10]
    weights, tokens, pair, columns, sem, out_sem = refs[10:]
    first, width = CHUNKS[0]
    rest = TOKENS - EARLY
    loads = [pltpu.make_async_copy(weights_in, weights, sem.at[0])]
    row = 0
    for k, ref in enumerate(blocks):
        rows = ref.shape[1]
        loads.append(pltpu.make_async_copy(ref, tokens.at[:, pl.ds(row, rows)], sem.at[1 + k]))
        row += rows
    early, late = pl.ds(0, EARLY), pl.ds(EARLY, rest)
    source = tokens_in.at[:, early, pl.ds(first, width)]
    more = [
        pltpu.make_async_copy(pair_in.at[:, :, early], pair.at[:, :, early], sem.at[5]),
        pltpu.make_async_copy(source, columns, sem.at[6]),
    ]
    for load in loads + more:
        load.start()
    for load in loads:
        load.wait()
    stores = [pltpu.make_async_copy(tokens, tokens_out.at[:, late], out_sem.at[0])]
    stores[0].start()
    tile = 256

    def step(i, carry):
        at = pl.ds(pl.multiple_of(i * tile, tile), tile)
        to = pl.ds(pl.multiple_of(EARLY + i * tile, tile), tile)
        pre = up_scale * lax.dot_general(
            weights[0], tokens[0, at], contract_last, preferred_element_type=jnp.float32
        )
        back = down_scale * lax.dot_general(
            weights[1], tokens[1, at], contract_last, preferred_element_type=jnp.float32
        )
        value, slope = gelu_pair(pre)
        pair[0, :, to] = (back * slope).astype(jnp.bfloat16)
        pair[1, :, to] = value.astype(jnp.bfloat16)
        return carry

    lax.fori_loop(0, rest // tile, step, 0)
    stores.append(pltpu.make_async_copy(pair.at[:, :, late], pair_out.at[:, :, late], out_sem.at[1]))
    stores[1].start()
    for load in more:
        load.wait()
    for which, scale in enumerate((up_scale, down_scale)):
        grad = jnp.dot(pair[which, :, :EARLY], columns[which], preferred_element_type=jnp.float32)
        grad += jnp.dot(
            pair[which, :, EARLY:],
            tokens[which, :, first : first + width],
            preferred_element_type=jnp.float32,
        )
        chunk[which] = (scale * grad).astype(jnp.bfloat16)
    for store in stores:
        store.wait()


def last_shared(weights, blocks, pair, tokens):
    width = CHUNKS[0][1]
    return pl.pallas_call(
        last_shared_kernel,
        out_shape=[
            jax.ShapeDtypeStruct((2, HELD, TOKENS), jnp.bfloat16),
            jax.ShapeDtypeStruct((2, TOKENS, D), jnp.bfloat16),
            jax.ShapeDtypeStruct((2, HELD, width), jnp.bfloat16),
        ],
        in_specs=[ANY] * 7,
        out_specs=[ANY] * 2 + [INSIDE],
        input_output_aliases={5: 0, 6: 1},
        scratch_shapes=[
            pltpu.VMEM((2, HELD, D), jnp.bfloat16),
            pltpu.VMEM((2, TOKENS - EARLY, D), jnp.bfloat16),
            pltpu.VMEM((2, HELD, TOKENS), jnp.bfloat16),
            pltpu.VMEM((2, EARLY, width), jnp.bfloat16),
            pltpu.SemaphoreType.DMA((7,)),
            pltpu.SemaphoreType.DMA((2,)),
        ],
        compiler_params=vmem(22),
        cost_estimate=cost(
            4 * HELD * ((TOKENS - EARLY) * D + TOKENS * width), 4 * (HELD + TOKENS - EARLY) * D
        ),
    )(weights, *blocks, pair, tokens)


def column_spec(c):
    first, width = CHUNKS[c]
    return pl.BlockSpec((HELD, width), lambda j: (0, first // width))


def token_spec(c):
    first, width = CHUNKS[c]
    return pl.BlockSpec((2, TOKENS, width), lambda j: (0, 0, first // width))


def pair_spec(c):
    return pl.BlockSpec((2, HELD, CHUNKS[c][1]), lambda j: (0, 0, 0))


def rows_spec(tokens):
    return pl.BlockSpec((2, HELD, tokens), lambda j: (0, 0, 0))


def theirs_kernel(pair, tokens, *refs):
    def step(which, carry):
        scale = jnp.where(which == 0, up_scale, down_scale)
        grad = jnp.dot(pair[which], tokens[which], preferred_element_type=jnp.float32)
        refs[-1][which] = (scale * grad).astype(jnp.bfloat16)
        return carry

    lax.fori_loop(0, 2, step, 0)


def theirs_chunk(c, pair, tokens, after):
    width = CHUNKS[c][1]
    return pl.pallas_call(
        theirs_kernel,
        out_shape=jax.ShapeDtypeStruct((2, HELD, width), jnp.bfloat16),
        grid=(1,),
        in_specs=[rows_spec(TOKENS), token_spec(c)] + [ANY] * len(after),
        out_specs=pair_spec(c),
        compiler_params=vmem(22),
        cost_estimate=cost(4 * HELD * TOKENS * width, 4 * TOKENS * (HELD + width)),
    )(pair, tokens, *after)


def adam_kernel(mixing, *refs):
    pair, pair_last, tokens, bias, arrived = refs[:5]
    state = refs[5:11]
    outs = refs[-8:-1]
    grads = refs[-1]

    def multiply(which, carry):
        scale = jnp.where(which == 0, up_scale, down_scale)
        early = jnp.dot(pair[which], tokens[which, :EARLY], preferred_element_type=jnp.float32)
        late = jnp.dot(pair_last[which], tokens[which, EARLY:], preferred_element_type=jnp.float32)
        grads[which] = scale * (early + late)
        return carry

    lax.fori_loop(0, 2, multiply, 0)
    tile = 32

    def step(i, carry):
        at = pl.ds(pl.multiple_of(i * tile, tile), tile)
        for which in (0, 1):
            weight, first, second = (ref[at] for ref in state[3 * which : 3 * which + 3])
            grad = grads[which, at] + arrived[which, at].astype(jnp.float32)
            first_new = beta_one * first.astype(jnp.float32) + (1.0 - beta_one) * grad
            second_new = beta_two * second.astype(jnp.float32) + (1.0 - beta_two) * grad * grad
            update = (learn_rate * bias[0]) * first_new / (jnp.sqrt(second_new * bias[1]) + adam_eps)
            outs[0][which, at] = (weight.astype(jnp.float32) - update).astype(jnp.bfloat16)
            outs[1 + 2 * which][at] = first_new.astype(jnp.bfloat16)
            outs[2 + 2 * which][at] = second_new.astype(jnp.bfloat16)
        return carry

    lax.fori_loop(0, HELD // tile, step, 0)
    if mixing:
        mix_kernel(refs[11], refs[12], *outs[-2:])


def mix_kernel(own, other, *refs):
    tile = 32

    def step(i, carry):
        at = pl.ds(pl.multiple_of(i * tile, tile), tile)
        for which in (0, 1):
            both = own[which, at].astype(jnp.float32) + other[which, at].astype(jnp.float32)
            refs[which - 2][at] = (both * 0.5).astype(jnp.bfloat16)
        return carry

    lax.fori_loop(0, HELD // tile, step, 0)


whole = jax.ShapeDtypeStruct((HELD, D), jnp.bfloat16)


def adam_chunk(c, sides, tokens, bias, arrived, state, mixed, results):
    width = CHUNKS[c][1]
    operands = [*sides, tokens, bias, arrived, *state, *mixed]
    aliases = {len(operands) + k: 1 + k for k in range(len(results))}
    before = max(c - 2, 0)
    mixing = [column_spec(before)] * 2 if mixed or not results else []
    early, last = rows_spec(EARLY), rows_spec(TOKENS - EARLY)
    smem = pl.BlockSpec(memory_space=pltpu.SMEM)
    return pl.pallas_call(
        functools.partial(adam_kernel, bool(mixed)),
        out_shape=[jax.ShapeDtypeStruct((2, HELD, width), jnp.bfloat16)] + [whole] * 6,
        grid=(1,),
        in_specs=[early, last, token_spec(c), smem, pair_spec(c)]
        + [column_spec(c)] * 6
        + [pair_spec(before)] * len(mixed)
        + [ANY] * len(results),
        out_specs=[pair_spec(c)] + [column_spec(c)] * 4 + (mixing or [ANY] * 2),
        input_output_aliases=aliases,
        scratch_shapes=[pltpu.VMEM((2, HELD, width), jnp.float32)],
        compiler_params=vmem(22),
        cost_estimate=cost(4 * HELD * TOKENS * width, 4 * TOKENS * (HELD + width) + 36 * HELD * width),
    )(*operands, *results)


def mix_chunk(c, own, other, results):
    return pl.pallas_call(
        mix_kernel,
        out_shape=[whole] * 2,
        grid=(1,),
        in_specs=[pair_spec(c)] * 2 + [ANY] * 2,
        out_specs=[column_spec(c)] * 2,
        input_output_aliases={2: 0, 3: 1},
        compiler_params=vmem(22),
        cost_estimate=cost(0, 12 * HELD * CHUNKS[c][1]),
    )(own, other, *results)


def on_device(
    inputs,
    cotangent,
    up_weight,
    down_weight,
    momentum_up,
    momentum_down,
    variance_up,
    variance_down,
    step_index,
):
    up, down = up_weight[0], down_weight[0]
    half = ROWS // 2

    weights_sent = moved(stack_weights(up, down), y_sharing)
    a, b = prepare(inputs[0], cotangent[0])
    a_x, a_y = moved(a, x_other), moved(a, y_same_half)
    b_up, b_down = moved(b, z_up), moved(b, z_down)
    quarter = half // 2
    a_far = [moved(a_x[:, :quarter], y_same_half), moved(a_y[:, quarter:], x_other)]
    b_far = [moved(b_up[:, :quarter], z_up), moved(b_down[:, quarter:], z_down)]
    a_all = join([a, a_x, a_y, *a_far], [])
    b_all = join([b, b_up, b_down, *b_far], [])

    a_up, a_down = moved(a_all, z_up), moved(a_all, z_down)
    b_x, b_y = moved(b_all, x_other), moved(b_all, y_same_half)
    held = ((0, 0, HELD), (1, 0, HELD))
    job = (0, 0, 512, 0)
    results = hidden_step((job,), held, [up, down], [a_all, b_all], (), (0, 512), 1)

    mid = 2 * half
    halves = cut([a_up, a_down, b_x, b_y], (0, mid, 0, mid), mid, [results[0]])
    last = [
        moved(halves[0], z_up),
        moved(halves[1], z_down),
        moved(halves[2], y_same_half),
        moved(halves[3], x_other),
    ]
    results = hidden_step(
        ((0, 0, 1024, 512), (1, 0, 1024, 512), (1, 1024, 512, 0)),
        held + ((None, HELD, HELD),),
        [up, down, weights_sent],
        [a_up, a_down, b_x, b_y, a_all, b_all],
        results,
        (512, 1024),
        2,
        halves[:1],
    )
    own_pair = results[0]
    pair, tokens, theirs = last_shared(weights_sent, last, *results[1:])

    count = step_index[0].astype(jnp.float32)
    bias_one = 1.0 - jnp.exp(count * math.log(beta_one))
    bias_two = 1.0 - jnp.exp(count * math.log(beta_two))
    bias = jnp.stack([1.0 / bias_one, 1.0 / bias_two])
    state = [up, momentum_up[0], variance_up[0], down, momentum_down[0], variance_down[0]]

    def finish(hop):
        route = [(g, (g + hop) % 4) for g in range(4)]
        news, updated, others = (), [], []
        second = theirs_chunk(1, pair, tokens, [])
        third = theirs_chunk(2, pair, tokens, [second])
        sent = [moved(t, y_sharing) for t in (theirs, second, third)]
        sides = [own_pair, last_own(up, down, tokens, [third])]
        for c in range(len(CHUNKS)):
            mixed = [updated[c - 2], others[c - 2]] if 2 <= c < MIXING else []
            out = adam_chunk(c, sides, tokens, bias, sent[c], state, mixed, news)
            updated.append(out[0])
            news = out[1:]
            others.append(lax.ppermute(out[0], "rep", route))
            if 3 <= c + 2 < len(CHUNKS):
                more = theirs_chunk(c + 2, pair, tokens, [out[0]])
                sent.append(moved(more, y_sharing))
        mixed = news[4:]
        for c in range(MIXING - 2, len(CHUNKS)):
            mixed = mix_chunk(c, updated[c], others[c], mixed)
        return mixed[0], mixed[1], news[0], news[2], news[1], news[3]

    outs = lax.cond(step_index[0] % 2 == 0, lambda: finish(1), lambda: finish(2))
    return tuple(o[None] for o in outs)


def solution(mesh):
    shard = P("rep", "fsdp", None)
    return jax.shard_map(
        on_device,
        mesh=mesh,
        in_specs=(shard,) * 8 + (P(),),
        out_specs=(shard,) * 6,
        check_vma=False,
    )
```

```python
import functools
import math

import jax
import jax.numpy as jnp
from jax import lax
from jax.experimental import pallas as pl
from jax.experimental.pallas import tpu as pltpu
from jax.sharding import PartitionSpec as P

D = 1792
FF = 14336

beta_one = 0.9
beta_two = 0.95
learn_rate = 0.05
adam_eps = 1e-08
norm_eps = 1e-06
root_coef = math.sqrt(2.0 / math.pi)
up_scale = 1.0 / math.sqrt(D)
down_scale = 1.0 / math.sqrt(FF)

ROWS = 128
HELD = 448
SHARED = 2 * HELD
TOKENS = 2048
WIDTH = 256
CHUNKS = D // WIDTH
FIRST_OWN = 2
OWN_LATER = ((1, 2, 2), (2, 4, 3))
MIXING = CHUNKS
EARLY = 1536
NZ, NX, NY = 4, 2, 4


def moved(block, place):
    route = []
    for z in range(NZ):
        for x in range(NX):
            for y in range(NY):
                a, b, c = place(z, x, y)
                route.append(((z * NX + x) * NY + y, (a % NZ * NX + b) * NY + c))
    return lax.ppermute(block, "fsdp", route)


def z_up(z, x, y):
    return z + 1, x, y


def z_down(z, x, y):
    return z - 1, x, y


def z_over(z, x, y):
    return z + 2, x, y


def x_other(z, x, y):
    return z, 1 - x, y


def y_same_half(z, x, y):
    return z, x, 3 - y


def diagonal(z, x, y):
    return z, 1 - x, 3 - y


def y_sharing(z, x, y):
    return z, x, y ^ 1


def gelu_pair(pre):
    square = pre * pre
    tangent = jnp.tanh(pre * (root_coef + (root_coef * 0.044715) * square))
    half = 0.5 * tangent + 0.5
    value = pre * half
    slope = half + pre * (0.5 - 0.5 * tangent * tangent) * (
        root_coef + (3.0 * 0.044715 * root_coef) * square
    )
    return (value, slope)


def normalize(rows):
    wide = rows.astype(jnp.float32)
    factor = lax.rsqrt(jnp.mean(wide * wide, axis=-1, keepdims=True) + norm_eps)
    return (wide * factor).astype(jnp.bfloat16)


contract_last = (((1,), (1,)), ((), ()))
ANY = pl.BlockSpec(memory_space=pl.ANY)
INSIDE = pl.BlockSpec(memory_space=pltpu.VMEM)


def vmem(mebibytes):
    return pltpu.CompilerParams(vmem_limit_bytes=mebibytes * 1024 * 1024)


def cost(flops, moved_bytes):
    return pl.CostEstimate(flops=2 * flops, bytes_accessed=moved_bytes, transcendentals=0)


def prepare_kernel(inputs, cotangent, a_ref, b_ref, held, sem):
    half = ROWS // 2
    loads = [
        pltpu.make_async_copy(inputs, held, sem.at[0]),
        pltpu.make_async_copy(cotangent.at[pl.ds(0, half)], a_ref.at[1], sem.at[1]),
        pltpu.make_async_copy(cotangent.at[pl.ds(half, half)], b_ref.at[1], sem.at[2]),
    ]
    for load in loads:
        load.start()
    loads[0].wait()
    a_ref[0] = normalize(held[:half])
    b_ref[0] = normalize(held[half:])
    for load in loads[1:]:
        load.wait()


def prepare(inputs, cotangent):
    half = jax.ShapeDtypeStruct((2, ROWS // 2, D), jnp.bfloat16)
    return pl.pallas_call(
        prepare_kernel,
        out_shape=[half, half],
        in_specs=[ANY] * 2,
        out_specs=[INSIDE] * 2,
        scratch_shapes=[pltpu.VMEM((ROWS, D), jnp.bfloat16), pltpu.SemaphoreType.DMA((3,))],
        compiler_params=vmem(16),
        cost_estimate=cost(0, 8 * ROWS * D),
    )(inputs, cotangent)


def stack_kernel(up, down, out, held, load_sem, store_sem):
    parts = 2
    rows = HELD // parts
    loads, stores = [], []
    for which, ref in enumerate((up, down)):
        for part in range(parts):
            k, at = which * parts + part, pl.ds(part * rows, rows)
            place = held.at[which, at]
            loads.append(pltpu.make_async_copy(ref.at[at], place, load_sem.at[k]))
            stores.append(pltpu.make_async_copy(place, out.at[which, at], store_sem.at[k]))
    for load in loads:
        load.start()
    for load, store in zip(loads, stores):
        load.wait()
        store.start()
    for store in stores:
        store.wait()


def stack_weights(up, down):
    shape = (2, HELD, D)
    return pl.pallas_call(
        stack_kernel,
        out_shape=jax.ShapeDtypeStruct(shape, jnp.bfloat16),
        in_specs=[ANY] * 2,
        out_specs=ANY,
        scratch_shapes=[pltpu.VMEM(shape, jnp.bfloat16)] + [pltpu.SemaphoreType.DMA((4,))] * 2,
        compiler_params=vmem(16),
        cost_estimate=cost(0, 8 * HELD * D),
    )(up, down)


def join_kernel(count, *refs):
    first = 0
    for ref in refs[:count]:
        rows = ref.shape[1]
        refs[-1][:, first : first + rows] = ref[...]
        first += rows


def join(pieces, after):
    rows = sum(p.shape[1] for p in pieces)
    return pl.pallas_call(
        functools.partial(join_kernel, len(pieces)),
        out_shape=jax.ShapeDtypeStruct((2, rows, D), jnp.bfloat16),
        in_specs=[INSIDE] * len(pieces) + [ANY] * len(after),
        out_specs=INSIDE,
        compiler_params=vmem(16),
        cost_estimate=cost(0, 8 * rows * D),
    )(*pieces, *after)


def cut_kernel(firsts, count_in, *refs):
    sem = refs[-1]
    loads = []
    for k, first in enumerate(firsts):
        out = refs[count_in + k]
        source = refs[k].at[:, pl.ds(first, out.shape[1])]
        loads.append(pltpu.make_async_copy(source, out, sem.at[k]))
        loads[-1].start()
    for load in loads:
        load.wait()


def cut(blocks, firsts, rows, after):
    out = jax.ShapeDtypeStruct((2, rows, D), jnp.bfloat16)
    operands = list(blocks) + list(after)
    return pl.pallas_call(
        functools.partial(cut_kernel, firsts, len(operands)),
        out_shape=[out] * len(blocks),
        in_specs=[ANY] * len(operands),
        out_specs=[INSIDE] * len(blocks),
        scratch_shapes=[pltpu.SemaphoreType.DMA((len(blocks),))],
        compiler_params=vmem(16),
        cost_estimate=cost(0, 8 * rows * D * len(blocks)),
    )(*operands)


def hidden_kernel(jobs, sizes, pieces, skipped, kept, tile, both, *refs):
    arrays = refs[: len(pieces)]
    blocks = refs[len(pieces) : len(pieces) + len(sizes)]
    refs = refs[len(pieces) + len(sizes) + skipped :]
    weights, tokens, pair, weight_sem, token_sem, out_sem, keep_sem = refs[-7:]
    top, total = weights.shape[1], tokens.shape[1]
    loads = []
    for k, (ref, (which, first, rows)) in enumerate(zip(arrays, pieces)):
        target = weights.at[:, pl.ds(first, rows)]
        if which is not None:
            target = weights.at[which, pl.ds(first, rows)]
        loads.append(pltpu.make_async_copy(ref, target, weight_sem.at[k]))
    first = 0
    for k, (ref, count) in enumerate(zip(blocks, sizes)):
        loads.append(pltpu.make_async_copy(ref, tokens.at[:, pl.ds(first, count)], token_sem.at[k]))
        first += count
    for load in loads:
        load.start()
    for load in loads:
        load.wait()
    stores = []
    if kept is not None:
        source = tokens.at[:, pl.ds(0, kept[1])]
        target = refs[2].at[:, pl.ds(kept[0], kept[1])]
        stores.append(pltpu.make_async_copy(source, target, keep_sem.at[0]))
        stores[-1].start()

    def step(i, carry):
        blocks = top // HELD
        here = i < blocks * both
        row = jnp.where(here, i % blocks, blocks - 1) * HELD
        token = jnp.where(here, i // blocks, i - (blocks - 1) * both) * tile
        rows = pl.ds(pl.multiple_of(row, HELD), HELD)
        at = pl.ds(pl.multiple_of(token, tile), tile)
        pre = up_scale * lax.dot_general(
            weights[0, rows], tokens[0, at], contract_last, preferred_element_type=jnp.float32
        )
        back = down_scale * lax.dot_general(
            weights[1, rows], tokens[1, at], contract_last, preferred_element_type=jnp.float32
        )
        value, slope = gelu_pair(pre)
        pair[0, rows, at] = (back * slope).astype(jnp.bfloat16)
        pair[1, rows, at] = value.astype(jnp.bfloat16)
        return carry

    lax.fori_loop(0, top // HELD * both + (total // tile - both), step, 0)
    for k, (shared, token, count, place) in enumerate(jobs):
        stores.append(
            pltpu.make_async_copy(
                pair.at[:, pl.ds(shared * HELD, HELD), pl.ds(token, count)],
                refs[shared].at[:, :, pl.ds(place, count)],
                out_sem.at[k],
            )
        )
        stores[-1].start()
    for store in stores:
        store.wait()


def hidden_step(jobs, pieces, arrays, blocks, results, kept, both, after=()):
    sizes = tuple(b.shape[1] for b in blocks)
    total = sum(sizes)
    top = max(first + rows for _, first, rows in pieces)
    shapes = ((2, HELD, EARLY), (2, HELD, TOKENS), (2, TOKENS, D))
    out = [jax.ShapeDtypeStruct(shape, jnp.bfloat16) for shape in shapes]
    operands = [*arrays, *blocks]
    aliases = {len(operands) + k: k for k in range(len(results))}
    operands += [*results, *after]
    flops = sum(4 * HELD * count * D for _, _, count, _ in jobs)
    skipped = len(results) + len(after)
    return pl.pallas_call(
        functools.partial(hidden_kernel, jobs, sizes, pieces, skipped, kept, 512, both),
        out_shape=out,
        in_specs=[ANY] * len(operands),
        out_specs=[ANY] * 3,
        input_output_aliases=aliases,
        scratch_shapes=[
            pltpu.VMEM((2, top, D), jnp.bfloat16),
            pltpu.VMEM((2, total, D), jnp.bfloat16),
            pltpu.VMEM((2, top, total), jnp.bfloat16),
            pltpu.SemaphoreType.DMA((len(pieces),)),
            pltpu.SemaphoreType.DMA((len(blocks),)),
            pltpu.SemaphoreType.DMA((len(jobs),)),
            pltpu.SemaphoreType.DMA((1,)),
        ],
        compiler_params=vmem(36 if len(jobs) > 1 else 24),
        cost_estimate=cost(flops, 4 * (total + top) * D + 4 * top * total),
    )(*operands)


def own_first_kernel(up, down, tokens_in, pair_in, *refs):
    out, pair, weights, tokens, columns, early, grads, sem = refs[-8:]
    width = FIRST_OWN * WIDTH
    loads = [
        pltpu.make_async_copy(up, weights.at[0], sem.at[0]),
        pltpu.make_async_copy(down, weights.at[1], sem.at[1]),
        pltpu.make_async_copy(tokens_in.at[:, pl.ds(EARLY, TOKENS - EARLY)], tokens, sem.at[2]),
        pltpu.make_async_copy(
            tokens_in.at[:, pl.ds(0, EARLY), pl.ds(0, width)], columns, sem.at[3]
        ),
        pltpu.make_async_copy(pair_in, early, sem.at[4]),
    ]
    for load in loads:
        load.start()
    for load in loads[:3]:
        load.wait()
    tile = 256

    def step(i, carry):
        at = pl.ds(pl.multiple_of(i * tile, tile), tile)
        pre = up_scale * lax.dot_general(
            weights[0], tokens[0, at], contract_last, preferred_element_type=jnp.float32
        )
        back = down_scale * lax.dot_general(
            weights[1], tokens[1, at], contract_last, preferred_element_type=jnp.float32
        )
        value, slope = gelu_pair(pre)
        pair[0, :, at] = (back * slope).astype(jnp.bfloat16)
        pair[1, :, at] = value.astype(jnp.bfloat16)
        return carry

    lax.fori_loop(0, (TOKENS - EARLY) // tile, step, 0)
    for load in loads[3:]:
        load.wait()

    def multiply(i, carry):
        which, k = i % 2, i // 2
        at = pl.ds(pl.multiple_of(k * WIDTH, WIDTH), WIDTH)
        grads[...] = jnp.dot(
            early[which], columns[which, :, at], preferred_element_type=jnp.float32
        )
        out[k, which] = grads[...] + jnp.dot(
            pair[which], tokens[which, :, at], preferred_element_type=jnp.float32
        )
        return carry

    lax.fori_loop(0, 2 * FIRST_OWN, multiply, 0)


def own_first(up, down, tokens, pair, after):
    rest = TOKENS - EARLY
    return pl.pallas_call(
        own_first_kernel,
        out_shape=[
            jax.ShapeDtypeStruct((FIRST_OWN, 2, HELD, WIDTH), jnp.float32),
            jax.ShapeDtypeStruct((2, HELD, rest), jnp.bfloat16),
        ],
        in_specs=[ANY] * (4 + len(after)),
        out_specs=[INSIDE] * 2,
        scratch_shapes=[
            pltpu.VMEM((2, HELD, D), jnp.bfloat16),
            pltpu.VMEM((2, rest, D), jnp.bfloat16),
            pltpu.VMEM((2, EARLY, FIRST_OWN * WIDTH), jnp.bfloat16),
            pltpu.VMEM((2, HELD, EARLY), jnp.bfloat16),
            pltpu.VMEM((HELD, WIDTH), jnp.float32),
            pltpu.SemaphoreType.DMA((5,)),
        ],
        compiler_params=vmem(24),
        cost_estimate=cost(4 * HELD * (rest * D + TOKENS * FIRST_OWN * WIDTH), 4 * (HELD + rest) * D),
    )(up, down, tokens, pair, *after)


def own_rest_kernel(pair, pair_last, tokens, out, grads):
    def multiply(which, carry):
        grads[...] = jnp.dot(pair[which], tokens[which, :EARLY], preferred_element_type=jnp.float32)
        out[0, which] = grads[...] + jnp.dot(
            pair_last[which], tokens[which, EARLY:], preferred_element_type=jnp.float32
        )
        return carry

    lax.fori_loop(0, 2, multiply, 0)


def own_rest(first, count, pair, pair_last, tokens, after):
    def kernel(*refs):
        own_rest_kernel(*refs[:3], *refs[-2:])

    return pl.pallas_call(
        kernel,
        out_shape=jax.ShapeDtypeStruct((count, 2, HELD, WIDTH), jnp.float32),
        grid=(count,),
        in_specs=[
            rows_spec(EARLY),
            rows_spec(TOKENS - EARLY),
            pl.BlockSpec((2, TOKENS, WIDTH), lambda j: (0, 0, j + first)),
        ]
        + [ANY] * len(after),
        out_specs=pl.BlockSpec((1, 2, HELD, WIDTH), lambda j: (j, 0, 0, 0)),
        scratch_shapes=[pltpu.VMEM((HELD, WIDTH), jnp.float32)],
        compiler_params=vmem(22),
        cost_estimate=cost(4 * HELD * TOKENS * count * WIDTH, 4 * TOKENS * (HELD + count * WIDTH)),
    )(pair, pair_last, tokens, *after)


def last_shared_kernel(*refs):
    weights_in, blocks = refs[0], refs[1:5]
    pair_in, tokens_in, pair_out, tokens_out, chunk = refs[5:10]
    weights, tokens, pair, columns, sem, out_sem = refs[10:]
    first, width = 0, WIDTH
    rest = TOKENS - EARLY
    loads = [pltpu.make_async_copy(weights_in, weights, sem.at[0])]
    row = 0
    for k, ref in enumerate(blocks):
        rows = ref.shape[1]
        loads.append(pltpu.make_async_copy(ref, tokens.at[:, pl.ds(row, rows)], sem.at[1 + k]))
        row += rows
    early, late = pl.ds(0, EARLY), pl.ds(EARLY, rest)
    source = tokens_in.at[:, early, pl.ds(first, width)]
    more = [
        pltpu.make_async_copy(pair_in.at[:, :, early], pair.at[:, :, early], sem.at[5]),
        pltpu.make_async_copy(source, columns, sem.at[6]),
    ]
    for load in loads + more:
        load.start()
    for load in loads:
        load.wait()
    stores = [pltpu.make_async_copy(tokens, tokens_out.at[:, late], out_sem.at[0])]
    stores[0].start()
    tile = 256

    def step(i, carry):
        at = pl.ds(pl.multiple_of(i * tile, tile), tile)
        to = pl.ds(pl.multiple_of(EARLY + i * tile, tile), tile)
        pre = up_scale * lax.dot_general(
            weights[0], tokens[0, at], contract_last, preferred_element_type=jnp.float32
        )
        back = down_scale * lax.dot_general(
            weights[1], tokens[1, at], contract_last, preferred_element_type=jnp.float32
        )
        value, slope = gelu_pair(pre)
        pair[0, :, to] = (back * slope).astype(jnp.bfloat16)
        pair[1, :, to] = value.astype(jnp.bfloat16)
        return carry

    lax.fori_loop(0, rest // tile, step, 0)
    stores.append(pltpu.make_async_copy(pair.at[:, :, late], pair_out.at[:, :, late], out_sem.at[1]))
    stores[1].start()
    for load in more:
        load.wait()
    for which, scale in enumerate((up_scale, down_scale)):
        grad = jnp.dot(pair[which, :, :EARLY], columns[which], preferred_element_type=jnp.float32)
        grad += jnp.dot(
            pair[which, :, EARLY:],
            tokens[which, :, first : first + width],
            preferred_element_type=jnp.float32,
        )
        chunk[which] = (scale * grad).astype(jnp.bfloat16)
    for store in stores:
        store.wait()


def last_shared(weights, blocks, pair, tokens):
    width = WIDTH
    return pl.pallas_call(
        last_shared_kernel,
        out_shape=[
            jax.ShapeDtypeStruct((2, HELD, TOKENS), jnp.bfloat16),
            jax.ShapeDtypeStruct((2, TOKENS, D), jnp.bfloat16),
            jax.ShapeDtypeStruct((2, HELD, width), jnp.bfloat16),
        ],
        in_specs=[ANY] * 7,
        out_specs=[ANY] * 2 + [INSIDE],
        input_output_aliases={5: 0, 6: 1},
        scratch_shapes=[
            pltpu.VMEM((2, HELD, D), jnp.bfloat16),
            pltpu.VMEM((2, TOKENS - EARLY, D), jnp.bfloat16),
            pltpu.VMEM((2, HELD, TOKENS), jnp.bfloat16),
            pltpu.VMEM((2, EARLY, width), jnp.bfloat16),
            pltpu.SemaphoreType.DMA((7,)),
            pltpu.SemaphoreType.DMA((2,)),
        ],
        compiler_params=vmem(22),
        cost_estimate=cost(
            4 * HELD * ((TOKENS - EARLY) * D + TOKENS * width), 4 * (HELD + TOKENS - EARLY) * D
        ),
    )(weights, *blocks, pair, tokens)


def column_spec(c):
    return pl.BlockSpec((HELD, WIDTH), lambda j: (0, c))


pair_spec = pl.BlockSpec((2, HELD, WIDTH), lambda j: (0, 0, 0))


def rows_spec(tokens):
    return pl.BlockSpec((2, HELD, tokens), lambda j: (0, 0, 0))


def theirs_kernel(count, skipped, pair, tokens, *refs):
    outs = refs[skipped : skipped + count]
    held, sem = refs[-2:]
    j = pl.program_id(0)
    slot = j % 2

    @pl.when(j >= 2)
    def _():
        pltpu.make_async_copy(held.at[slot], outs[0], sem.at[slot]).wait()

    def multiply(which, carry):
        scale = jnp.where(which == 0, up_scale, down_scale)
        grad = jnp.dot(pair[which], tokens[which], preferred_element_type=jnp.float32)
        held[slot, which] = (scale * grad).astype(jnp.bfloat16)
        return carry

    lax.fori_loop(0, 2, multiply, 0)
    for k, out in enumerate(outs):

        @pl.when(j == k)
        def _(out=out):
            pltpu.make_async_copy(held.at[slot], out, sem.at[slot]).start()

    @pl.when(j == count - 1)
    def _():
        for last in range(max(count - 2, 0), count):
            pltpu.make_async_copy(held.at[last % 2], outs[last], sem.at[last % 2]).wait()


def theirs_chunks(first, count, pair, tokens, after):
    return pl.pallas_call(
        functools.partial(theirs_kernel, count, len(after)),
        out_shape=[jax.ShapeDtypeStruct((2, HELD, WIDTH), jnp.bfloat16)] * count,
        grid=(count,),
        in_specs=[rows_spec(TOKENS), pl.BlockSpec((2, TOKENS, WIDTH), lambda j: (0, 0, j + first))]
        + [ANY] * len(after),
        out_specs=[ANY] * count,
        scratch_shapes=[
            pltpu.VMEM((2, 2, HELD, WIDTH), jnp.bfloat16),
            pltpu.SemaphoreType.DMA((2,)),
        ],
        compiler_params=vmem(22),
        cost_estimate=cost(4 * HELD * TOKENS * count * WIDTH, 4 * TOKENS * (HELD + count * WIDTH)),
    )(pair, tokens, *after)


def adam_kernel(mixing, *refs):
    own, bias, arrived = refs[:3]
    state = refs[3:9]
    outs = refs[-7 - mixing[1] :]
    tile = 32

    def step(i, carry):
        at = pl.ds(pl.multiple_of(i * tile, tile), tile)
        for which in (0, 1):
            weight, first, second = (ref[at] for ref in state[3 * which : 3 * which + 3])
            scale = (up_scale, down_scale)[which]
            grad = scale * own[0, which, at] + arrived[which, at].astype(jnp.float32)
            first_new = beta_one * first.astype(jnp.float32) + (1.0 - beta_one) * grad
            second_new = beta_two * second.astype(jnp.float32) + (1.0 - beta_two) * grad * grad
            update = (learn_rate * bias[0]) * first_new / (jnp.sqrt(second_new * bias[1]) + adam_eps)
            outs[0][which, at] = (weight.astype(jnp.float32) - update).astype(jnp.bfloat16)
            outs[1 + 2 * which][at] = first_new.astype(jnp.bfloat16)
            outs[2 + 2 * which][at] = second_new.astype(jnp.bfloat16)
            if mixing[0]:
                both = refs[9][which, at].astype(jnp.float32) + refs[10][which, at].astype(jnp.float32)
                outs[5 + which][at] = (both * 0.5).astype(jnp.bfloat16)
        return carry

    lax.fori_loop(0, HELD // tile, step, 0)


def mix_kernel(own, other, *refs):
    tile = 32

    def step(i, carry):
        at = pl.ds(pl.multiple_of(i * tile, tile), tile)
        for which in (0, 1):
            both = own[which, at].astype(jnp.float32) + other[which, at].astype(jnp.float32)
            refs[which - 2][at] = (both * 0.5).astype(jnp.bfloat16)
        return carry

    lax.fori_loop(0, HELD // tile, step, 0)


whole = jax.ShapeDtypeStruct((HELD, D), jnp.bfloat16)


def adam_chunk(c, own, bias, arrived, state, mixed, results, passing):
    operands = [own[0], bias, arrived, *state, *mixed]
    aliases = {len(operands) + k: 1 + k for k in range(len(results))}
    operands += results
    if passing:
        aliases[len(operands)] = 7
        operands += passing
    before = max(c - 2, 0)
    mixing = [column_spec(before)] * 2 if mixed or not results else [ANY] * 2
    block, place = (1, 2, HELD, WIDTH), own[1]
    smem = pl.BlockSpec(memory_space=pltpu.SMEM)
    pair = jax.ShapeDtypeStruct((2, HELD, WIDTH), jnp.bfloat16)
    return pl.pallas_call(
        functools.partial(adam_kernel, (bool(mixed), len(passing))),
        out_shape=[pair] + [whole] * 6 + [pair] * len(passing),
        grid=(1,),
        in_specs=[pl.BlockSpec(block, lambda j: (place, 0, 0, 0)), smem, pair_spec]
        + [column_spec(c)] * 6
        + [pair_spec] * len(mixed)
        + [ANY] * (len(results) + len(passing)),
        out_specs=[pair_spec] + [column_spec(c)] * 4 + mixing + [ANY] * len(passing),
        input_output_aliases=aliases,
        compiler_params=vmem(22),
        cost_estimate=cost(0, 60 * HELD * WIDTH),
    )(*operands)


def mix_chunk(c, own, other, results):
    return pl.pallas_call(
        mix_kernel,
        out_shape=[whole] * 2,
        grid=(1,),
        in_specs=[pair_spec] * 2 + [ANY] * 2,
        out_specs=[column_spec(c)] * 2,
        input_output_aliases={2: 0, 3: 1},
        compiler_params=vmem(22),
        cost_estimate=cost(0, 12 * HELD * WIDTH),
    )(own, other, *results)


def on_device(
    inputs,
    cotangent,
    up_weight,
    down_weight,
    momentum_up,
    momentum_down,
    variance_up,
    variance_down,
    step_index,
):
    up, down = up_weight[0], down_weight[0]
    half = ROWS // 2

    weights_sent = moved(stack_weights(up, down), y_sharing)
    a, b = prepare(inputs[0], cotangent[0])
    a_x, a_y = moved(a, x_other), moved(a, y_same_half)
    b_up, b_down = moved(b, z_up), moved(b, z_down)
    quarter = half // 2
    a_far = [moved(a_x[:, :quarter], y_same_half), moved(a_y[:, quarter:], x_other)]
    b_far = [moved(b_up[:, :quarter], z_up), moved(b_down[:, quarter:], z_down)]
    a_all = join([a, a_x, a_y, *a_far], [])
    b_all = join([b, b_up, b_down, *b_far], [])

    a_up, a_down = moved(a_all, z_up), moved(a_all, z_down)
    b_x, b_y = moved(b_all, x_other), moved(b_all, y_same_half)
    held = ((0, 0, HELD), (1, 0, HELD))
    job = (0, 0, 512, 0)
    results = hidden_step((job,), held, [up, down], [a_all, b_all], (), (0, 512), 1)

    mid = 2 * half
    halves = cut([a_up, a_down, b_x, b_y], (0, mid, 0, mid), mid, [results[0]])
    last = [
        moved(halves[0], z_up),
        moved(halves[1], z_down),
        moved(halves[2], y_same_half),
        moved(halves[3], x_other),
    ]
    results = hidden_step(
        ((0, 0, 1024, 512), (1, 0, 1024, 512), (1, 1024, 512, 0)),
        held + ((None, HELD, HELD),),
        [up, down, weights_sent],
        [a_up, a_down, b_x, b_y, a_all, b_all],
        results,
        (512, 1024),
        2,
        halves[:1],
    )
    own_pair = results[0]
    pair, tokens, theirs = last_shared(weights_sent, last, *results[1:])

    count = step_index[0].astype(jnp.float32)
    bias_one = 1.0 - jnp.exp(count * math.log(beta_one))
    bias_two = 1.0 - jnp.exp(count * math.log(beta_two))
    bias = jnp.stack([1.0 / bias_one, 1.0 / bias_two])
    state = [up, momentum_up[0], variance_up[0], down, momentum_down[0], variance_down[0]]

    def finish(hop):
        route = [(g, (g + hop) % 4) for g in range(4)]
        news, updated, others = (), [], []
        sent = [moved(theirs, y_sharing)]
        more = theirs_chunks(1, 2, pair, tokens, [])
        sent.append(moved(more[0], y_sharing))
        own, last_pair = own_first(up, down, tokens, own_pair, more[:1])
        place = [(own, c) for c in range(FIRST_OWN)]
        for c in range(CHUNKS):
            mixed = [updated[c - 2], others[c - 2]] if 2 <= c < MIXING else []
            passing = more[c + 1 : c + 2]
            out = adam_chunk(c, place[c], bias, sent[c], state, mixed, news, passing)
            updated.append(out[0])
            news = out[1:7]
            others.append(lax.ppermute(out[0], "rep", route))
            if passing:
                sent.append(moved(out[7], y_sharing))
            if c == 0:
                more += theirs_chunks(3, CHUNKS - 3, pair, tokens, [out[0]])
            for after, first, count in OWN_LATER:
                if c == after:
                    own = own_rest(first, count, own_pair, last_pair, tokens, [out[0]])
                    place += [(own, k) for k in range(count)]
        mixed = news[4:]
        for c in range(MIXING - 2, CHUNKS):
            mixed = mix_chunk(c, updated[c], others[c], mixed)
        return mixed[0], mixed[1], news[0], news[2], news[1], news[3]

    outs = lax.cond(step_index[0] % 2 == 0, lambda: finish(1), lambda: finish(2))
    return tuple(o[None] for o in outs)


def solution(mesh):
    shard = P("rep", "fsdp", None)
    return jax.shard_map(
        on_device,
        mesh=mesh,
        in_specs=(shard,) * 8 + (P(),),
        out_specs=(shard,) * 6,
        check_vma=False,
    )
```

```python
import functools
import math

import jax
import jax.numpy as jnp
from jax import lax
from jax.experimental import pallas as pl
from jax.experimental.pallas import tpu as pltpu
from jax.sharding import PartitionSpec as P

D = 1792
FF = 14336

beta_one = 0.9
beta_two = 0.95
learn_rate = 0.05
adam_eps = 1e-08
norm_eps = 1e-06
root_coef = math.sqrt(2.0 / math.pi)
up_scale = 1.0 / math.sqrt(D)
down_scale = 1.0 / math.sqrt(FF)

ROWS = 128
HELD = 448
SHARED = 2 * HELD
TOKENS = 2048
WIDTH = 256
CHUNKS = D // WIDTH
FIRST_OWN = 2
OWN_LATER = ((1, 2, 2), (2, 4, 3))
MIXING = CHUNKS
EARLY = 1536
NZ, NX, NY = 4, 2, 4


def moved(block, place):
    route = []
    for z in range(NZ):
        for x in range(NX):
            for y in range(NY):
                a, b, c = place(z, x, y)
                route.append(((z * NX + x) * NY + y, (a % NZ * NX + b) * NY + c))
    return lax.ppermute(block, "fsdp", route)


def z_up(z, x, y):
    return z + 1, x, y


def z_down(z, x, y):
    return z - 1, x, y


def z_over(z, x, y):
    return z + 2, x, y


def x_other(z, x, y):
    return z, 1 - x, y


def y_same_half(z, x, y):
    return z, x, 3 - y


def diagonal(z, x, y):
    return z, 1 - x, 3 - y


def y_sharing(z, x, y):
    return z, x, y ^ 1


def gelu_pair(pre):
    square = pre * pre
    tangent = jnp.tanh(pre * (root_coef + (root_coef * 0.044715) * square))
    half = 0.5 * tangent + 0.5
    value = pre * half
    slope = half + pre * (0.5 - 0.5 * tangent * tangent) * (
        root_coef + (3.0 * 0.044715 * root_coef) * square
    )
    return (value, slope)


def normalize(rows):
    wide = rows.astype(jnp.float32)
    factor = lax.rsqrt(jnp.mean(wide * wide, axis=-1, keepdims=True) + norm_eps)
    return (wide * factor).astype(jnp.bfloat16)


contract_last = (((1,), (1,)), ((), ()))
ANY = pl.BlockSpec(memory_space=pl.ANY)
INSIDE = pl.BlockSpec(memory_space=pltpu.VMEM)


def vmem(mebibytes):
    return pltpu.CompilerParams(vmem_limit_bytes=mebibytes * 1024 * 1024)


def cost(flops, moved_bytes):
    return pl.CostEstimate(flops=2 * flops, bytes_accessed=moved_bytes, transcendentals=0)


def prepare_kernel(inputs, cotangent, a_ref, b_ref, held, sem):
    half = ROWS // 2
    loads = [
        pltpu.make_async_copy(inputs, held, sem.at[0]),
        pltpu.make_async_copy(cotangent.at[pl.ds(0, half)], a_ref.at[1], sem.at[1]),
        pltpu.make_async_copy(cotangent.at[pl.ds(half, half)], b_ref.at[1], sem.at[2]),
    ]
    for load in loads:
        load.start()
    loads[0].wait()
    a_ref[0] = normalize(held[:half])
    b_ref[0] = normalize(held[half:])
    for load in loads[1:]:
        load.wait()


def prepare(inputs, cotangent):
    half = jax.ShapeDtypeStruct((2, ROWS // 2, D), jnp.bfloat16)
    return pl.pallas_call(
        prepare_kernel,
        out_shape=[half, half],
        in_specs=[ANY] * 2,
        out_specs=[INSIDE] * 2,
        scratch_shapes=[pltpu.VMEM((ROWS, D), jnp.bfloat16), pltpu.SemaphoreType.DMA((3,))],
        compiler_params=vmem(8),
        cost_estimate=cost(0, 8 * ROWS * D),
    )(inputs, cotangent)


def stack_kernel(up, down, out, held, load_sem, store_sem):
    parts = 2
    rows = HELD // parts
    loads, stores = [], []
    for which, ref in enumerate((up, down)):
        for part in range(parts):
            k, at = which * parts + part, pl.ds(part * rows, rows)
            place = held.at[which, at]
            loads.append(pltpu.make_async_copy(ref.at[at], place, load_sem.at[k]))
            stores.append(pltpu.make_async_copy(place, out.at[which, at], store_sem.at[k]))
    for load in loads:
        load.start()
    for load, store in zip(loads, stores):
        load.wait()
        store.start()
    for store in stores:
        store.wait()


def stack_weights(up, down):
    shape = (2, HELD, D)
    return pl.pallas_call(
        stack_kernel,
        out_shape=jax.ShapeDtypeStruct(shape, jnp.bfloat16),
        in_specs=[ANY] * 2,
        out_specs=ANY,
        scratch_shapes=[pltpu.VMEM(shape, jnp.bfloat16)] + [pltpu.SemaphoreType.DMA((4,))] * 2,
        compiler_params=vmem(8),
        cost_estimate=cost(0, 8 * HELD * D),
    )(up, down)


def join_kernel(count, *refs):
    first = 0
    for ref in refs[:count]:
        rows = ref.shape[1]
        refs[-1][:, first : first + rows] = ref[...]
        first += rows


def join(pieces, after):
    rows = sum(p.shape[1] for p in pieces)
    return pl.pallas_call(
        functools.partial(join_kernel, len(pieces)),
        out_shape=jax.ShapeDtypeStruct((2, rows, D), jnp.bfloat16),
        in_specs=[INSIDE] * len(pieces) + [ANY] * len(after),
        out_specs=INSIDE,
        compiler_params=vmem(8),
        cost_estimate=cost(0, 8 * rows * D),
    )(*pieces, *after)


def cut_kernel(firsts, count_in, *refs):
    sem = refs[-1]
    loads = []
    for k, first in enumerate(firsts):
        out = refs[count_in + k]
        source = refs[k].at[:, pl.ds(first, out.shape[1])]
        loads.append(pltpu.make_async_copy(source, out, sem.at[k]))
        loads[-1].start()
    for load in loads:
        load.wait()


def cut(blocks, firsts, rows, after):
    out = jax.ShapeDtypeStruct((2, rows, D), jnp.bfloat16)
    operands = list(blocks) + list(after)
    return pl.pallas_call(
        functools.partial(cut_kernel, firsts, len(operands)),
        out_shape=[out] * len(blocks),
        in_specs=[ANY] * len(operands),
        out_specs=[INSIDE] * len(blocks),
        scratch_shapes=[pltpu.SemaphoreType.DMA((len(blocks),))],
        compiler_params=vmem(8),
        cost_estimate=cost(0, 8 * rows * D * len(blocks)),
    )(*operands)


def hidden_kernel(jobs, sizes, pieces, skipped, kept, tile, both, *refs):
    arrays = refs[: len(pieces)]
    blocks = refs[len(pieces) : len(pieces) + len(sizes)]
    refs = refs[len(pieces) + len(sizes) + skipped :]
    weights, tokens, pair, weight_sem, token_sem, out_sem, keep_sem = refs[-7:]
    top, total = weights.shape[1], tokens.shape[1]
    loads = []
    for k, (ref, (which, first, rows)) in enumerate(zip(arrays, pieces)):
        target = weights.at[:, pl.ds(first, rows)]
        if which is not None:
            target = weights.at[which, pl.ds(first, rows)]
        loads.append(pltpu.make_async_copy(ref, target, weight_sem.at[k]))
    first = 0
    for k, (ref, count) in enumerate(zip(blocks, sizes)):
        loads.append(pltpu.make_async_copy(ref, tokens.at[:, pl.ds(first, count)], token_sem.at[k]))
        first += count
    for load in loads:
        load.start()
    for load in loads:
        load.wait()
    stores = []
    if kept is not None:
        source = tokens.at[:, pl.ds(0, kept[1])]
        target = refs[2].at[:, pl.ds(kept[0], kept[1])]
        stores.append(pltpu.make_async_copy(source, target, keep_sem.at[0]))
        stores[-1].start()

    def step(i, carry):
        blocks = top // HELD
        here = i < blocks * both
        row = jnp.where(here, i % blocks, blocks - 1) * HELD
        token = jnp.where(here, i // blocks, i - (blocks - 1) * both) * tile
        rows = pl.ds(pl.multiple_of(row, HELD), HELD)
        at = pl.ds(pl.multiple_of(token, tile), tile)
        pre = up_scale * lax.dot_general(
            weights[0, rows], tokens[0, at], contract_last, preferred_element_type=jnp.float32
        )
        back = down_scale * lax.dot_general(
            weights[1, rows], tokens[1, at], contract_last, preferred_element_type=jnp.float32
        )
        value, slope = gelu_pair(pre)
        pair[0, rows, at] = (back * slope).astype(jnp.bfloat16)
        pair[1, rows, at] = value.astype(jnp.bfloat16)
        return carry

    lax.fori_loop(0, top // HELD * both + (total // tile - both), step, 0)
    for k, (shared, token, count, place) in enumerate(jobs):
        stores.append(
            pltpu.make_async_copy(
                pair.at[:, pl.ds(shared * HELD, HELD), pl.ds(token, count)],
                refs[shared].at[:, :, pl.ds(place, count)],
                out_sem.at[k],
            )
        )
        stores[-1].start()
    for store in stores:
        store.wait()


def hidden_step(jobs, pieces, arrays, blocks, results, kept, both, after=()):
    sizes = tuple(b.shape[1] for b in blocks)
    total = sum(sizes)
    top = max(first + rows for _, first, rows in pieces)
    shapes = ((2, HELD, EARLY), (2, HELD, TOKENS), (2, TOKENS, D))
    out = [jax.ShapeDtypeStruct(shape, jnp.bfloat16) for shape in shapes]
    operands = [*arrays, *blocks]
    aliases = {len(operands) + k: k for k in range(len(results))}
    operands += [*results, *after]
    flops = sum(4 * HELD * count * D for _, _, count, _ in jobs)
    skipped = len(results) + len(after)
    return pl.pallas_call(
        functools.partial(hidden_kernel, jobs, sizes, pieces, skipped, kept, 512, both),
        out_shape=out,
        in_specs=[ANY] * len(operands),
        out_specs=[ANY] * 3,
        input_output_aliases=aliases,
        scratch_shapes=[
            pltpu.VMEM((2, top, D), jnp.bfloat16),
            pltpu.VMEM((2, total, D), jnp.bfloat16),
            pltpu.VMEM((2, top, total), jnp.bfloat16),
            pltpu.SemaphoreType.DMA((len(pieces),)),
            pltpu.SemaphoreType.DMA((len(blocks),)),
            pltpu.SemaphoreType.DMA((len(jobs),)),
            pltpu.SemaphoreType.DMA((1,)),
        ],
        compiler_params=vmem(30 if len(jobs) > 1 else 16),
        cost_estimate=cost(flops, 4 * (total + top) * D + 4 * top * total),
    )(*operands)


def own_first_kernel(up, down, tokens_in, pair_in, *refs):
    out, pair, weights, tokens, columns, early, grads, sem = refs[-8:]
    width = FIRST_OWN * WIDTH
    loads = [
        pltpu.make_async_copy(up, weights.at[0], sem.at[0]),
        pltpu.make_async_copy(down, weights.at[1], sem.at[1]),
        pltpu.make_async_copy(tokens_in.at[:, pl.ds(EARLY, TOKENS - EARLY)], tokens, sem.at[2]),
        pltpu.make_async_copy(
            tokens_in.at[:, pl.ds(0, EARLY), pl.ds(0, width)], columns, sem.at[3]
        ),
        pltpu.make_async_copy(pair_in, early, sem.at[4]),
    ]
    for load in loads:
        load.start()
    for load in loads[:3]:
        load.wait()
    tile = 256

    def step(i, carry):
        at = pl.ds(pl.multiple_of(i * tile, tile), tile)
        pre = up_scale * lax.dot_general(
            weights[0], tokens[0, at], contract_last, preferred_element_type=jnp.float32
        )
        back = down_scale * lax.dot_general(
            weights[1], tokens[1, at], contract_last, preferred_element_type=jnp.float32
        )
        value, slope = gelu_pair(pre)
        pair[0, :, at] = (back * slope).astype(jnp.bfloat16)
        pair[1, :, at] = value.astype(jnp.bfloat16)
        return carry

    lax.fori_loop(0, (TOKENS - EARLY) // tile, step, 0)
    for load in loads[3:]:
        load.wait()

    def multiply(i, carry):
        which, k = i % 2, i // 2
        at = pl.ds(pl.multiple_of(k * WIDTH, WIDTH), WIDTH)
        grads[...] = jnp.dot(
            early[which], columns[which, :, at], preferred_element_type=jnp.float32
        )
        out[k, which] = grads[...] + jnp.dot(
            pair[which], tokens[which, :, at], preferred_element_type=jnp.float32
        )
        return carry

    lax.fori_loop(0, 2 * FIRST_OWN, multiply, 0)


def own_first(up, down, tokens, pair, after):
    rest = TOKENS - EARLY
    return pl.pallas_call(
        own_first_kernel,
        out_shape=[
            jax.ShapeDtypeStruct((FIRST_OWN, 2, HELD, WIDTH), jnp.float32),
            jax.ShapeDtypeStruct((2, HELD, rest), jnp.bfloat16),
        ],
        in_specs=[ANY] * (4 + len(after)),
        out_specs=[INSIDE] * 2,
        scratch_shapes=[
            pltpu.VMEM((2, HELD, D), jnp.bfloat16),
            pltpu.VMEM((2, rest, D), jnp.bfloat16),
            pltpu.VMEM((2, EARLY, FIRST_OWN * WIDTH), jnp.bfloat16),
            pltpu.VMEM((2, HELD, EARLY), jnp.bfloat16),
            pltpu.VMEM((HELD, WIDTH), jnp.float32),
            pltpu.SemaphoreType.DMA((5,)),
        ],
        compiler_params=vmem(20),
        cost_estimate=cost(4 * HELD * (rest * D + TOKENS * FIRST_OWN * WIDTH), 4 * (HELD + rest) * D),
    )(up, down, tokens, pair, *after)


def own_rest_kernel(pair, pair_last, tokens, out, grads):
    def multiply(which, carry):
        grads[...] = jnp.dot(pair[which], tokens[which, :EARLY], preferred_element_type=jnp.float32)
        out[0, which] = grads[...] + jnp.dot(
            pair_last[which], tokens[which, EARLY:], preferred_element_type=jnp.float32
        )
        return carry

    lax.fori_loop(0, 2, multiply, 0)


def own_rest(first, count, pair, pair_last, tokens, after):
    def kernel(*refs):
        own_rest_kernel(*refs[:3], *refs[-2:])

    return pl.pallas_call(
        kernel,
        out_shape=jax.ShapeDtypeStruct((count, 2, HELD, WIDTH), jnp.float32),
        grid=(count,),
        in_specs=[
            rows_spec(EARLY),
            rows_spec(TOKENS - EARLY),
            pl.BlockSpec((2, TOKENS, WIDTH), lambda j: (0, 0, j + first)),
        ]
        + [ANY] * len(after),
        out_specs=pl.BlockSpec((1, 2, HELD, WIDTH), lambda j: (j, 0, 0, 0)),
        scratch_shapes=[pltpu.VMEM((HELD, WIDTH), jnp.float32)],
        compiler_params=vmem(18),
        cost_estimate=cost(4 * HELD * TOKENS * count * WIDTH, 4 * TOKENS * (HELD + count * WIDTH)),
    )(pair, pair_last, tokens, *after)


def last_shared_kernel(*refs):
    weights_in, blocks = refs[0], refs[1:5]
    pair_in, tokens_in, pair_out, tokens_out, chunk = refs[5:10]
    weights, tokens, pair, columns, sem, out_sem = refs[10:]
    first, width = 0, WIDTH
    rest = TOKENS - EARLY
    weights_load = pltpu.make_async_copy(weights_in, weights, sem.at[0])
    loads, row = [], 0
    for k, ref in enumerate(blocks):
        rows = ref.shape[1]
        loads.append(pltpu.make_async_copy(ref, tokens.at[:, pl.ds(row, rows)], sem.at[1 + k]))
        row += rows
    early, late = pl.ds(0, EARLY), pl.ds(EARLY, rest)
    source = tokens_in.at[:, early, pl.ds(first, width)]
    more = [
        pltpu.make_async_copy(pair_in.at[:, :, early], pair.at[:, :, early], sem.at[5]),
        pltpu.make_async_copy(source, columns, sem.at[6]),
    ]
    for load in [*loads[:2], weights_load, *loads[2:], *more]:
        load.start()
    weights_load.wait()
    tile = 256

    def step(i, carry):
        at = pl.ds(pl.multiple_of(i * tile, tile), tile)
        to = pl.ds(pl.multiple_of(EARLY + i * tile, tile), tile)
        pre = up_scale * lax.dot_general(
            weights[0], tokens[0, at], contract_last, preferred_element_type=jnp.float32
        )
        back = down_scale * lax.dot_general(
            weights[1], tokens[1, at], contract_last, preferred_element_type=jnp.float32
        )
        value, slope = gelu_pair(pre)
        pair[0, :, to] = (back * slope).astype(jnp.bfloat16)
        pair[1, :, to] = value.astype(jnp.bfloat16)
        return carry

    def arriving(i, carry):
        for parity in (0, 1):

            @pl.when(i == parity)
            def _(parity=parity):
                for load in loads[2 * parity : 2 * parity + 2]:
                    load.wait()

        return step(i, carry)

    lax.fori_loop(0, rest // tile, arriving, 0)
    stores = [pltpu.make_async_copy(tokens, tokens_out.at[:, late], out_sem.at[0])]
    stores[0].start()
    stores.append(pltpu.make_async_copy(pair.at[:, :, late], pair_out.at[:, :, late], out_sem.at[1]))
    stores[1].start()
    for load in more:
        load.wait()
    for which, scale in enumerate((up_scale, down_scale)):
        grad = jnp.dot(pair[which, :, :EARLY], columns[which], preferred_element_type=jnp.float32)
        grad += jnp.dot(
            pair[which, :, EARLY:],
            tokens[which, :, first : first + width],
            preferred_element_type=jnp.float32,
        )
        chunk[which] = (scale * grad).astype(jnp.bfloat16)
    for store in stores:
        store.wait()


def last_shared(weights, blocks, pair, tokens):
    width = WIDTH
    return pl.pallas_call(
        last_shared_kernel,
        out_shape=[
            jax.ShapeDtypeStruct((2, HELD, TOKENS), jnp.bfloat16),
            jax.ShapeDtypeStruct((2, TOKENS, D), jnp.bfloat16),
            jax.ShapeDtypeStruct((2, HELD, width), jnp.bfloat16),
        ],
        in_specs=[ANY] * 7,
        out_specs=[ANY] * 2 + [INSIDE],
        input_output_aliases={5: 0, 6: 1},
        scratch_shapes=[
            pltpu.VMEM((2, HELD, D), jnp.bfloat16),
            pltpu.VMEM((2, TOKENS - EARLY, D), jnp.bfloat16),
            pltpu.VMEM((2, HELD, TOKENS), jnp.bfloat16),
            pltpu.VMEM((2, EARLY, width), jnp.bfloat16),
            pltpu.SemaphoreType.DMA((7,)),
            pltpu.SemaphoreType.DMA((2,)),
        ],
        compiler_params=vmem(16),
        cost_estimate=cost(
            4 * HELD * ((TOKENS - EARLY) * D + TOKENS * width), 4 * (HELD + TOKENS - EARLY) * D
        ),
    )(weights, *blocks, pair, tokens)


def column_spec(c):
    return pl.BlockSpec((HELD, WIDTH), lambda j: (0, c))


pair_spec = pl.BlockSpec((2, HELD, WIDTH), lambda j: (0, 0, 0))


def rows_spec(tokens):
    return pl.BlockSpec((2, HELD, tokens), lambda j: (0, 0, 0))


def theirs_kernel(count, skipped, pair, tokens, *refs):
    outs = refs[skipped : skipped + count]
    held, sem = refs[-2:]
    j = pl.program_id(0)
    slot = j % 2

    @pl.when(j >= 2)
    def _():
        pltpu.make_async_copy(held.at[slot], outs[0], sem.at[slot]).wait()

    def multiply(which, carry):
        scale = jnp.where(which == 0, up_scale, down_scale)
        grad = jnp.dot(pair[which], tokens[which], preferred_element_type=jnp.float32)
        held[slot, which] = (scale * grad).astype(jnp.bfloat16)
        return carry

    lax.fori_loop(0, 2, multiply, 0)
    for k, out in enumerate(outs):

        @pl.when(j == k)
        def _(out=out):
            pltpu.make_async_copy(held.at[slot], out, sem.at[slot]).start()

    @pl.when(j == count - 1)
    def _():
        for last in range(max(count - 2, 0), count):
            pltpu.make_async_copy(held.at[last % 2], outs[last], sem.at[last % 2]).wait()


def theirs_chunks(first, count, pair, tokens, after):
    return pl.pallas_call(
        functools.partial(theirs_kernel, count, len(after)),
        out_shape=[jax.ShapeDtypeStruct((2, HELD, WIDTH), jnp.bfloat16)] * count,
        grid=(count,),
        in_specs=[rows_spec(TOKENS), pl.BlockSpec((2, TOKENS, WIDTH), lambda j: (0, 0, j + first))]
        + [ANY] * len(after),
        out_specs=[ANY] * count,
        scratch_shapes=[
            pltpu.VMEM((2, 2, HELD, WIDTH), jnp.bfloat16),
            pltpu.SemaphoreType.DMA((2,)),
        ],
        compiler_params=vmem(16),
        cost_estimate=cost(4 * HELD * TOKENS * count * WIDTH, 4 * TOKENS * (HELD + count * WIDTH)),
    )(pair, tokens, *after)


def adam_kernel(mixing, *refs):
    own, bias, arrived = refs[:3]
    state = refs[3:9]
    outs = refs[-7 - mixing[1] :]
    tile = 32

    def step(i, carry):
        at = pl.ds(pl.multiple_of(i * tile, tile), tile)
        for which in (0, 1):
            weight, first, second = (ref[at] for ref in state[3 * which : 3 * which + 3])
            scale = (up_scale, down_scale)[which]
            grad = scale * own[0, which, at] + arrived[which, at].astype(jnp.float32)
            first_new = beta_one * first.astype(jnp.float32) + (1.0 - beta_one) * grad
            second_new = beta_two * second.astype(jnp.float32) + (1.0 - beta_two) * grad * grad
            update = (learn_rate * bias[0]) * first_new / (jnp.sqrt(second_new * bias[1]) + adam_eps)
            outs[0][which, at] = (weight.astype(jnp.float32) - update).astype(jnp.bfloat16)
            outs[1 + 2 * which][at] = first_new.astype(jnp.bfloat16)
            outs[2 + 2 * which][at] = second_new.astype(jnp.bfloat16)
            if mixing[0]:
                both = refs[9][which, at].astype(jnp.float32) + refs[10][which, at].astype(jnp.float32)
                outs[5 + which][at] = (both * 0.5).astype(jnp.bfloat16)
        return carry

    lax.fori_loop(0, HELD // tile, step, 0)


def mix_kernel(own, other, *refs):
    tile = 32

    def step(i, carry):
        at = pl.ds(pl.multiple_of(i * tile, tile), tile)
        for which in (0, 1):
            both = own[which, at].astype(jnp.float32) + other[which, at].astype(jnp.float32)
            refs[which - 2][at] = (both * 0.5).astype(jnp.bfloat16)
        return carry

    lax.fori_loop(0, HELD // tile, step, 0)


whole = jax.ShapeDtypeStruct((HELD, D), jnp.bfloat16)


def adam_chunk(c, own, bias, arrived, state, mixed, results, passing):
    operands = [own[0], bias, arrived, *state, *mixed]
    aliases = {len(operands) + k: 1 + k for k in range(len(results))}
    operands += results
    if passing:
        aliases[len(operands)] = 7
        operands += passing
    before = max(c - 2, 0)
    mixing = [column_spec(before)] * 2 if mixed or not results else [ANY] * 2
    block, place = (1, 2, HELD, WIDTH), own[1]
    smem = pl.BlockSpec(memory_space=pltpu.SMEM)
    pair = jax.ShapeDtypeStruct((2, HELD, WIDTH), jnp.bfloat16)
    return pl.pallas_call(
        functools.partial(adam_kernel, (bool(mixed), len(passing))),
        out_shape=[pair] + [whole] * 6 + [pair] * len(passing),
        grid=(1,),
        in_specs=[pl.BlockSpec(block, lambda j: (place, 0, 0, 0)), smem, pair_spec]
        + [column_spec(c)] * 6
        + [pair_spec] * len(mixed)
        + [ANY] * (len(results) + len(passing)),
        out_specs=[pair_spec] + [column_spec(c)] * 4 + mixing + [ANY] * len(passing),
        input_output_aliases=aliases,
        compiler_params=vmem(12),
        cost_estimate=cost(0, 60 * HELD * WIDTH),
    )(*operands)


def mix_chunk(c, own, other, results):
    return pl.pallas_call(
        mix_kernel,
        out_shape=[whole] * 2,
        grid=(1,),
        in_specs=[pair_spec] * 2 + [ANY] * 2,
        out_specs=[column_spec(c)] * 2,
        input_output_aliases={2: 0, 3: 1},
        compiler_params=vmem(8),
        cost_estimate=cost(0, 12 * HELD * WIDTH),
    )(own, other, *results)


def on_device(
    inputs,
    cotangent,
    up_weight,
    down_weight,
    momentum_up,
    momentum_down,
    variance_up,
    variance_down,
    step_index,
):
    up, down = up_weight[0], down_weight[0]
    half = ROWS // 2

    weights_sent = moved(stack_weights(up, down), y_sharing)
    a, b = prepare(inputs[0], cotangent[0])
    a_x, a_y = moved(a, x_other), moved(a, y_same_half)
    b_up, b_down = moved(b, z_up), moved(b, z_down)
    quarter = half // 2
    a_far = [moved(a_x[:, :quarter], y_same_half), moved(a_y[:, quarter:], x_other)]
    b_far = [moved(b_up[:, :quarter], z_up), moved(b_down[:, quarter:], z_down)]
    a_all = join([a, a_x, a_y, *a_far], [])
    b_all = join([b, b_up, b_down, *b_far], [])

    a_up, a_down = moved(a_all, z_up), moved(a_all, z_down)
    b_x, b_y = moved(b_all, x_other), moved(b_all, y_same_half)
    held = ((0, 0, HELD), (1, 0, HELD))
    job = (0, 0, 512, 0)
    results = hidden_step((job,), held, [up, down], [a_all, b_all], (), (0, 512), 1)

    mid = 2 * half
    halves = cut([a_up, a_down], (0, mid), mid, [results[0]])
    halves += cut([b_x, b_y], (0, mid), mid, [results[0]])
    last = [
        moved(halves[0], z_up),
        moved(halves[1], z_down),
        moved(halves[2], y_same_half),
        moved(halves[3], x_other),
    ]
    results = hidden_step(
        ((0, 0, 1024, 512), (1, 0, 1024, 512), (1, 1024, 512, 0)),
        held + ((None, HELD, HELD),),
        [up, down, weights_sent],
        [a_up, a_down, b_x, b_y, a_all, b_all],
        results,
        (512, 1024),
        2,
        halves[::2],
    )
    own_pair = results[0]
    pair, tokens, theirs = last_shared(weights_sent, last, *results[1:])

    count = step_index[0].astype(jnp.float32)
    bias_one = 1.0 - jnp.exp(count * math.log(beta_one))
    bias_two = 1.0 - jnp.exp(count * math.log(beta_two))
    bias = jnp.stack([1.0 / bias_one, 1.0 / bias_two])
    state = [up, momentum_up[0], variance_up[0], down, momentum_down[0], variance_down[0]]

    def finish(hop):
        route = [(g, (g + hop) % 4) for g in range(4)]
        news, updated, others = (), [], []
        sent = [moved(theirs, y_sharing)]
        more = theirs_chunks(1, 2, pair, tokens, [])
        sent.append(moved(more[0], y_sharing))
        own, last_pair = own_first(up, down, tokens, own_pair, more[:1])
        place = [(own, c) for c in range(FIRST_OWN)]
        for c in range(CHUNKS):
            mixed = [updated[c - 2], others[c - 2]] if 2 <= c < MIXING else []
            passing = more[c + 1 : c + 2]
            out = adam_chunk(c, place[c], bias, sent[c], state, mixed, news, passing)
            updated.append(out[0])
            news = out[1:7]
            others.append(lax.ppermute(out[0], "rep", route))
            if passing:
                sent.append(moved(out[7], y_sharing))
            if c == 0:
                more += theirs_chunks(3, CHUNKS - 3, pair, tokens, [out[0]])
            for after, first, count in OWN_LATER:
                if c == after:
                    own = own_rest(first, count, own_pair, last_pair, tokens, [out[0]])
                    place += [(own, k) for k in range(count)]
        mixed = news[4:]
        for c in range(MIXING - 2, CHUNKS):
            mixed = mix_chunk(c, updated[c], others[c], mixed)
        return mixed[0], mixed[1], news[0], news[2], news[1], news[3]

    outs = lax.cond(step_index[0] % 2 == 0, lambda: finish(1), lambda: finish(2))
    return tuple(o[None] for o in outs)


def solution(mesh):
    shard = P("rep", "fsdp", None)
    return jax.shard_map(
        on_device,
        mesh=mesh,
        in_specs=(shard,) * 8 + (P(),),
        out_specs=(shard,) * 6,
        check_vma=False,
    )
```

```python
import functools
import math

import jax
import jax.numpy as jnp
from jax import lax
from jax.experimental import pallas as pl
from jax.experimental.pallas import tpu as pltpu
from jax.sharding import PartitionSpec as P

D = 1792
FF = 14336

beta_one = 0.9
beta_two = 0.95
learn_rate = 0.05
adam_eps = 1e-08
norm_eps = 1e-06
root_coef = math.sqrt(2.0 / math.pi)
up_scale = 1.0 / math.sqrt(D)
down_scale = 1.0 / math.sqrt(FF)

ROWS = 128
HELD = 448
SHARED = 2 * HELD
TOKENS = 2048
WIDTH = 256
BLOCKS = D // WIDTH
CHUNKS = tuple((WIDTH * k, WIDTH) for k in range(BLOCKS - 1)) + ((D - 256, 128), (D - 128, 128))
FIRST_OWN = 2
OWN_LATER = ((1, 2, 2), (2, 4, 3))
THEIRS_LATER = ((0, 3, 2), (2, 5, 2))
MIXING = 7
EARLY = 1536
NZ, NX, NY = 4, 2, 4


def moved(block, place):
    route = []
    for z in range(NZ):
        for x in range(NX):
            for y in range(NY):
                a, b, c = place(z, x, y)
                route.append(((z * NX + x) * NY + y, (a % NZ * NX + b) * NY + c))
    return lax.ppermute(block, "fsdp", route)


def z_up(z, x, y):
    return z + 1, x, y


def z_down(z, x, y):
    return z - 1, x, y


def z_over(z, x, y):
    return z + 2, x, y


def x_other(z, x, y):
    return z, 1 - x, y


def y_same_half(z, x, y):
    return z, x, 3 - y


def diagonal(z, x, y):
    return z, 1 - x, 3 - y


def y_sharing(z, x, y):
    return z, x, y ^ 1


def gelu_pair(pre):
    square = pre * pre
    tangent = jnp.tanh(pre * (root_coef + (root_coef * 0.044715) * square))
    half = 0.5 * tangent + 0.5
    value = pre * half
    slope = half + pre * (0.5 - 0.5 * tangent * tangent) * (
        root_coef + (3.0 * 0.044715 * root_coef) * square
    )
    return (value, slope)


def normalize(rows):
    wide = rows.astype(jnp.float32)
    factor = lax.rsqrt(jnp.mean(wide * wide, axis=-1, keepdims=True) + norm_eps)
    return (wide * factor).astype(jnp.bfloat16)


contract_last = (((1,), (1,)), ((), ()))
ANY = pl.BlockSpec(memory_space=pl.ANY)
INSIDE = pl.BlockSpec(memory_space=pltpu.VMEM)


def vmem(mebibytes):
    return pltpu.CompilerParams(vmem_limit_bytes=mebibytes * 1024 * 1024)


def cost(flops, moved_bytes):
    return pl.CostEstimate(flops=2 * flops, bytes_accessed=moved_bytes, transcendentals=0)


def prepare_kernel(inputs, cotangent, a_ref, b_ref, held, sem):
    half = ROWS // 2
    loads = [
        pltpu.make_async_copy(inputs, held, sem.at[0]),
        pltpu.make_async_copy(cotangent.at[pl.ds(0, half)], a_ref.at[1], sem.at[1]),
        pltpu.make_async_copy(cotangent.at[pl.ds(half, half)], b_ref.at[1], sem.at[2]),
    ]
    for load in loads:
        load.start()
    loads[0].wait()
    a_ref[0] = normalize(held[:half])
    b_ref[0] = normalize(held[half:])
    for load in loads[1:]:
        load.wait()


def prepare(inputs, cotangent):
    half = jax.ShapeDtypeStruct((2, ROWS // 2, D), jnp.bfloat16)
    return pl.pallas_call(
        prepare_kernel,
        out_shape=[half, half],
        in_specs=[ANY] * 2,
        out_specs=[INSIDE] * 2,
        scratch_shapes=[pltpu.VMEM((ROWS, D), jnp.bfloat16), pltpu.SemaphoreType.DMA((3,))],
        compiler_params=vmem(8),
        cost_estimate=cost(0, 8 * ROWS * D),
    )(inputs, cotangent)


def stack_kernel(up, down, out, held, load_sem, store_sem):
    parts = 2
    rows = HELD // parts
    loads, stores = [], []
    for which, ref in enumerate((up, down)):
        for part in range(parts):
            k, at = which * parts + part, pl.ds(part * rows, rows)
            place = held.at[which, at]
            loads.append(pltpu.make_async_copy(ref.at[at], place, load_sem.at[k]))
            stores.append(pltpu.make_async_copy(place, out.at[which, at], store_sem.at[k]))
    for load in loads:
        load.start()
    for load, store in zip(loads, stores):
        load.wait()
        store.start()
    for store in stores:
        store.wait()


def stack_weights(up, down):
    shape = (2, HELD, D)
    return pl.pallas_call(
        stack_kernel,
        out_shape=jax.ShapeDtypeStruct(shape, jnp.bfloat16),
        in_specs=[ANY] * 2,
        out_specs=ANY,
        scratch_shapes=[pltpu.VMEM(shape, jnp.bfloat16)] + [pltpu.SemaphoreType.DMA((4,))] * 2,
        compiler_params=vmem(8),
        cost_estimate=cost(0, 8 * HELD * D),
    )(up, down)


def join_kernel(count, *refs):
    first = 0
    for ref in refs[:count]:
        rows = ref.shape[1]
        refs[-1][:, first : first + rows] = ref[...]
        first += rows


def join(pieces, after):
    rows = sum(p.shape[1] for p in pieces)
    return pl.pallas_call(
        functools.partial(join_kernel, len(pieces)),
        out_shape=jax.ShapeDtypeStruct((2, rows, D), jnp.bfloat16),
        in_specs=[INSIDE] * len(pieces) + [ANY] * len(after),
        out_specs=INSIDE,
        compiler_params=vmem(8),
        cost_estimate=cost(0, 8 * rows * D),
    )(*pieces, *after)


def cut_kernel(firsts, count_in, *refs):
    sem = refs[-1]
    loads = []
    for k, first in enumerate(firsts):
        out = refs[count_in + k]
        source = refs[k].at[:, pl.ds(first, out.shape[1])]
        loads.append(pltpu.make_async_copy(source, out, sem.at[k]))
        loads[-1].start()
    for load in loads:
        load.wait()


def cut(blocks, firsts, rows, after):
    out = jax.ShapeDtypeStruct((2, rows, D), jnp.bfloat16)
    operands = list(blocks) + list(after)
    return pl.pallas_call(
        functools.partial(cut_kernel, firsts, len(operands)),
        out_shape=[out] * len(blocks),
        in_specs=[ANY] * len(operands),
        out_specs=[INSIDE] * len(blocks),
        scratch_shapes=[pltpu.SemaphoreType.DMA((len(blocks),))],
        compiler_params=vmem(8),
        cost_estimate=cost(0, 8 * rows * D * len(blocks)),
    )(*operands)


def hidden_kernel(jobs, sizes, pieces, skipped, kept, tile, both, *refs):
    arrays = refs[: len(pieces)]
    blocks = refs[len(pieces) : len(pieces) + len(sizes)]
    refs = refs[len(pieces) + len(sizes) + skipped :]
    weights, tokens, pair, weight_sem, token_sem, out_sem, keep_sem = refs[-7:]
    top, total = weights.shape[1], tokens.shape[1]
    loads = []
    for k, (ref, (which, first, rows)) in enumerate(zip(arrays, pieces)):
        target = weights.at[:, pl.ds(first, rows)]
        if which is not None:
            target = weights.at[which, pl.ds(first, rows)]
        loads.append(pltpu.make_async_copy(ref, target, weight_sem.at[k]))
    first = 0
    for k, (ref, count) in enumerate(zip(blocks, sizes)):
        loads.append(pltpu.make_async_copy(ref, tokens.at[:, pl.ds(first, count)], token_sem.at[k]))
        first += count
    for load in loads:
        load.start()
    for load in loads:
        load.wait()
    stores = []
    if kept is not None:
        source = tokens.at[:, pl.ds(0, kept[1])]
        target = refs[2].at[:, pl.ds(kept[0], kept[1])]
        stores.append(pltpu.make_async_copy(source, target, keep_sem.at[0]))
        stores[-1].start()

    def step(i, carry):
        blocks = top // HELD
        here = i < blocks * both
        row = jnp.where(here, i % blocks, blocks - 1) * HELD
        token = jnp.where(here, i // blocks, i - (blocks - 1) * both) * tile
        rows = pl.ds(pl.multiple_of(row, HELD), HELD)
        at = pl.ds(pl.multiple_of(token, tile), tile)
        pre = up_scale * lax.dot_general(
            weights[0, rows], tokens[0, at], contract_last, preferred_element_type=jnp.float32
        )
        back = down_scale * lax.dot_general(
            weights[1, rows], tokens[1, at], contract_last, preferred_element_type=jnp.float32
        )
        value, slope = gelu_pair(pre)
        pair[0, rows, at] = (back * slope).astype(jnp.bfloat16)
        pair[1, rows, at] = value.astype(jnp.bfloat16)
        return carry

    lax.fori_loop(0, top // HELD * both + (total // tile - both), step, 0)
    for k, (shared, token, count, place) in enumerate(jobs):
        stores.append(
            pltpu.make_async_copy(
                pair.at[:, pl.ds(shared * HELD, HELD), pl.ds(token, count)],
                refs[shared].at[:, :, pl.ds(place, count)],
                out_sem.at[k],
            )
        )
        stores[-1].start()
    for store in stores:
        store.wait()


def hidden_step(jobs, pieces, arrays, blocks, results, kept, both, after=()):
    sizes = tuple(b.shape[1] for b in blocks)
    total = sum(sizes)
    top = max(first + rows for _, first, rows in pieces)
    shapes = ((2, HELD, EARLY), (2, HELD, TOKENS), (2, TOKENS, D))
    out = [jax.ShapeDtypeStruct(shape, jnp.bfloat16) for shape in shapes]
    operands = [*arrays, *blocks]
    aliases = {len(operands) + k: k for k in range(len(results))}
    operands += [*results, *after]
    flops = sum(4 * HELD * count * D for _, _, count, _ in jobs)
    skipped = len(results) + len(after)
    return pl.pallas_call(
        functools.partial(hidden_kernel, jobs, sizes, pieces, skipped, kept, 512, both),
        out_shape=out,
        in_specs=[ANY] * len(operands),
        out_specs=[ANY] * 3,
        input_output_aliases=aliases,
        scratch_shapes=[
            pltpu.VMEM((2, top, D), jnp.bfloat16),
            pltpu.VMEM((2, total, D), jnp.bfloat16),
            pltpu.VMEM((2, top, total), jnp.bfloat16),
            pltpu.SemaphoreType.DMA((len(pieces),)),
            pltpu.SemaphoreType.DMA((len(blocks),)),
            pltpu.SemaphoreType.DMA((len(jobs),)),
            pltpu.SemaphoreType.DMA((1,)),
        ],
        compiler_params=vmem(30 if len(jobs) > 1 else 16),
        cost_estimate=cost(flops, 4 * (total + top) * D + 4 * top * total),
    )(*operands)


def own_first_kernel(up, down, tokens_in, pair_in, *refs):
    out, pair, weights, tokens, columns, early, grads, sem = refs[-8:]
    width = FIRST_OWN * WIDTH
    loads = [
        pltpu.make_async_copy(up, weights.at[0], sem.at[0]),
        pltpu.make_async_copy(down, weights.at[1], sem.at[1]),
        pltpu.make_async_copy(tokens_in.at[:, pl.ds(EARLY, TOKENS - EARLY)], tokens, sem.at[2]),
        pltpu.make_async_copy(
            tokens_in.at[:, pl.ds(0, EARLY), pl.ds(0, width)], columns, sem.at[3]
        ),
        pltpu.make_async_copy(pair_in, early, sem.at[4]),
    ]
    for load in loads:
        load.start()
    for load in loads[:3]:
        load.wait()
    tile = 256

    def step(i, carry):
        at = pl.ds(pl.multiple_of(i * tile, tile), tile)
        pre = up_scale * lax.dot_general(
            weights[0], tokens[0, at], contract_last, preferred_element_type=jnp.float32
        )
        back = down_scale * lax.dot_general(
            weights[1], tokens[1, at], contract_last, preferred_element_type=jnp.float32
        )
        value, slope = gelu_pair(pre)
        pair[0, :, at] = (back * slope).astype(jnp.bfloat16)
        pair[1, :, at] = value.astype(jnp.bfloat16)
        return carry

    lax.fori_loop(0, (TOKENS - EARLY) // tile, step, 0)
    for load in loads[3:]:
        load.wait()

    def multiply(i, carry):
        which, k = i % 2, i // 2
        at = pl.ds(pl.multiple_of(k * WIDTH, WIDTH), WIDTH)
        grads[...] = jnp.dot(
            early[which], columns[which, :, at], preferred_element_type=jnp.float32
        )
        out[k, which] = grads[...] + jnp.dot(
            pair[which], tokens[which, :, at], preferred_element_type=jnp.float32
        )
        return carry

    lax.fori_loop(0, 2 * FIRST_OWN, multiply, 0)


def own_first(up, down, tokens, pair, after):
    rest = TOKENS - EARLY
    return pl.pallas_call(
        own_first_kernel,
        out_shape=[
            jax.ShapeDtypeStruct((FIRST_OWN, 2, HELD, WIDTH), jnp.float32),
            jax.ShapeDtypeStruct((2, HELD, rest), jnp.bfloat16),
        ],
        in_specs=[ANY] * (4 + len(after)),
        out_specs=[INSIDE] * 2,
        scratch_shapes=[
            pltpu.VMEM((2, HELD, D), jnp.bfloat16),
            pltpu.VMEM((2, rest, D), jnp.bfloat16),
            pltpu.VMEM((2, EARLY, FIRST_OWN * WIDTH), jnp.bfloat16),
            pltpu.VMEM((2, HELD, EARLY), jnp.bfloat16),
            pltpu.VMEM((HELD, WIDTH), jnp.float32),
            pltpu.SemaphoreType.DMA((5,)),
        ],
        compiler_params=vmem(20),
        cost_estimate=cost(4 * HELD * (rest * D + TOKENS * FIRST_OWN * WIDTH), 4 * (HELD + rest) * D),
    )(up, down, tokens, pair, *after)


def own_rest_kernel(pair, pair_last, tokens, out, grads):
    def multiply(which, carry):
        grads[...] = jnp.dot(pair[which], tokens[which, :EARLY], preferred_element_type=jnp.float32)
        out[0, which] = grads[...] + jnp.dot(
            pair_last[which], tokens[which, EARLY:], preferred_element_type=jnp.float32
        )
        return carry

    lax.fori_loop(0, 2, multiply, 0)


def own_rest(first, count, pair, pair_last, tokens, after):
    def kernel(*refs):
        own_rest_kernel(*refs[:3], *refs[-2:])

    return pl.pallas_call(
        kernel,
        out_shape=jax.ShapeDtypeStruct((count, 2, HELD, WIDTH), jnp.float32),
        grid=(count,),
        in_specs=[
            rows_spec(EARLY),
            rows_spec(TOKENS - EARLY),
            pl.BlockSpec((2, TOKENS, WIDTH), lambda j: (0, 0, j + first)),
        ]
        + [ANY] * len(after),
        out_specs=pl.BlockSpec((1, 2, HELD, WIDTH), lambda j: (j, 0, 0, 0)),
        scratch_shapes=[pltpu.VMEM((HELD, WIDTH), jnp.float32)],
        compiler_params=vmem(18),
        cost_estimate=cost(4 * HELD * TOKENS * count * WIDTH, 4 * TOKENS * (HELD + count * WIDTH)),
    )(pair, pair_last, tokens, *after)


def last_shared_kernel(*refs):
    weights_in, blocks = refs[0], refs[1:5]
    pair_in, tokens_in, pair_out, tokens_out, chunk = refs[5:10]
    weights, tokens, pair, columns, sem, out_sem = refs[10:]
    first, width = 0, WIDTH
    rest = TOKENS - EARLY
    weights_load = pltpu.make_async_copy(weights_in, weights, sem.at[0])
    loads, row = [], 0
    for k, ref in enumerate(blocks):
        rows = ref.shape[1]
        loads.append(pltpu.make_async_copy(ref, tokens.at[:, pl.ds(row, rows)], sem.at[1 + k]))
        row += rows
    early, late = pl.ds(0, EARLY), pl.ds(EARLY, rest)
    source = tokens_in.at[:, early, pl.ds(first, width)]
    more = [
        pltpu.make_async_copy(pair_in.at[:, :, early], pair.at[:, :, early], sem.at[5]),
        pltpu.make_async_copy(source, columns, sem.at[6]),
    ]
    for load in [*loads[:2], weights_load, *loads[2:], *more]:
        load.start()
    weights_load.wait()
    tile = 256

    def step(i, carry):
        at = pl.ds(pl.multiple_of(i * tile, tile), tile)
        to = pl.ds(pl.multiple_of(EARLY + i * tile, tile), tile)
        pre = up_scale * lax.dot_general(
            weights[0], tokens[0, at], contract_last, preferred_element_type=jnp.float32
        )
        back = down_scale * lax.dot_general(
            weights[1], tokens[1, at], contract_last, preferred_element_type=jnp.float32
        )
        value, slope = gelu_pair(pre)
        pair[0, :, to] = (back * slope).astype(jnp.bfloat16)
        pair[1, :, to] = value.astype(jnp.bfloat16)
        return carry

    def arriving(i, carry):
        for parity in (0, 1):

            @pl.when(i == parity)
            def _(parity=parity):
                for load in loads[2 * parity : 2 * parity + 2]:
                    load.wait()

        return step(i, carry)

    lax.fori_loop(0, rest // tile, arriving, 0)
    stores = [pltpu.make_async_copy(tokens, tokens_out.at[:, late], out_sem.at[0])]
    stores[0].start()
    stores.append(pltpu.make_async_copy(pair.at[:, :, late], pair_out.at[:, :, late], out_sem.at[1]))
    stores[1].start()
    for load in more:
        load.wait()
    for which, scale in enumerate((up_scale, down_scale)):
        grad = jnp.dot(pair[which, :, :EARLY], columns[which], preferred_element_type=jnp.float32)
        grad += jnp.dot(
            pair[which, :, EARLY:],
            tokens[which, :, first : first + width],
            preferred_element_type=jnp.float32,
        )
        chunk[which] = (scale * grad).astype(jnp.bfloat16)
    for store in stores:
        store.wait()


def last_shared(weights, blocks, pair, tokens):
    width = WIDTH
    return pl.pallas_call(
        last_shared_kernel,
        out_shape=[
            jax.ShapeDtypeStruct((2, HELD, TOKENS), jnp.bfloat16),
            jax.ShapeDtypeStruct((2, TOKENS, D), jnp.bfloat16),
            jax.ShapeDtypeStruct((2, HELD, width), jnp.bfloat16),
        ],
        in_specs=[ANY] * 7,
        out_specs=[ANY] * 2 + [INSIDE],
        input_output_aliases={5: 0, 6: 1},
        scratch_shapes=[
            pltpu.VMEM((2, HELD, D), jnp.bfloat16),
            pltpu.VMEM((2, TOKENS - EARLY, D), jnp.bfloat16),
            pltpu.VMEM((2, HELD, TOKENS), jnp.bfloat16),
            pltpu.VMEM((2, EARLY, width), jnp.bfloat16),
            pltpu.SemaphoreType.DMA((7,)),
            pltpu.SemaphoreType.DMA((2,)),
        ],
        compiler_params=vmem(16),
        cost_estimate=cost(
            4 * HELD * ((TOKENS - EARLY) * D + TOKENS * width), 4 * (HELD + TOKENS - EARLY) * D
        ),
    )(weights, *blocks, pair, tokens)


def column_spec(c):
    first, width = CHUNKS[c]
    return pl.BlockSpec((HELD, width), lambda j: (0, first // width))


def pair_spec(c):
    return pl.BlockSpec((2, HELD, CHUNKS[c][1]), lambda j: (0, 0, 0))


def rows_spec(tokens):
    return pl.BlockSpec((2, HELD, tokens), lambda j: (0, 0, 0))


def theirs_kernel(targets, skipped, pair, tokens, *refs):
    outs = refs[skipped : skipped + len(targets)]
    held, sem = refs[-2:]
    j = pl.program_id(0)
    slot = j % 2

    def copy(k):
        block, first, width = targets[k]
        source = held.at[block % 2, :, :, pl.ds(first, width)]
        return pltpu.make_async_copy(source, outs[k], sem.at[k])

    for k, (block, _, _) in enumerate(targets):

        @pl.when(j == block + 2)
        def _(k=k):
            copy(k).wait()

    def multiply(which, carry):
        scale = jnp.where(which == 0, up_scale, down_scale)
        grad = jnp.dot(pair[which], tokens[which], preferred_element_type=jnp.float32)
        held[slot, which] = (scale * grad).astype(jnp.bfloat16)
        return carry

    lax.fori_loop(0, 2, multiply, 0)
    blocks = targets[-1][0] + 1
    for k, (block, _, _) in enumerate(targets):

        @pl.when(j == block)
        def _(k=k):
            copy(k).start()

    @pl.when(j == blocks - 1)
    def _():
        for k, (block, _, _) in enumerate(targets):
            if block >= blocks - 2:
                copy(k).wait()


def theirs_chunks(first, count, pair, tokens, after):
    targets = tuple(
        (column // WIDTH - first, column % WIDTH, width)
        for column, width in CHUNKS
        if first <= column // WIDTH < first + count
    )
    return pl.pallas_call(
        functools.partial(theirs_kernel, targets, len(after)),
        out_shape=[jax.ShapeDtypeStruct((2, HELD, w), jnp.bfloat16) for _, _, w in targets],
        grid=(count,),
        in_specs=[rows_spec(TOKENS), pl.BlockSpec((2, TOKENS, WIDTH), lambda j: (0, 0, j + first))]
        + [ANY] * len(after),
        out_specs=[ANY] * len(targets),
        scratch_shapes=[
            pltpu.VMEM((2, 2, HELD, WIDTH), jnp.bfloat16),
            pltpu.SemaphoreType.DMA((len(targets),)),
        ],
        compiler_params=vmem(16),
        cost_estimate=cost(4 * HELD * TOKENS * count * WIDTH, 4 * TOKENS * (HELD + count * WIDTH)),
    )(pair, tokens, *after)


def adam_kernel(mixing, *refs):
    own, bias, arrived = refs[:3]
    state = refs[3:9]
    outs = refs[-7 - mixing[1] :]
    tile = 32

    def step(i, carry):
        at = pl.ds(pl.multiple_of(i * tile, tile), tile)
        for which in (0, 1):
            weight, first, second = (ref[at] for ref in state[3 * which : 3 * which + 3])
            scale = (up_scale, down_scale)[which]
            grad = scale * own[0, which, at] + arrived[which, at].astype(jnp.float32)
            first_new = beta_one * first.astype(jnp.float32) + (1.0 - beta_one) * grad
            second_new = beta_two * second.astype(jnp.float32) + (1.0 - beta_two) * grad * grad
            update = (learn_rate * bias[0]) * first_new / (jnp.sqrt(second_new * bias[1]) + adam_eps)
            outs[0][which, at] = (weight.astype(jnp.float32) - update).astype(jnp.bfloat16)
            outs[1 + 2 * which][at] = first_new.astype(jnp.bfloat16)
            outs[2 + 2 * which][at] = second_new.astype(jnp.bfloat16)
            if mixing[0]:
                both = refs[9][which, at].astype(jnp.float32) + refs[10][which, at].astype(jnp.float32)
                outs[5 + which][at] = (both * 0.5).astype(jnp.bfloat16)
        return carry

    lax.fori_loop(0, HELD // tile, step, 0)


def mix_kernel(own, other, *refs):
    tile = 32

    def step(i, carry):
        at = pl.ds(pl.multiple_of(i * tile, tile), tile)
        for which in (0, 1):
            both = own[which, at].astype(jnp.float32) + other[which, at].astype(jnp.float32)
            refs[which - 2][at] = (both * 0.5).astype(jnp.bfloat16)
        return carry

    lax.fori_loop(0, HELD // tile, step, 0)


whole = jax.ShapeDtypeStruct((HELD, D), jnp.bfloat16)


def adam_chunk(c, own, bias, arrived, state, mixed, results, passing):
    operands = [own[0], bias, arrived, *state, *mixed]
    aliases = {len(operands) + k: 1 + k for k in range(len(results))}
    operands += results
    if passing:
        aliases[len(operands)] = 7
        operands += passing
    before = max(c - 2, 0)
    mixing = [column_spec(before)] * 2 if mixed or not results else [ANY] * 2
    (first, width), place = CHUNKS[c], own[1]
    block, half = (1, 2, HELD, width), first % WIDTH // width
    smem = pl.BlockSpec(memory_space=pltpu.SMEM)
    pair = jax.ShapeDtypeStruct((2, HELD, width), jnp.bfloat16)
    handed = [jax.ShapeDtypeStruct(p.shape, p.dtype) for p in passing]
    return pl.pallas_call(
        functools.partial(adam_kernel, (bool(mixed), len(passing))),
        out_shape=[pair] + [whole] * 6 + handed,
        grid=(1,),
        in_specs=[pl.BlockSpec(block, lambda j: (place, 0, 0, half)), smem, pair_spec(c)]
        + [column_spec(c)] * 6
        + [pair_spec(before)] * len(mixed)
        + [ANY] * (len(results) + len(passing)),
        out_specs=[pair_spec(c)] + [column_spec(c)] * 4 + mixing + [ANY] * len(passing),
        input_output_aliases=aliases,
        compiler_params=vmem(12),
        cost_estimate=cost(0, 60 * HELD * WIDTH),
    )(*operands)


def mix_chunk(c, own, other, results):
    return pl.pallas_call(
        mix_kernel,
        out_shape=[whole] * 2,
        grid=(1,),
        in_specs=[pair_spec(c)] * 2 + [ANY] * 2,
        out_specs=[column_spec(c)] * 2,
        input_output_aliases={2: 0, 3: 1},
        compiler_params=vmem(8),
        cost_estimate=cost(0, 12 * HELD * WIDTH),
    )(own, other, *results)


def on_device(
    inputs,
    cotangent,
    up_weight,
    down_weight,
    momentum_up,
    momentum_down,
    variance_up,
    variance_down,
    step_index,
):
    up, down = up_weight[0], down_weight[0]
    half = ROWS // 2

    weights_sent = moved(stack_weights(up, down), y_sharing)
    a, b = prepare(inputs[0], cotangent[0])
    a_x, a_y = moved(a, x_other), moved(a, y_same_half)
    b_up, b_down = moved(b, z_up), moved(b, z_down)
    quarter = half // 2
    a_far = [moved(a_x[:, :quarter], y_same_half), moved(a_y[:, quarter:], x_other)]
    b_far = [moved(b_up[:, :quarter], z_up), moved(b_down[:, quarter:], z_down)]
    a_all = join([a, a_x, a_y, *a_far], [])
    b_all = join([b, b_up, b_down, *b_far], [])

    a_up, a_down = moved(a_all, z_up), moved(a_all, z_down)
    b_x, b_y = moved(b_all, x_other), moved(b_all, y_same_half)
    held = ((0, 0, HELD), (1, 0, HELD))
    job = (0, 0, 512, 0)
    results = hidden_step((job,), held, [up, down], [a_all, b_all], (), (0, 512), 1)

    mid = 2 * half
    halves = cut([a_up, a_down], (0, mid), mid, [results[0]])
    halves += cut([b_x, b_y], (0, mid), mid, [results[0]])
    last = [
        moved(halves[0], z_up),
        moved(halves[1], z_down),
        moved(halves[2], y_same_half),
        moved(halves[3], x_other),
    ]
    results = hidden_step(
        ((0, 0, 1024, 512), (1, 0, 1024, 512), (1, 1024, 512, 0)),
        held + ((None, HELD, HELD),),
        [up, down, weights_sent],
        [a_up, a_down, b_x, b_y, a_all, b_all],
        results,
        (512, 1024),
        2,
        halves[::2],
    )
    own_pair = results[0]
    pair, tokens, theirs = last_shared(weights_sent, last, *results[1:])

    count = step_index[0].astype(jnp.float32)
    bias_one = 1.0 - jnp.exp(count * math.log(beta_one))
    bias_two = 1.0 - jnp.exp(count * math.log(beta_two))
    bias = jnp.stack([1.0 / bias_one, 1.0 / bias_two])
    state = [up, momentum_up[0], variance_up[0], down, momentum_down[0], variance_down[0]]

    def finish(hop):
        route = [(g, (g + hop) % 4) for g in range(4)]
        news, updated, others = (), [], []
        more = [theirs, *theirs_chunks(1, 2, pair, tokens, [])]
        sent = [moved(t, y_sharing) for t in more[:2]]
        own, last_pair = own_first(up, down, tokens, own_pair, more[1:2])
        place = [(own, k) for k in range(FIRST_OWN)]
        for c in range(len(CHUNKS)):
            mixed = [updated[c - 2], others[c - 2]] if 2 <= c < MIXING else []
            passing = more[c + 2 : c + 3]
            block = place[CHUNKS[c][0] // WIDTH]
            out = adam_chunk(c, block, bias, sent[c], state, mixed, news, passing)
            updated.append(out[0])
            news = out[1:7]
            others.append(lax.ppermute(out[0], "rep", route))
            if passing:
                sent.append(moved(out[7], y_sharing))
            for after, first, count in THEIRS_LATER:
                if c == after:
                    more += theirs_chunks(first, count, pair, tokens, [out[0]])
            for after, first, count in OWN_LATER:
                if c == after:
                    own = own_rest(first, count, own_pair, last_pair, tokens, [out[0]])
                    place += [(own, k) for k in range(count)]
        mixed = news[4:]
        for c in range(MIXING - 2, len(CHUNKS)):
            mixed = mix_chunk(c, updated[c], others[c], mixed)
        return mixed[0], mixed[1], news[0], news[2], news[1], news[3]

    outs = lax.cond(step_index[0] % 2 == 0, lambda: finish(1), lambda: finish(2))
    return tuple(o[None] for o in outs)


def solution(mesh):
    shard = P("rep", "fsdp", None)
    return jax.shard_map(
        on_device,
        mesh=mesh,
        in_specs=(shard,) * 8 + (P(),),
        out_specs=(shard,) * 6,
        check_vma=False,
    )
```

```python
import functools
import math

import jax
import jax.numpy as jnp
from jax import lax
from jax.experimental import pallas as pl
from jax.experimental.pallas import tpu as pltpu
from jax.sharding import PartitionSpec as P

D = 1792
FF = 14336

beta_one = 0.9
beta_two = 0.95
learn_rate = 0.05
adam_eps = 1e-08
norm_eps = 1e-06
root_coef = math.sqrt(2.0 / math.pi)
up_scale = 1.0 / math.sqrt(D)
down_scale = 1.0 / math.sqrt(FF)

ROWS = 128
HELD = 448
SHARED = 2 * HELD
TOKENS = 2048
WIDTH = 256
BLOCKS = D // WIDTH
CHUNKS = tuple((WIDTH * k, WIDTH) for k in range(BLOCKS - 1)) + ((D - 256, 128), (D - 128, 128))
FIRST_OWN = 2
OWN_LATER = ((1, 2, 2), (2, 4, 3))
THEIRS_LATER = ((0, 3, 2), (2, 5, 2))
MIXING = 7
EARLY = 1536
NZ, NX, NY = 4, 2, 4


def moved(block, place):
    route = []
    for z in range(NZ):
        for x in range(NX):
            for y in range(NY):
                a, b, c = place(z, x, y)
                route.append(((z * NX + x) * NY + y, (a % NZ * NX + b) * NY + c))
    return lax.ppermute(block, "fsdp", route)


def z_up(z, x, y):
    return z + 1, x, y


def z_down(z, x, y):
    return z - 1, x, y


def z_over(z, x, y):
    return z + 2, x, y


def x_other(z, x, y):
    return z, 1 - x, y


def y_same_half(z, x, y):
    return z, x, 3 - y


def diagonal(z, x, y):
    return z, 1 - x, 3 - y


def y_sharing(z, x, y):
    return z, x, y ^ 1


def gelu_pair(pre):
    square = pre * pre
    tangent = jnp.tanh(pre * (root_coef + (root_coef * 0.044715) * square))
    half = 0.5 * tangent + 0.5
    value = pre * half
    slope = half + pre * (0.5 - 0.5 * tangent * tangent) * (
        root_coef + (3.0 * 0.044715 * root_coef) * square
    )
    return (value, slope)


def normalize(rows):
    wide = rows.astype(jnp.float32)
    factor = lax.rsqrt(jnp.mean(wide * wide, axis=-1, keepdims=True) + norm_eps)
    return (wide * factor).astype(jnp.bfloat16)


contract_last = (((1,), (1,)), ((), ()))
ANY = pl.BlockSpec(memory_space=pl.ANY)
INSIDE = pl.BlockSpec(memory_space=pltpu.VMEM)


def vmem(mebibytes):
    return pltpu.CompilerParams(vmem_limit_bytes=mebibytes * 1024 * 1024)


def cost(flops, moved_bytes):
    return pl.CostEstimate(flops=2 * flops, bytes_accessed=moved_bytes, transcendentals=0)


def prepare_kernel(inputs, cotangent, a_ref, b_ref, held, sem):
    half = ROWS // 2
    loads = [
        pltpu.make_async_copy(inputs, held, sem.at[0]),
        pltpu.make_async_copy(cotangent.at[pl.ds(0, half)], a_ref.at[1], sem.at[1]),
        pltpu.make_async_copy(cotangent.at[pl.ds(half, half)], b_ref.at[1], sem.at[2]),
    ]
    for load in loads:
        load.start()
    loads[0].wait()
    a_ref[0] = normalize(held[:half])
    b_ref[0] = normalize(held[half:])
    for load in loads[1:]:
        load.wait()


def prepare(inputs, cotangent):
    half = jax.ShapeDtypeStruct((2, ROWS // 2, D), jnp.bfloat16)
    return pl.pallas_call(
        prepare_kernel,
        out_shape=[half, half],
        in_specs=[ANY] * 2,
        out_specs=[INSIDE] * 2,
        scratch_shapes=[pltpu.VMEM((ROWS, D), jnp.bfloat16), pltpu.SemaphoreType.DMA((3,))],
        compiler_params=vmem(8),
        cost_estimate=cost(0, 8 * ROWS * D),
    )(inputs, cotangent)


def stack_kernel(up, down, out, held, load_sem, store_sem):
    parts = 2
    rows = HELD // parts
    loads, stores = [], []
    for which, ref in enumerate((up, down)):
        for part in range(parts):
            k, at = which * parts + part, pl.ds(part * rows, rows)
            place = held.at[which, at]
            loads.append(pltpu.make_async_copy(ref.at[at], place, load_sem.at[k]))
            stores.append(pltpu.make_async_copy(place, out.at[which, at], store_sem.at[k]))
    for load in loads:
        load.start()
    for load, store in zip(loads, stores):
        load.wait()
        store.start()
    for store in stores:
        store.wait()


def stack_weights(up, down):
    shape = (2, HELD, D)
    return pl.pallas_call(
        stack_kernel,
        out_shape=jax.ShapeDtypeStruct(shape, jnp.bfloat16),
        in_specs=[ANY] * 2,
        out_specs=ANY,
        scratch_shapes=[pltpu.VMEM(shape, jnp.bfloat16)] + [pltpu.SemaphoreType.DMA((4,))] * 2,
        compiler_params=vmem(8),
        cost_estimate=cost(0, 8 * HELD * D),
    )(up, down)


def join_kernel(count, *refs):
    first = 0
    for ref in refs[:count]:
        rows = ref.shape[1]
        refs[-1][:, first : first + rows] = ref[...]
        first += rows


def join(pieces, after):
    rows = sum(p.shape[1] for p in pieces)
    return pl.pallas_call(
        functools.partial(join_kernel, len(pieces)),
        out_shape=jax.ShapeDtypeStruct((2, rows, D), jnp.bfloat16),
        in_specs=[INSIDE] * len(pieces) + [ANY] * len(after),
        out_specs=INSIDE,
        compiler_params=vmem(8),
        cost_estimate=cost(0, 8 * rows * D),
    )(*pieces, *after)


def cut_kernel(firsts, count_in, *refs):
    sem = refs[-1]
    loads = []
    for k, first in enumerate(firsts):
        out = refs[count_in + k]
        source = refs[k].at[:, pl.ds(first, out.shape[1])]
        loads.append(pltpu.make_async_copy(source, out, sem.at[k]))
        loads[-1].start()
    for load in loads:
        load.wait()


def cut(blocks, firsts, rows, after):
    out = jax.ShapeDtypeStruct((2, rows, D), jnp.bfloat16)
    operands = list(blocks) + list(after)
    return pl.pallas_call(
        functools.partial(cut_kernel, firsts, len(operands)),
        out_shape=[out] * len(blocks),
        in_specs=[ANY] * len(operands),
        out_specs=[INSIDE] * len(blocks),
        scratch_shapes=[pltpu.SemaphoreType.DMA((len(blocks),))],
        compiler_params=vmem(8),
        cost_estimate=cost(0, 8 * rows * D * len(blocks)),
    )(*operands)


def hidden_kernel(jobs, sizes, pieces, skipped, kept, tile, both, chunk, *refs):
    arrays = refs[: len(pieces)]
    blocks = refs[len(pieces) : len(pieces) + len(sizes)]
    refs = refs[len(pieces) + len(sizes) + skipped :]
    weights, tokens, pair, weight_sem, token_sem, out_sem, keep_sem = refs[-7:]
    top, total = weights.shape[1], tokens.shape[1]
    loads = []
    for k, (ref, (which, first, rows)) in enumerate(zip(arrays, pieces)):
        target = weights.at[:, pl.ds(first, rows)]
        if which is not None:
            target = weights.at[which, pl.ds(first, rows)]
        loads.append(pltpu.make_async_copy(ref, target, weight_sem.at[k]))
    first, arriving = 0, {}
    for k, (ref, count) in enumerate(zip(blocks, sizes)):
        load = pltpu.make_async_copy(ref, tokens.at[:, pl.ds(first, count)], token_sem.at[k])
        at = first // tile
        at = at * (top // HELD) if at < both else at + (top // HELD - 1) * both
        arriving.setdefault(at, []).append(load)
        first += count
    for load in [*arriving[0], *loads, *sum((l for at, l in arriving.items() if at), [])]:
        load.start()
    for load in loads:
        load.wait()
    stores = []

    def step(i, carry):
        for at, expected in arriving.items():

            @pl.when(i == at)
            def _(expected=expected):
                for load in expected:
                    load.wait()

        blocks = top // HELD
        here = i < blocks * both
        row = jnp.where(here, i % blocks, blocks - 1) * HELD
        token = jnp.where(here, i // blocks, i - (blocks - 1) * both) * tile
        rows = pl.ds(pl.multiple_of(row, HELD), HELD)
        at = pl.ds(pl.multiple_of(token, tile), tile)
        pre = up_scale * lax.dot_general(
            weights[0, rows], tokens[0, at], contract_last, preferred_element_type=jnp.float32
        )
        back = down_scale * lax.dot_general(
            weights[1, rows], tokens[1, at], contract_last, preferred_element_type=jnp.float32
        )
        value, slope = gelu_pair(pre)
        pair[0, rows, at] = (back * slope).astype(jnp.bfloat16)
        pair[1, rows, at] = value.astype(jnp.bfloat16)
        return carry

    lax.fori_loop(0, top // HELD * both + (total // tile - both), step, 0)
    for k, (shared, token, count, place) in enumerate(jobs):
        stores.append(
            pltpu.make_async_copy(
                pair.at[:, pl.ds(shared * HELD, HELD), pl.ds(token, count)],
                refs[shared].at[:, :, pl.ds(place, count)],
                out_sem.at[k],
            )
        )
        stores[-1].start()
    if kept is not None:
        source = tokens.at[:, pl.ds(0, kept[1])]
        target = refs[2].at[:, pl.ds(kept[0], kept[1])]
        stores.append(pltpu.make_async_copy(source, target, keep_sem.at[0]))
        stores[-1].start()
    if chunk:

        def multiply(which, carry):
            refs[3][which] = jnp.dot(
                pair[which, HELD:], tokens[which, :, :WIDTH], preferred_element_type=jnp.float32
            )
            return carry

        lax.fori_loop(0, 2, multiply, 0)
    for store in stores:
        store.wait()


def hidden_step(jobs, pieces, arrays, blocks, results, kept, both, after=(), chunk=False):
    sizes = tuple(b.shape[1] for b in blocks)
    total = sum(sizes)
    top = max(first + rows for _, first, rows in pieces)
    shapes = ((2, HELD, EARLY), (2, HELD, TOKENS), (2, TOKENS, D))
    out = [jax.ShapeDtypeStruct(shape, jnp.bfloat16) for shape in shapes]
    out += [jax.ShapeDtypeStruct((2, HELD, WIDTH), jnp.float32)] * chunk
    operands = [*arrays, *blocks]
    aliases = {len(operands) + k: k for k in range(len(results))}
    operands += [*results, *after]
    flops = sum(4 * HELD * count * D for _, _, count, _ in jobs)
    skipped = len(results) + len(after)
    return pl.pallas_call(
        functools.partial(hidden_kernel, jobs, sizes, pieces, skipped, kept, 512, both, chunk),
        out_shape=out,
        in_specs=[ANY] * len(operands),
        out_specs=[ANY] * 3 + [INSIDE] * chunk,
        input_output_aliases=aliases,
        scratch_shapes=[
            pltpu.VMEM((2, top, D), jnp.bfloat16),
            pltpu.VMEM((2, total, D), jnp.bfloat16),
            pltpu.VMEM((2, top, total), jnp.bfloat16),
            pltpu.SemaphoreType.DMA((len(pieces),)),
            pltpu.SemaphoreType.DMA((len(blocks),)),
            pltpu.SemaphoreType.DMA((len(jobs),)),
            pltpu.SemaphoreType.DMA((1,)),
        ],
        compiler_params=vmem(30 if len(jobs) > 1 else 16),
        cost_estimate=cost(flops, 4 * (total + top) * D + 4 * top * total),
    )(*operands)


def own_first_kernel(up, down, tokens_in, pair_in, *refs):
    out, pair, weights, tokens, columns, early, grads, sem = refs[-8:]
    width = FIRST_OWN * WIDTH
    loads = [
        pltpu.make_async_copy(up, weights.at[0], sem.at[0]),
        pltpu.make_async_copy(down, weights.at[1], sem.at[1]),
        pltpu.make_async_copy(tokens_in.at[:, pl.ds(EARLY, TOKENS - EARLY)], tokens, sem.at[2]),
        pltpu.make_async_copy(
            tokens_in.at[:, pl.ds(0, EARLY), pl.ds(0, width)], columns, sem.at[3]
        ),
        pltpu.make_async_copy(pair_in, early, sem.at[4]),
    ]
    for load in loads:
        load.start()
    for load in loads[:3]:
        load.wait()
    tile = 256

    def step(i, carry):
        at = pl.ds(pl.multiple_of(i * tile, tile), tile)
        pre = up_scale * lax.dot_general(
            weights[0], tokens[0, at], contract_last, preferred_element_type=jnp.float32
        )
        back = down_scale * lax.dot_general(
            weights[1], tokens[1, at], contract_last, preferred_element_type=jnp.float32
        )
        value, slope = gelu_pair(pre)
        pair[0, :, at] = (back * slope).astype(jnp.bfloat16)
        pair[1, :, at] = value.astype(jnp.bfloat16)
        return carry

    lax.fori_loop(0, (TOKENS - EARLY) // tile, step, 0)
    for load in loads[3:]:
        load.wait()

    def multiply(i, carry):
        which, k = i % 2, i // 2
        at = pl.ds(pl.multiple_of(k * WIDTH, WIDTH), WIDTH)
        grads[...] = jnp.dot(
            early[which], columns[which, :, at], preferred_element_type=jnp.float32
        )
        out[k, which] = grads[...] + jnp.dot(
            pair[which], tokens[which, :, at], preferred_element_type=jnp.float32
        )
        return carry

    lax.fori_loop(0, 2 * FIRST_OWN, multiply, 0)


def own_first(up, down, tokens, pair, after):
    rest = TOKENS - EARLY
    return pl.pallas_call(
        own_first_kernel,
        out_shape=[
            jax.ShapeDtypeStruct((FIRST_OWN, 2, HELD, WIDTH), jnp.float32),
            jax.ShapeDtypeStruct((2, HELD, rest), jnp.bfloat16),
        ],
        in_specs=[ANY] * (4 + len(after)),
        out_specs=[INSIDE] * 2,
        scratch_shapes=[
            pltpu.VMEM((2, HELD, D), jnp.bfloat16),
            pltpu.VMEM((2, rest, D), jnp.bfloat16),
            pltpu.VMEM((2, EARLY, FIRST_OWN * WIDTH), jnp.bfloat16),
            pltpu.VMEM((2, HELD, EARLY), jnp.bfloat16),
            pltpu.VMEM((HELD, WIDTH), jnp.float32),
            pltpu.SemaphoreType.DMA((5,)),
        ],
        compiler_params=vmem(20),
        cost_estimate=cost(4 * HELD * (rest * D + TOKENS * FIRST_OWN * WIDTH), 4 * (HELD + rest) * D),
    )(up, down, tokens, pair, *after)


def own_rest_kernel(pair, pair_last, tokens, out, grads):
    def multiply(which, carry):
        grads[...] = jnp.dot(pair[which], tokens[which, :EARLY], preferred_element_type=jnp.float32)
        out[0, which] = grads[...] + jnp.dot(
            pair_last[which], tokens[which, EARLY:], preferred_element_type=jnp.float32
        )
        return carry

    lax.fori_loop(0, 2, multiply, 0)


def own_rest(first, count, pair, pair_last, tokens, after):
    def kernel(*refs):
        own_rest_kernel(*refs[:3], *refs[-2:])

    return pl.pallas_call(
        kernel,
        out_shape=jax.ShapeDtypeStruct((count, 2, HELD, WIDTH), jnp.float32),
        grid=(count,),
        in_specs=[
            rows_spec(EARLY),
            rows_spec(TOKENS - EARLY),
            pl.BlockSpec((2, TOKENS, WIDTH), lambda j: (0, 0, j + first)),
        ]
        + [ANY] * len(after),
        out_specs=pl.BlockSpec((1, 2, HELD, WIDTH), lambda j: (j, 0, 0, 0)),
        scratch_shapes=[pltpu.VMEM((HELD, WIDTH), jnp.float32)],
        compiler_params=vmem(18),
        cost_estimate=cost(4 * HELD * TOKENS * count * WIDTH, 4 * TOKENS * (HELD + count * WIDTH)),
    )(pair, pair_last, tokens, *after)


def last_shared_kernel(*refs):
    weights_in, blocks = refs[0], refs[1:5]
    partial, pair_out, tokens_out, chunk = refs[7:11]
    weights, tokens, pair, early, sem, out_sem = refs[11:]
    first, width = 0, WIDTH
    rest = TOKENS - EARLY
    weights_load = pltpu.make_async_copy(weights_in, weights, sem.at[0])
    loads, row = [], 0
    for k, ref in enumerate(blocks):
        rows = ref.shape[1]
        loads.append(pltpu.make_async_copy(ref, tokens.at[:, pl.ds(row, rows)], sem.at[1 + k]))
        row += rows
    late = pl.ds(EARLY, rest)
    more = [pltpu.make_async_copy(partial, early, sem.at[5])]
    for load in [*loads[:2], weights_load, *loads[2:], *more]:
        load.start()
    weights_load.wait()
    tile = 256

    def step(i, carry):
        at = pl.ds(pl.multiple_of(i * tile, tile), tile)
        pre = up_scale * lax.dot_general(
            weights[0], tokens[0, at], contract_last, preferred_element_type=jnp.float32
        )
        back = down_scale * lax.dot_general(
            weights[1], tokens[1, at], contract_last, preferred_element_type=jnp.float32
        )
        value, slope = gelu_pair(pre)
        pair[0, :, at] = (back * slope).astype(jnp.bfloat16)
        pair[1, :, at] = value.astype(jnp.bfloat16)
        return carry

    def arriving(i, carry):
        for parity in (0, 1):

            @pl.when(i == parity)
            def _(parity=parity):
                for load in loads[2 * parity : 2 * parity + 2]:
                    load.wait()

        return step(i, carry)

    lax.fori_loop(0, rest // tile, arriving, 0)
    stores = [pltpu.make_async_copy(tokens, tokens_out.at[:, late], out_sem.at[0])]
    stores[0].start()
    stores.append(pltpu.make_async_copy(pair, pair_out.at[:, :, late], out_sem.at[1]))
    stores[1].start()
    for load in more:
        load.wait()
    for which, scale in enumerate((up_scale, down_scale)):
        grad = early[which] + jnp.dot(
            pair[which],
            tokens[which, :, first : first + width],
            preferred_element_type=jnp.float32,
        )
        chunk[which] = (scale * grad).astype(jnp.bfloat16)
    for store in stores:
        store.wait()


def last_shared(weights, blocks, pair, tokens, partial):
    width = WIDTH
    return pl.pallas_call(
        last_shared_kernel,
        out_shape=[
            jax.ShapeDtypeStruct((2, HELD, TOKENS), jnp.bfloat16),
            jax.ShapeDtypeStruct((2, TOKENS, D), jnp.bfloat16),
            jax.ShapeDtypeStruct((2, HELD, width), jnp.bfloat16),
        ],
        in_specs=[ANY] * 8,
        out_specs=[ANY] * 2 + [INSIDE],
        input_output_aliases={5: 0, 6: 1},
        scratch_shapes=[
            pltpu.VMEM((2, HELD, D), jnp.bfloat16),
            pltpu.VMEM((2, TOKENS - EARLY, D), jnp.bfloat16),
            pltpu.VMEM((2, HELD, TOKENS - EARLY), jnp.bfloat16),
            pltpu.VMEM((2, HELD, width), jnp.float32),
            pltpu.SemaphoreType.DMA((6,)),
            pltpu.SemaphoreType.DMA((2,)),
        ],
        compiler_params=vmem(16),
        cost_estimate=cost(
            4 * HELD * ((TOKENS - EARLY) * D + TOKENS * width), 4 * (HELD + TOKENS - EARLY) * D
        ),
    )(weights, *blocks, pair, tokens, partial)


def column_spec(c):
    first, width = CHUNKS[c]
    return pl.BlockSpec((HELD, width), lambda j: (0, first // width))


def pair_spec(c):
    return pl.BlockSpec((2, HELD, CHUNKS[c][1]), lambda j: (0, 0, 0))


def rows_spec(tokens):
    return pl.BlockSpec((2, HELD, tokens), lambda j: (0, 0, 0))


def theirs_kernel(targets, skipped, pair, tokens, *refs):
    outs = refs[skipped : skipped + len(targets)]
    held, sem = refs[-2:]
    j = pl.program_id(0)
    slot = j % 2

    def copy(k):
        block, first, width = targets[k]
        source = held.at[block % 2, :, :, pl.ds(first, width)]
        return pltpu.make_async_copy(source, outs[k], sem.at[k])

    for k, (block, _, _) in enumerate(targets):

        @pl.when(j == block + 2)
        def _(k=k):
            copy(k).wait()

    def multiply(which, carry):
        scale = jnp.where(which == 0, up_scale, down_scale)
        grad = jnp.dot(pair[which], tokens[which], preferred_element_type=jnp.float32)
        held[slot, which] = (scale * grad).astype(jnp.bfloat16)
        return carry

    lax.fori_loop(0, 2, multiply, 0)
    blocks = targets[-1][0] + 1
    for k, (block, _, _) in enumerate(targets):

        @pl.when(j == block)
        def _(k=k):
            copy(k).start()

    @pl.when(j == blocks - 1)
    def _():
        for k, (block, _, _) in enumerate(targets):
            if block >= blocks - 2:
                copy(k).wait()


def theirs_chunks(first, count, pair, tokens, after):
    targets = tuple(
        (column // WIDTH - first, column % WIDTH, width)
        for column, width in CHUNKS
        if first <= column // WIDTH < first + count
    )
    return pl.pallas_call(
        functools.partial(theirs_kernel, targets, len(after)),
        out_shape=[jax.ShapeDtypeStruct((2, HELD, w), jnp.bfloat16) for _, _, w in targets],
        grid=(count,),
        in_specs=[rows_spec(TOKENS), pl.BlockSpec((2, TOKENS, WIDTH), lambda j: (0, 0, j + first))]
        + [ANY] * len(after),
        out_specs=[ANY] * len(targets),
        scratch_shapes=[
            pltpu.VMEM((2, 2, HELD, WIDTH), jnp.bfloat16),
            pltpu.SemaphoreType.DMA((len(targets),)),
        ],
        compiler_params=vmem(16),
        cost_estimate=cost(4 * HELD * TOKENS * count * WIDTH, 4 * TOKENS * (HELD + count * WIDTH)),
    )(pair, tokens, *after)


def adam_kernel(mixing, *refs):
    own, bias, arrived = refs[:3]
    state = refs[3:9]
    outs = refs[-7 - mixing[1] :]
    tile = 32

    def step(i, carry):
        at = pl.ds(pl.multiple_of(i * tile, tile), tile)
        for which in (0, 1):
            weight, first, second = (ref[at] for ref in state[3 * which : 3 * which + 3])
            scale = (up_scale, down_scale)[which]
            grad = scale * own[0, which, at] + arrived[which, at].astype(jnp.float32)
            first_new = beta_one * first.astype(jnp.float32) + (1.0 - beta_one) * grad
            second_new = beta_two * second.astype(jnp.float32) + (1.0 - beta_two) * grad * grad
            update = (learn_rate * bias[0]) * first_new / (jnp.sqrt(second_new * bias[1]) + adam_eps)
            outs[0][which, at] = (weight.astype(jnp.float32) - update).astype(jnp.bfloat16)
            outs[1 + 2 * which][at] = first_new.astype(jnp.bfloat16)
            outs[2 + 2 * which][at] = second_new.astype(jnp.bfloat16)
            if mixing[0]:
                both = refs[9][which, at].astype(jnp.float32) + refs[10][which, at].astype(jnp.float32)
                outs[5 + which][at] = (both * 0.5).astype(jnp.bfloat16)
        return carry

    lax.fori_loop(0, HELD // tile, step, 0)


def mix_kernel(own, other, *refs):
    tile = 32

    def step(i, carry):
        at = pl.ds(pl.multiple_of(i * tile, tile), tile)
        for which in (0, 1):
            both = own[which, at].astype(jnp.float32) + other[which, at].astype(jnp.float32)
            refs[which - 2][at] = (both * 0.5).astype(jnp.bfloat16)
        return carry

    lax.fori_loop(0, HELD // tile, step, 0)


whole = jax.ShapeDtypeStruct((HELD, D), jnp.bfloat16)


def adam_chunk(c, own, bias, arrived, state, mixed, results, passing):
    operands = [own[0], bias, arrived, *state, *mixed]
    aliases = {len(operands) + k: 1 + k for k in range(len(results))}
    operands += results
    if passing:
        aliases[len(operands)] = 7
        operands += passing
    before = max(c - 2, 0)
    mixing = [column_spec(before)] * 2 if mixed or not results else [ANY] * 2
    (first, width), place = CHUNKS[c], own[1]
    block, half = (1, 2, HELD, width), first % WIDTH // width
    smem = pl.BlockSpec(memory_space=pltpu.SMEM)
    pair = jax.ShapeDtypeStruct((2, HELD, width), jnp.bfloat16)
    handed = [jax.ShapeDtypeStruct(p.shape, p.dtype) for p in passing]
    return pl.pallas_call(
        functools.partial(adam_kernel, (bool(mixed), len(passing))),
        out_shape=[pair] + [whole] * 6 + handed,
        grid=(1,),
        in_specs=[pl.BlockSpec(block, lambda j: (place, 0, 0, half)), smem, pair_spec(c)]
        + [column_spec(c)] * 6
        + [pair_spec(before)] * len(mixed)
        + [ANY] * (len(results) + len(passing)),
        out_specs=[pair_spec(c)] + [column_spec(c)] * 4 + mixing + [ANY] * len(passing),
        input_output_aliases=aliases,
        compiler_params=vmem(12),
        cost_estimate=cost(0, 60 * HELD * WIDTH),
    )(*operands)


def mix_chunk(c, own, other, results):
    return pl.pallas_call(
        mix_kernel,
        out_shape=[whole] * 2,
        grid=(1,),
        in_specs=[pair_spec(c)] * 2 + [ANY] * 2,
        out_specs=[column_spec(c)] * 2,
        input_output_aliases={2: 0, 3: 1},
        compiler_params=vmem(8),
        cost_estimate=cost(0, 12 * HELD * WIDTH),
    )(own, other, *results)


def on_device(
    inputs,
    cotangent,
    up_weight,
    down_weight,
    momentum_up,
    momentum_down,
    variance_up,
    variance_down,
    step_index,
):
    up, down = up_weight[0], down_weight[0]
    half = ROWS // 2

    weights_sent = moved(stack_weights(up, down), y_sharing)
    a, b = prepare(inputs[0], cotangent[0])
    a_x, a_y = moved(a, x_other), moved(a, y_same_half)
    b_up, b_down = moved(b, z_up), moved(b, z_down)
    quarter = half // 2
    a_far = [moved(a_x[:, :quarter], y_same_half), moved(a_y[:, quarter:], x_other)]
    b_far = [moved(b_up[:, :quarter], z_up), moved(b_down[:, quarter:], z_down)]
    a_all = join([a, a_x, a_y, *a_far], [])
    b_all = join([b, b_up, b_down, *b_far], [])

    a_up, a_down = moved(a_all, z_up), moved(a_all, z_down)
    b_x, b_y = moved(b_all, x_other), moved(b_all, y_same_half)
    held = ((0, 0, HELD), (1, 0, HELD))
    job = (0, 0, 512, 0)
    results = hidden_step((job,), held, [up, down], [a_all, b_all], (), (0, 512), 1)

    mid = 2 * half
    halves = cut([a_up, a_down], (0, mid), mid, [results[0]])
    halves += cut([b_x, b_y], (0, mid), mid, [results[0]])
    last = [
        moved(halves[0], z_up),
        moved(halves[1], z_down),
        moved(halves[2], y_same_half),
        moved(halves[3], x_other),
    ]
    results = hidden_step(
        ((0, 0, 1024, 512), (1, 0, 1024, 512), (1, 1024, 512, 0)),
        held + ((None, HELD, HELD),),
        [up, down, weights_sent],
        [a_up, a_down, b_x, b_y, a_all, b_all],
        results,
        (512, 1024),
        2,
        halves[::2],
        True,
    )
    own_pair = results[0]
    pair, tokens, theirs = last_shared(weights_sent, last, *results[1:])

    count = step_index[0].astype(jnp.float32)
    bias_one = 1.0 - jnp.exp(count * math.log(beta_one))
    bias_two = 1.0 - jnp.exp(count * math.log(beta_two))
    bias = jnp.stack([1.0 / bias_one, 1.0 / bias_two])
    state = [up, momentum_up[0], variance_up[0], down, momentum_down[0], variance_down[0]]

    def finish(hop):
        route = [(g, (g + hop) % 4) for g in range(4)]
        news, updated, others = (), [], []
        more = [theirs, *theirs_chunks(1, 2, pair, tokens, [])]
        sent = [moved(t, y_sharing) for t in more[:2]]
        own, last_pair = own_first(up, down, tokens, own_pair, more[1:2])
        place = [(own, k) for k in range(FIRST_OWN)]
        for c in range(len(CHUNKS)):
            mixed = [updated[c - 2], others[c - 2]] if 2 <= c < MIXING else []
            passing = more[c + 2 : c + 3]
            block = place[CHUNKS[c][0] // WIDTH]
            out = adam_chunk(c, block, bias, sent[c], state, mixed, news, passing)
            updated.append(out[0])
            news = out[1:7]
            others.append(lax.ppermute(out[0], "rep", route))
            if passing:
                sent.append(moved(out[7], y_sharing))
            for after, first, count in THEIRS_LATER:
                if c == after:
                    more += theirs_chunks(first, count, pair, tokens, [out[0]])
            for after, first, count in OWN_LATER:
                if c == after:
                    own = own_rest(first, count, own_pair, last_pair, tokens, [out[0]])
                    place += [(own, k) for k in range(count)]
        mixed = news[4:]
        for c in range(MIXING - 2, len(CHUNKS)):
            mixed = mix_chunk(c, updated[c], others[c], mixed)
        return mixed[0], mixed[1], news[0], news[2], news[1], news[3]

    outs = lax.cond(step_index[0] % 2 == 0, lambda: finish(1), lambda: finish(2))
    return tuple(o[None] for o in outs)


def solution(mesh):
    shard = P("rep", "fsdp", None)
    return jax.shard_map(
        on_device,
        mesh=mesh,
        in_specs=(shard,) * 8 + (P(),),
        out_specs=(shard,) * 6,
        check_vma=False,
    )
```

```python
import functools
import math

import jax
import jax.numpy as jnp
from jax import lax
from jax.experimental import pallas as pl
from jax.experimental.pallas import tpu as pltpu
from jax.sharding import PartitionSpec as P

D = 1792
FF = 14336

beta_one = 0.9
beta_two = 0.95
learn_rate = 0.05
adam_eps = 1e-08
norm_eps = 1e-06
root_coef = math.sqrt(2.0 / math.pi)
up_scale = 1.0 / math.sqrt(D)
down_scale = 1.0 / math.sqrt(FF)

ROWS = 128
HELD = 448
SHARED = 2 * HELD
TOKENS = 2048
WIDTH = 256
BLOCKS = D // WIDTH
CHUNKS = tuple((WIDTH * k, WIDTH) for k in range(BLOCKS - 1)) + ((D - 256, 128), (D - 128, 128))
FIRST_OWN = 2
OWN_LATER = ((1, 2, 2), (2, 4, 3))
THEIRS_LATER = ((0, 3, 2), (2, 5, 2))
MIXING = 7
EARLY = 1536
NZ, NX, NY = 4, 2, 4


def moved(block, place):
    route = []
    for z in range(NZ):
        for x in range(NX):
            for y in range(NY):
                a, b, c = place(z, x, y)
                route.append(((z * NX + x) * NY + y, (a % NZ * NX + b) * NY + c))
    return lax.ppermute(block, "fsdp", route)


def z_up(z, x, y):
    return z + 1, x, y


def z_down(z, x, y):
    return z - 1, x, y


def z_over(z, x, y):
    return z + 2, x, y


def x_other(z, x, y):
    return z, 1 - x, y


def y_same_half(z, x, y):
    return z, x, 3 - y


def diagonal(z, x, y):
    return z, 1 - x, 3 - y


def y_sharing(z, x, y):
    return z, x, y ^ 1


def gelu_pair(pre):
    square = pre * pre
    tangent = jnp.tanh(pre * (root_coef + (root_coef * 0.044715) * square))
    half = 0.5 * tangent + 0.5
    value = pre * half
    slope = half + pre * (0.5 - 0.5 * tangent * tangent) * (
        root_coef + (3.0 * 0.044715 * root_coef) * square
    )
    return (value, slope)


def normalize(rows):
    wide = rows.astype(jnp.float32)
    factor = lax.rsqrt(jnp.mean(wide * wide, axis=-1, keepdims=True) + norm_eps)
    return (wide * factor).astype(jnp.bfloat16)


contract_last = (((1,), (1,)), ((), ()))
ANY = pl.BlockSpec(memory_space=pl.ANY)
INSIDE = pl.BlockSpec(memory_space=pltpu.VMEM)


def vmem(mebibytes):
    return pltpu.CompilerParams(vmem_limit_bytes=mebibytes * 1024 * 1024)


def cost(flops, moved_bytes):
    return pl.CostEstimate(flops=2 * flops, bytes_accessed=moved_bytes, transcendentals=0)


def prepare_kernel(inputs, cotangent, a_ref, b_ref, held, sem):
    half = ROWS // 2
    loads = [
        pltpu.make_async_copy(inputs, held, sem.at[0]),
        pltpu.make_async_copy(cotangent.at[pl.ds(0, half)], a_ref.at[1], sem.at[1]),
        pltpu.make_async_copy(cotangent.at[pl.ds(half, half)], b_ref.at[1], sem.at[2]),
    ]
    for load in loads:
        load.start()
    loads[0].wait()
    a_ref[0] = normalize(held[:half])
    b_ref[0] = normalize(held[half:])
    for load in loads[1:]:
        load.wait()


def prepare(inputs, cotangent):
    half = jax.ShapeDtypeStruct((2, ROWS // 2, D), jnp.bfloat16)
    return pl.pallas_call(
        prepare_kernel,
        out_shape=[half, half],
        in_specs=[ANY] * 2,
        out_specs=[INSIDE] * 2,
        scratch_shapes=[pltpu.VMEM((ROWS, D), jnp.bfloat16), pltpu.SemaphoreType.DMA((3,))],
        compiler_params=vmem(8),
        cost_estimate=cost(0, 8 * ROWS * D),
    )(inputs, cotangent)


def stack_kernel(up, down, out, held, load_sem, store_sem):
    parts = 2
    rows = HELD // parts
    loads, stores = [], []
    for which, ref in enumerate((up, down)):
        for part in range(parts):
            k, at = which * parts + part, pl.ds(part * rows, rows)
            place = held.at[which, at]
            loads.append(pltpu.make_async_copy(ref.at[at], place, load_sem.at[k]))
            stores.append(pltpu.make_async_copy(place, out.at[which, at], store_sem.at[k]))
    for load in loads:
        load.start()
    for load, store in zip(loads, stores):
        load.wait()
        store.start()
    for store in stores:
        store.wait()


def stack_weights(up, down):
    shape = (2, HELD, D)
    return pl.pallas_call(
        stack_kernel,
        out_shape=jax.ShapeDtypeStruct(shape, jnp.bfloat16),
        in_specs=[ANY] * 2,
        out_specs=ANY,
        scratch_shapes=[pltpu.VMEM(shape, jnp.bfloat16)] + [pltpu.SemaphoreType.DMA((4,))] * 2,
        compiler_params=vmem(8),
        cost_estimate=cost(0, 8 * HELD * D),
    )(up, down)


def join_kernel(count, *refs):
    first = 0
    for ref in refs[:count]:
        rows = ref.shape[1]
        refs[-1][:, first : first + rows] = ref[...]
        first += rows


def join(pieces, after):
    rows = sum(p.shape[1] for p in pieces)
    return pl.pallas_call(
        functools.partial(join_kernel, len(pieces)),
        out_shape=jax.ShapeDtypeStruct((2, rows, D), jnp.bfloat16),
        in_specs=[INSIDE] * len(pieces) + [ANY] * len(after),
        out_specs=INSIDE,
        compiler_params=vmem(8),
        cost_estimate=cost(0, 8 * rows * D),
    )(*pieces, *after)


def cut_kernel(firsts, count_in, *refs):
    sem = refs[-1]
    loads = []
    for k, first in enumerate(firsts):
        out = refs[count_in + k]
        source = refs[k].at[:, pl.ds(first, out.shape[1])]
        loads.append(pltpu.make_async_copy(source, out, sem.at[k]))
        loads[-1].start()
    for load in loads:
        load.wait()


def cut(blocks, firsts, rows, after):
    out = jax.ShapeDtypeStruct((2, rows, D), jnp.bfloat16)
    operands = list(blocks) + list(after)
    return pl.pallas_call(
        functools.partial(cut_kernel, firsts, len(operands)),
        out_shape=[out] * len(blocks),
        in_specs=[ANY] * len(operands),
        out_specs=[INSIDE] * len(blocks),
        scratch_shapes=[pltpu.SemaphoreType.DMA((len(blocks),))],
        compiler_params=vmem(8),
        cost_estimate=cost(0, 8 * rows * D * len(blocks)),
    )(*operands)


def hidden_kernel(jobs, sizes, pieces, skipped, kept, tile, both, chunk, *refs):
    arrays = refs[: len(pieces)]
    blocks = refs[len(pieces) : len(pieces) + len(sizes)]
    refs = refs[len(pieces) + len(sizes) + skipped :]
    weights, tokens, pair, weight_sem, token_sem, out_sem, keep_sem = refs[-7:]
    top, total = weights.shape[1], tokens.shape[1]
    loads = []
    for k, (ref, (which, first, rows)) in enumerate(zip(arrays, pieces)):
        target = weights.at[:, pl.ds(first, rows)]
        if which is not None:
            target = weights.at[which, pl.ds(first, rows)]
        loads.append(pltpu.make_async_copy(ref, target, weight_sem.at[k]))
    first, arriving = 0, {}
    for k, (ref, count) in enumerate(zip(blocks, sizes)):
        load = pltpu.make_async_copy(ref, tokens.at[:, pl.ds(first, count)], token_sem.at[k])
        at = first // tile
        at = at * (top // HELD) if at < both else at + (top // HELD - 1) * both
        arriving.setdefault(at, []).append(load)
        first += count
    for load in [*arriving[0], *loads, *sum((l for at, l in arriving.items() if at), [])]:
        load.start()
    for load in loads:
        load.wait()
    stores = []

    def step(i, carry):
        for at, expected in arriving.items():

            @pl.when(i == at)
            def _(expected=expected):
                for load in expected:
                    load.wait()

        blocks = top // HELD
        here = i < blocks * both
        row = jnp.where(here, i % blocks, blocks - 1) * HELD
        token = jnp.where(here, i // blocks, i - (blocks - 1) * both) * tile
        rows = pl.ds(pl.multiple_of(row, HELD), HELD)
        at = pl.ds(pl.multiple_of(token, tile), tile)
        pre = up_scale * lax.dot_general(
            weights[0, rows], tokens[0, at], contract_last, preferred_element_type=jnp.float32
        )
        back = down_scale * lax.dot_general(
            weights[1, rows], tokens[1, at], contract_last, preferred_element_type=jnp.float32
        )
        value, slope = gelu_pair(pre)
        pair[0, rows, at] = (back * slope).astype(jnp.bfloat16)
        pair[1, rows, at] = value.astype(jnp.bfloat16)
        return carry

    lax.fori_loop(0, top // HELD * both + (total // tile - both), step, 0)
    for k, (shared, token, count, place) in enumerate(jobs):
        stores.append(
            pltpu.make_async_copy(
                pair.at[:, pl.ds(shared * HELD, HELD), pl.ds(token, count)],
                refs[shared].at[:, :, pl.ds(place, count)],
                out_sem.at[k],
            )
        )
        stores[-1].start()
    if kept is not None:
        source = tokens.at[:, pl.ds(0, kept[1])]
        target = refs[2].at[:, pl.ds(kept[0], kept[1])]
        stores.append(pltpu.make_async_copy(source, target, keep_sem.at[0]))
        stores[-1].start()
    if chunk:

        def multiply(which, carry):
            refs[3][which] = jnp.dot(
                pair[which, HELD:], tokens[which, :, :WIDTH], preferred_element_type=jnp.float32
            )
            return carry

        lax.fori_loop(0, 2, multiply, 0)
    for store in stores:
        store.wait()


def hidden_step(jobs, pieces, arrays, blocks, results, kept, both, after=(), chunk=False):
    sizes = tuple(b.shape[1] for b in blocks)
    total = sum(sizes)
    top = max(first + rows for _, first, rows in pieces)
    shapes = ((2, HELD, EARLY), (2, HELD, TOKENS), (2, TOKENS, D))
    out = [jax.ShapeDtypeStruct(shape, jnp.bfloat16) for shape in shapes]
    out += [jax.ShapeDtypeStruct((2, HELD, WIDTH), jnp.float32)] * chunk
    operands = [*arrays, *blocks]
    aliases = {len(operands) + k: k for k in range(len(results))}
    operands += [*results, *after]
    flops = sum(4 * HELD * count * D for _, _, count, _ in jobs)
    skipped = len(results) + len(after)
    return pl.pallas_call(
        functools.partial(hidden_kernel, jobs, sizes, pieces, skipped, kept, 512, both, chunk),
        out_shape=out,
        in_specs=[ANY] * len(operands),
        out_specs=[ANY] * 3 + [INSIDE] * chunk,
        input_output_aliases=aliases,
        scratch_shapes=[
            pltpu.VMEM((2, top, D), jnp.bfloat16),
            pltpu.VMEM((2, total, D), jnp.bfloat16),
            pltpu.VMEM((2, top, total), jnp.bfloat16),
            pltpu.SemaphoreType.DMA((len(pieces),)),
            pltpu.SemaphoreType.DMA((len(blocks),)),
            pltpu.SemaphoreType.DMA((len(jobs),)),
            pltpu.SemaphoreType.DMA((1,)),
        ],
        compiler_params=vmem(30 if len(jobs) > 1 else 16),
        cost_estimate=cost(flops, 4 * (total + top) * D + 4 * top * total),
    )(*operands)


def own_first_kernel(up, down, tokens_in, pair_in, *refs):
    out, pair, weights, tokens, columns, early, grads, sem = refs[-8:]
    width = FIRST_OWN * WIDTH
    loads = [
        pltpu.make_async_copy(up, weights.at[0], sem.at[0]),
        pltpu.make_async_copy(down, weights.at[1], sem.at[1]),
        pltpu.make_async_copy(tokens_in.at[:, pl.ds(EARLY, TOKENS - EARLY)], tokens, sem.at[2]),
        pltpu.make_async_copy(
            tokens_in.at[:, pl.ds(0, EARLY), pl.ds(0, width)], columns, sem.at[3]
        ),
        pltpu.make_async_copy(pair_in, early, sem.at[4]),
    ]
    for load in loads:
        load.start()
    for load in loads[:3]:
        load.wait()
    tile = 256

    def step(i, carry):
        at = pl.ds(pl.multiple_of(i * tile, tile), tile)
        pre = up_scale * lax.dot_general(
            weights[0], tokens[0, at], contract_last, preferred_element_type=jnp.float32
        )
        back = down_scale * lax.dot_general(
            weights[1], tokens[1, at], contract_last, preferred_element_type=jnp.float32
        )
        value, slope = gelu_pair(pre)
        pair[0, :, at] = (back * slope).astype(jnp.bfloat16)
        pair[1, :, at] = value.astype(jnp.bfloat16)
        return carry

    lax.fori_loop(0, (TOKENS - EARLY) // tile, step, 0)
    for load in loads[3:]:
        load.wait()

    def multiply(i, carry):
        which, k = i % 2, i // 2
        at = pl.ds(pl.multiple_of(k * WIDTH, WIDTH), WIDTH)
        grads[...] = jnp.dot(
            early[which], columns[which, :, at], preferred_element_type=jnp.float32
        )
        out[k, which] = grads[...] + jnp.dot(
            pair[which], tokens[which, :, at], preferred_element_type=jnp.float32
        )
        return carry

    lax.fori_loop(0, 2 * FIRST_OWN, multiply, 0)


def own_first(up, down, tokens, pair, after):
    rest = TOKENS - EARLY
    return pl.pallas_call(
        own_first_kernel,
        out_shape=[
            jax.ShapeDtypeStruct((FIRST_OWN, 2, HELD, WIDTH), jnp.float32),
            jax.ShapeDtypeStruct((2, HELD, rest), jnp.bfloat16),
        ],
        in_specs=[ANY] * (4 + len(after)),
        out_specs=[INSIDE] * 2,
        scratch_shapes=[
            pltpu.VMEM((2, HELD, D), jnp.bfloat16),
            pltpu.VMEM((2, rest, D), jnp.bfloat16),
            pltpu.VMEM((2, EARLY, FIRST_OWN * WIDTH), jnp.bfloat16),
            pltpu.VMEM((2, HELD, EARLY), jnp.bfloat16),
            pltpu.VMEM((HELD, WIDTH), jnp.float32),
            pltpu.SemaphoreType.DMA((5,)),
        ],
        compiler_params=vmem(20),
        cost_estimate=cost(4 * HELD * (rest * D + TOKENS * FIRST_OWN * WIDTH), 4 * (HELD + rest) * D),
    )(up, down, tokens, pair, *after)


def own_rest_kernel(pair, pair_last, tokens, out, grads):
    def multiply(which, carry):
        grads[...] = jnp.dot(pair[which], tokens[which, :EARLY], preferred_element_type=jnp.float32)
        out[0, which] = grads[...] + jnp.dot(
            pair_last[which], tokens[which, EARLY:], preferred_element_type=jnp.float32
        )
        return carry

    lax.fori_loop(0, 2, multiply, 0)


def own_rest(first, count, pair, pair_last, tokens, after):
    def kernel(*refs):
        own_rest_kernel(*refs[:3], *refs[-2:])

    return pl.pallas_call(
        kernel,
        out_shape=jax.ShapeDtypeStruct((count, 2, HELD, WIDTH), jnp.float32),
        grid=(count,),
        in_specs=[
            rows_spec(EARLY),
            rows_spec(TOKENS - EARLY),
            pl.BlockSpec((2, TOKENS, WIDTH), lambda j: (0, 0, j + first)),
        ]
        + [ANY] * len(after),
        out_specs=pl.BlockSpec((1, 2, HELD, WIDTH), lambda j: (j, 0, 0, 0)),
        scratch_shapes=[pltpu.VMEM((HELD, WIDTH), jnp.float32)],
        compiler_params=vmem(18),
        cost_estimate=cost(4 * HELD * TOKENS * count * WIDTH, 4 * TOKENS * (HELD + count * WIDTH)),
    )(pair, pair_last, tokens, *after)


def last_shared_kernel(*refs):
    weights_in, blocks = refs[0], refs[1:5]
    partial, pair_out, tokens_out, chunk = refs[7:11]
    weights, tokens, pair, early, sem, out_sem = refs[11:]
    first, width = 0, WIDTH
    rest = TOKENS - EARLY
    weights_load = pltpu.make_async_copy(weights_in, weights, sem.at[0])
    loads, row = [], 0
    for k, ref in enumerate(blocks):
        rows = ref.shape[1]
        loads.append(pltpu.make_async_copy(ref, tokens.at[:, pl.ds(row, rows)], sem.at[1 + k]))
        row += rows
    late = pl.ds(EARLY, rest)
    more = [pltpu.make_async_copy(partial, early, sem.at[5])]
    for load in [*loads[:2], weights_load, *loads[2:], *more]:
        load.start()
    weights_load.wait()
    tile = 256

    def step(i, carry):
        at = pl.ds(pl.multiple_of(i * tile, tile), tile)
        pre = up_scale * lax.dot_general(
            weights[0], tokens[0, at], contract_last, preferred_element_type=jnp.float32
        )
        back = down_scale * lax.dot_general(
            weights[1], tokens[1, at], contract_last, preferred_element_type=jnp.float32
        )
        value, slope = gelu_pair(pre)
        pair[0, :, at] = (back * slope).astype(jnp.bfloat16)
        pair[1, :, at] = value.astype(jnp.bfloat16)
        return carry

    def arriving(i, carry):
        for parity in (0, 1):

            @pl.when(i == parity)
            def _(parity=parity):
                for load in loads[2 * parity : 2 * parity + 2]:
                    load.wait()

        return step(i, carry)

    lax.fori_loop(0, rest // tile, arriving, 0)
    stores = [pltpu.make_async_copy(tokens, tokens_out.at[:, late], out_sem.at[0])]
    stores[0].start()
    stores.append(pltpu.make_async_copy(pair, pair_out.at[:, :, late], out_sem.at[1]))
    stores[1].start()
    for load in more:
        load.wait()
    for which, scale in enumerate((up_scale, down_scale)):
        grad = early[which] + jnp.dot(
            pair[which],
            tokens[which, :, first : first + width],
            preferred_element_type=jnp.float32,
        )
        chunk[which] = (scale * grad).astype(jnp.bfloat16)
    for store in stores:
        store.wait()


def last_shared(weights, blocks, pair, tokens, partial):
    width = WIDTH
    return pl.pallas_call(
        last_shared_kernel,
        out_shape=[
            jax.ShapeDtypeStruct((2, HELD, TOKENS), jnp.bfloat16),
            jax.ShapeDtypeStruct((2, TOKENS, D), jnp.bfloat16),
            jax.ShapeDtypeStruct((2, HELD, width), jnp.bfloat16),
        ],
        in_specs=[ANY] * 8,
        out_specs=[ANY] * 2 + [INSIDE],
        input_output_aliases={5: 0, 6: 1},
        scratch_shapes=[
            pltpu.VMEM((2, HELD, D), jnp.bfloat16),
            pltpu.VMEM((2, TOKENS - EARLY, D), jnp.bfloat16),
            pltpu.VMEM((2, HELD, TOKENS - EARLY), jnp.bfloat16),
            pltpu.VMEM((2, HELD, width), jnp.float32),
            pltpu.SemaphoreType.DMA((6,)),
            pltpu.SemaphoreType.DMA((2,)),
        ],
        compiler_params=vmem(16),
        cost_estimate=cost(
            4 * HELD * ((TOKENS - EARLY) * D + TOKENS * width), 4 * (HELD + TOKENS - EARLY) * D
        ),
    )(weights, *blocks, pair, tokens, partial)


def column_spec(c):
    first, width = CHUNKS[c]
    return pl.BlockSpec((HELD, width), lambda j: (0, first // width))


def pair_spec(c):
    return pl.BlockSpec((2, HELD, CHUNKS[c][1]), lambda j: (0, 0, 0))


def rows_spec(tokens):
    return pl.BlockSpec((2, HELD, tokens), lambda j: (0, 0, 0))


def theirs_kernel(targets, skipped, pair, tokens, *refs):
    outs = refs[skipped : skipped + len(targets)]
    held, sem = refs[-2:]
    j = pl.program_id(0)
    slot = j % 2

    def copy(k):
        block, first, width = targets[k]
        source = held.at[block % 2, :, :, pl.ds(first, width)]
        return pltpu.make_async_copy(source, outs[k], sem.at[k])

    for k, (block, _, _) in enumerate(targets):

        @pl.when(j == block + 2)
        def _(k=k):
            copy(k).wait()

    def multiply(which, carry):
        scale = jnp.where(which == 0, up_scale, down_scale)
        grad = jnp.dot(pair[which], tokens[which], preferred_element_type=jnp.float32)
        held[slot, which] = (scale * grad).astype(jnp.bfloat16)
        return carry

    lax.fori_loop(0, 2, multiply, 0)
    blocks = targets[-1][0] + 1
    for k, (block, _, _) in enumerate(targets):

        @pl.when(j == block)
        def _(k=k):
            copy(k).start()

    @pl.when(j == blocks - 1)
    def _():
        for k, (block, _, _) in enumerate(targets):
            if block >= blocks - 2:
                copy(k).wait()


def theirs_chunks(first, count, pair, tokens, after):
    targets = tuple(
        (column // WIDTH - first, column % WIDTH, width)
        for column, width in CHUNKS
        if first <= column // WIDTH < first + count
    )
    return pl.pallas_call(
        functools.partial(theirs_kernel, targets, len(after)),
        out_shape=[jax.ShapeDtypeStruct((2, HELD, w), jnp.bfloat16) for _, _, w in targets],
        grid=(count,),
        in_specs=[rows_spec(TOKENS), pl.BlockSpec((2, TOKENS, WIDTH), lambda j: (0, 0, j + first))]
        + [ANY] * len(after),
        out_specs=[ANY] * len(targets),
        scratch_shapes=[
            pltpu.VMEM((2, 2, HELD, WIDTH), jnp.bfloat16),
            pltpu.SemaphoreType.DMA((len(targets),)),
        ],
        compiler_params=vmem(16),
        cost_estimate=cost(4 * HELD * TOKENS * count * WIDTH, 4 * TOKENS * (HELD + count * WIDTH)),
    )(pair, tokens, *after)


def adam_kernel(mixing, *refs):
    own, bias, arrived = refs[:3]
    state = refs[3:9]
    outs = refs[-7 - mixing[1] :]
    tile = 32

    def step(i, carry):
        at = pl.ds(pl.multiple_of(i * tile, tile), tile)
        for which in (0, 1):
            weight, first, second = (ref[at] for ref in state[3 * which : 3 * which + 3])
            scale = (up_scale, down_scale)[which]
            grad = scale * own[0, which, at] + arrived[which, at].astype(jnp.float32)
            first_new = beta_one * first.astype(jnp.float32) + (1.0 - beta_one) * grad
            second_new = beta_two * second.astype(jnp.float32) + (1.0 - beta_two) * grad * grad
            update = (learn_rate * bias[0]) * first_new / (jnp.sqrt(second_new * bias[1]) + adam_eps)
            outs[0][which, at] = (weight.astype(jnp.float32) - update).astype(jnp.bfloat16)
            outs[1 + 2 * which][at] = first_new.astype(jnp.bfloat16)
            outs[2 + 2 * which][at] = second_new.astype(jnp.bfloat16)
            if mixing[0]:
                both = refs[9][which, at].astype(jnp.float32) + refs[10][which, at].astype(jnp.float32)
                outs[5 + which][at] = (both * 0.5).astype(jnp.bfloat16)
        return carry

    lax.fori_loop(0, HELD // tile, step, 0)


def mix_kernel(own, other, *refs):
    tile = 32

    def step(i, carry):
        at = pl.ds(pl.multiple_of(i * tile, tile), tile)
        for which in (0, 1):
            both = own[which, at].astype(jnp.float32) + other[which, at].astype(jnp.float32)
            refs[which - 2][at] = (both * 0.5).astype(jnp.bfloat16)
        return carry

    lax.fori_loop(0, HELD // tile, step, 0)


whole = jax.ShapeDtypeStruct((HELD, D), jnp.bfloat16)


def adam_chunk(c, own, bias, arrived, state, mixed, results, passing):
    operands = [own[0], bias, arrived, *state, *mixed]
    aliases = {len(operands) + k: 1 + k for k in range(len(results))}
    operands += results
    if passing:
        aliases[len(operands)] = 7
        operands += passing
    before = max(c - 2, 0)
    mixing = [column_spec(before)] * 2 if mixed or not results else [ANY] * 2
    (first, width), place = CHUNKS[c], own[1]
    block, half = (1, 2, HELD, width), first % WIDTH // width
    smem = pl.BlockSpec(memory_space=pltpu.SMEM)
    pair = jax.ShapeDtypeStruct((2, HELD, width), jnp.bfloat16)
    handed = [jax.ShapeDtypeStruct(p.shape, p.dtype) for p in passing]
    return pl.pallas_call(
        functools.partial(adam_kernel, (bool(mixed), len(passing))),
        out_shape=[pair] + [whole] * 6 + handed,
        grid=(1,),
        in_specs=[pl.BlockSpec(block, lambda j: (place, 0, 0, half)), smem, pair_spec(c)]
        + [column_spec(c)] * 6
        + [pair_spec(before)] * len(mixed)
        + [ANY] * (len(results) + len(passing)),
        out_specs=[pair_spec(c)] + [column_spec(c)] * 4 + mixing + [ANY] * len(passing),
        input_output_aliases=aliases,
        compiler_params=vmem(12),
        cost_estimate=cost(0, 60 * HELD * WIDTH),
    )(*operands)


def mix_chunk(c, own, other, results):
    return pl.pallas_call(
        mix_kernel,
        out_shape=[whole] * 2,
        grid=(1,),
        in_specs=[pair_spec(c)] * 2 + [ANY] * 2,
        out_specs=[column_spec(c)] * 2,
        input_output_aliases={2: 0, 3: 1},
        compiler_params=vmem(8),
        cost_estimate=cost(0, 12 * HELD * WIDTH),
    )(own, other, *results)


def on_device(
    inputs,
    cotangent,
    up_weight,
    down_weight,
    momentum_up,
    momentum_down,
    variance_up,
    variance_down,
    step_index,
):
    up, down = up_weight[0], down_weight[0]
    half = ROWS // 2

    weights_sent = moved(stack_weights(up, down), y_sharing)
    a, b = prepare(inputs[0], cotangent[0])
    a_x, a_y = moved(a, x_other), moved(a, y_same_half)
    b_up, b_down = moved(b, z_up), moved(b, z_down)
    quarter = half // 2
    a_far = [moved(a_x[:, :quarter], y_same_half), moved(a_y[:, quarter:], x_other)]
    b_far = [moved(b_up[:, :quarter], z_up), moved(b_down[:, quarter:], z_down)]
    a_all = join([a, a_x, a_y, *a_far], [])
    b_all = join([b, b_up, b_down, *b_far], [])

    a_up, a_down = moved(a_all, z_up), moved(a_all, z_down)
    b_x, b_y = moved(b_all, x_other), moved(b_all, y_same_half)
    held = ((0, 0, HELD), (1, 0, HELD))
    job = (0, 0, 512, 0)
    results = hidden_step((job,), held, [up, down], [a_all, b_all], (), (0, 512), 1)

    mid = 2 * half
    halves = cut([a_up, a_down], (0, mid), mid, [results[0]])
    halves += cut([b_x, b_y], (0, mid), mid, [results[0]])
    last = [
        moved(halves[0], z_up),
        moved(halves[1], z_down),
        moved(halves[3], x_other),
        moved(halves[2], y_same_half),
    ]
    results = hidden_step(
        ((0, 0, 1024, 512), (1, 0, 1024, 512), (1, 1024, 512, 0)),
        held + ((None, HELD, HELD),),
        [up, down, weights_sent],
        [a_up, a_down, b_x, b_y, a_all, b_all],
        results,
        (512, 1024),
        2,
        halves[::2],
        True,
    )
    own_pair = results[0]
    pair, tokens, theirs = last_shared(weights_sent, last, *results[1:])

    count = step_index[0].astype(jnp.float32)
    bias_one = 1.0 - jnp.exp(count * math.log(beta_one))
    bias_two = 1.0 - jnp.exp(count * math.log(beta_two))
    bias = jnp.stack([1.0 / bias_one, 1.0 / bias_two])
    state = [up, momentum_up[0], variance_up[0], down, momentum_down[0], variance_down[0]]

    def finish(hop):
        route = [(g, (g + hop) % 4) for g in range(4)]
        news, updated, others = (), [], []
        more = [theirs, *theirs_chunks(1, 2, pair, tokens, [])]
        sent = [moved(t, y_sharing) for t in more[:2]]
        own, last_pair = own_first(up, down, tokens, own_pair, more[1:2])
        place = [(own, k) for k in range(FIRST_OWN)]
        for c in range(len(CHUNKS)):
            mixed = [updated[c - 2], others[c - 2]] if 2 <= c < MIXING else []
            passing = more[c + 2 : c + 3]
            block = place[CHUNKS[c][0] // WIDTH]
            out = adam_chunk(c, block, bias, sent[c], state, mixed, news, passing)
            updated.append(out[0])
            news = out[1:7]
            others.append(lax.ppermute(out[0], "rep", route))
            if passing:
                sent.append(moved(out[7], y_sharing))
            for after, first, count in THEIRS_LATER:
                if c == after:
                    more += theirs_chunks(first, count, pair, tokens, [out[0]])
            for after, first, count in OWN_LATER:
                if c == after:
                    own = own_rest(first, count, own_pair, last_pair, tokens, [out[0]])
                    place += [(own, k) for k in range(count)]
        mixed = news[4:]
        for c in range(MIXING - 2, len(CHUNKS)):
            mixed = mix_chunk(c, updated[c], others[c], mixed)
        return mixed[0], mixed[1], news[0], news[2], news[1], news[3]

    outs = lax.cond(step_index[0] % 2 == 0, lambda: finish(1), lambda: finish(2))
    return tuple(o[None] for o in outs)


def solution(mesh):
    shard = P("rep", "fsdp", None)
    return jax.shard_map(
        on_device,
        mesh=mesh,
        in_specs=(shard,) * 8 + (P(),),
        out_specs=(shard,) * 6,
        check_vma=False,
    )
```
